32 devices in a mesh: clip: 16 (over z, y, core), map: 2 (over x).
Axes of the slice: x: 2, y: 2, z: 4, core: 2. Of those that a mesh axis runs over, the one named last changes fastest.
Arguments:
- patches: bfloat16 [2, 32, 32, 196, 768], P(None, 'clip', 'map'), may hold values from -6 to 6
- keep: int32 [2, 32, 32, 196], P(None, 'clip', 'map'), may hold values 0 or 1
- tl_gain: bfloat16 [768], P('clip'), may hold values from 0.099609375 to 1.8984375
- tl_bias: bfloat16 [768], P('clip'), may hold values from -3 to 3
- map_w1: bfloat16 [768, 64], P('clip'), may hold values from -0.21875 to 0.21875
- map_b1: bfloat16 [64], P('clip'), may hold values from -3 to 3
- map_w2: bfloat16 [64, 8], P('clip'), may hold values from -1.5 to 1.5
- map_b2: bfloat16 [8], replicated, may hold values from -3 to 3
- ln1_gain: bfloat16 [768], P('clip'), may hold values from 0.099609375 to 1.8984375
- ln1_bias: bfloat16 [768], P('clip'), may hold values from -3 to 3
- qkv_weight: bfloat16 [768, 2304], P('clip'), may hold values from -0.21875 to 0.21875
- qv_bias: bfloat16 [2, 768], P(None, 'clip'), may hold values from -3 to 3
- out_weight: bfloat16 [768, 768], P('clip'), may hold values from -0.625 to 0.625
- out_bias: bfloat16 [768], P('clip'), may hold values from -3 to 3
- ln2_gain: bfloat16 [768], P('clip'), may hold values from 0.099609375 to 1.8984375
- ln2_bias: bfloat16 [768], P('clip'), may hold values from -3 to 3
- fc1_weight: bfloat16 [768, 3072], P('clip'), may hold values from -0.21875 to 0.21875
- fc1_bias: bfloat16 [3072], P('clip'), may hold values from -3 to 3
- fc2_weight: bfloat16 [3072, 768], P('clip'), may hold values from -0.15625 to 0.15625
- fc2_bias: bfloat16 [768], P('clip'), may hold values from -3 to 3
- cotangent: bfloat16 [2, 32, 256, 768], P(None, ('clip', 'map')), may hold values from -6 to 6
Outputs:
- layer_out: bfloat16 [2, 32, 256, 768], P(None, ('clip', 'map'))
- patch_grad: bfloat16 [2, 32, 32, 196, 768], P(None, 'clip', 'map')
- tl_gain_grad: float32 [768], P('clip')
- tl_bias_grad: float32 [768], P('clip')
- map_w1_grad: float32 [768, 64], P('clip')
- map_b1_grad: float32 [64], P('clip')
- map_w2_grad: float32 [64, 8], P('clip')
- map_b2_grad: float32 [8], replicated
- ln1_gain_grad: float32 [768], P('clip')
- ln1_bias_grad: float32 [768], P('clip')
- qkv_weight_grad: float32 [768, 2304], P('clip')
- qv_bias_grad: float32 [2, 768], P(None, 'clip')
- out_weight_grad: float32 [768, 768], P('clip')
- out_bias_grad: float32 [768], P('clip')
- ln2_gain_grad: float32 [768], P('clip')
- ln2_bias_grad: float32 [768], P('clip')
- fc1_weight_grad: float32 [768, 3072], P('clip')
- fc1_bias_grad: float32 [3072], P('clip')
- fc2_weight_grad: float32 [3072, 768], P('clip')
- fc2_bias_grad: float32 [768], P('clip')
The draws below stay inside these ranges and needn't reach their ends.
Inputs may be any that keep to these rules, and one draw needn't show every extreme that they name: `keep`: 1 keeps a patch, 0 drops it.
All inputs are finite; a program needn't handle non-finite values. No bound on the sum of `keep` on one device may be relied on, other than what follows from the above.
Results may differ from the reference program's by a relative error of at most 0.03.
Values may be sent and summed in bfloat16 or wider, within the bound.
A program may use at most 320 MiB of HBM per device.

```python
import jax
import jax.numpy as jnp
from jax import lax

D = 768
HEADS = 12
HEAD = 64
FF = 3072
MAPHID = 64
MAPS = 8
FRAMES = 32
PATCHES = 196
MICRO = 2
CLIPS = 32
SEQ = 256


def place_ends(entries, rng, low, high):
    longest = entries.shape.index(max(entries.shape))
    spots = []
    for shift in (0, 1):
        where = [jax.random.randint(jax.random.fold_in(rng, axis), (), 0, length) for axis, length in enumerate(entries.shape)]
        where[longest] = (where[longest] + shift) % entries.shape[longest]
        spots.append(tuple(where))
    return entries.at[spots[0]].set(low).at[spots[1]].set(high)


def block_levels(key, shape, shards, smallest, largest):
    def one(position, parts):
        steps = jax.random.uniform(jax.random.fold_in(jax.random.fold_in(key, 6), position), (parts,), jnp.float32, smallest / len(shards), largest / len(shards))
        return jnp.repeat(jnp.exp(steps), shape[position] // parts).reshape((-1,) + (1,) * (len(shape) - position - 1))

    gain = one(*shards[0])
    for cut in shards[1:]:
        gain = gain * one(*cut)
    return gain


def bell_draw(own_key, dims, scale, most, split=(), held_as=jnp.bfloat16):
    factor_of = block_levels(own_key, dims, split, -0.22, 0.18) if split else 1.0
    values = jax.random.normal(own_key, dims, jnp.float32) * scale * factor_of
    return jnp.minimum(jnp.maximum(values, -most), most).astype(held_as)


def setup_inputs(seed: int = 0) -> dict:
    seeds = jax.random.split(jax.random.key(seed), 22)
    patches = bell_draw(seeds[0], (MICRO, CLIPS, FRAMES, PATCHES, D), 1.0, 6.0, ((1, 16), (2, 2)))
    keep = place_ends((jax.random.randint(seeds[1], (MICRO, CLIPS, FRAMES, PATCHES), 0, 4) < 3).astype(jnp.int32), jax.random.fold_in(seeds[1], 1), 0, 1)
    tl_gain = jnp.clip(1.0 + 0.18 * jax.random.normal(seeds[2], (D,), jnp.float32), 0.099609375, 1.8984375).astype(jnp.bfloat16)
    tl_bias = bell_draw(seeds[3], (D,), 0.3, 3.0, ((0, 16),))
    map_w1 = bell_draw(seeds[4], (D, MAPHID), D ** -0.5, 0.21875, ((0, 16),))
    map_b1 = bell_draw(seeds[5], (MAPHID,), 0.3, 3.0, ((0, 16),))
    map_w2 = bell_draw(seeds[6], (MAPHID, MAPS), (MAPHID // 4) ** -0.5, 1.5, ((0, 16),))
    map_b2 = bell_draw(seeds[7], (MAPS,), 0.5, 3.0)
    ln1_gain = jnp.clip(1.0 + 0.18 * jax.random.normal(seeds[8], (D,), jnp.float32), 0.099609375, 1.8984375).astype(jnp.bfloat16)
    ln1_bias = bell_draw(seeds[9], (D,), 0.3, 3.0, ((0, 16),))
    qkv_weight = bell_draw(seeds[10], (D, 3 * D), D ** -0.5, 0.21875, ((0, 16),))
    qv_bias = bell_draw(seeds[11], (2, D), 0.3, 3.0, ((1, 16),))
    out_weight = bell_draw(seeds[12], (D, D), (D // 8) ** -0.5, 0.625, ((0, 16),))
    out_bias = bell_draw(seeds[13], (D,), 0.3, 3.0, ((0, 16),))
    ln2_gain = jnp.clip(1.0 + 0.18 * jax.random.normal(seeds[14], (D,), jnp.float32), 0.099609375, 1.8984375).astype(jnp.bfloat16)
    ln2_bias = bell_draw(seeds[15], (D,), 0.3, 3.0, ((0, 16),))
    fc1_weight = bell_draw(seeds[16], (D, FF), D ** -0.5, 0.21875, ((0, 16),))
    fc1_bias = bell_draw(seeds[17], (FF,), 0.3, 3.0, ((0, 16),))
    fc2_weight = bell_draw(seeds[18], (FF, D), (FF // 2) ** -0.5, 0.15625, ((0, 16),))
    fc2_bias = bell_draw(seeds[19], (D,), 0.3, 3.0, ((0, 16),))
    cotangent = bell_draw(seeds[20], (MICRO, CLIPS, SEQ, D), 1.0, 6.0, ((1, 32),))
    return {"patches": patches, "keep": keep, "tl_gain": tl_gain, "tl_bias": tl_bias, "map_w1": map_w1, "map_b1": map_b1, "map_w2": map_w2, "map_b2": map_b2, "ln1_gain": ln1_gain, "ln1_bias": ln1_bias, "qkv_weight": qkv_weight, "qv_bias": qv_bias, "out_weight": out_weight, "out_bias": out_bias, "ln2_gain": ln2_gain, "ln2_bias": ln2_bias, "fc1_weight": fc1_weight, "fc1_bias": fc1_bias, "fc2_weight": fc2_weight, "fc2_bias": fc2_bias, "cotangent": cotangent}


@jax.custom_vjp
def low(v):
    return lax.optimization_barrier(v.astype(jnp.bfloat16)).astype(jnp.float32)

@jax.custom_vjp
def low_back(v):
    return v

def low_keep(v):
    return (low(v), None)

def low_pass(kept, grad):
    return (grad,)

def back_keep(v):
    return (v, None)

def back_low(kept, grad):
    return (low(grad),)
low.defvjp(low_keep, low_pass)
low_back.defvjp(back_keep, back_low)
EPSILON = 1e-06
HIGHEST = lax.Precision.HIGHEST

def normalize(values_in, gain_in, shift_in):
    center = lax.optimization_barrier(jnp.mean(values_in, axis=-1, keepdims=True))
    centered = values_in - center
    spread = lax.optimization_barrier(jnp.mean(centered * centered, axis=-1, keepdims=True))
    return centered * lax.rsqrt(spread + EPSILON) * gain_in + shift_in

def gelu_tanh(value_in):
    return 0.5 * value_in * (1.0 + jnp.tanh(0.7978845608028654 * (value_in + 0.044715 * value_in * value_in * value_in)))

def softmax_rows(scores):
    peak = lax.optimization_barrier(jnp.max(scores, axis=-1, keepdims=True))
    expo = jnp.exp(scores - peak)
    return expo / lax.optimization_barrier(jnp.sum(expo, axis=-1, keepdims=True))

def clip_forward(params, clip_patches, clip_keep):
    tl_gain, tl_bias, map_w1, map_b1, map_w2, map_b2, ln1_gain, ln1_bias, qkv_weight, qv_bias, out_weight, out_bias, ln2_gain, ln2_bias, fc1_weight, fc1_bias, fc2_weight, fc2_bias = params
    tl_normed = low(normalize(clip_patches, tl_gain, tl_bias))
    map_pre = low_back(jnp.einsum('fpd,dh->fph', tl_normed, map_w1, precision=HIGHEST) + map_b1)
    map_act = low(gelu_tanh(map_pre))
    map_logit = low_back(jnp.einsum('fph,hk->fpk', map_act, map_w2, precision=HIGHEST) + map_b2)
    selection = low(jax.nn.sigmoid(map_logit) * clip_keep[:, :, None])
    pooled = jnp.einsum('fpk,fpd->fkd', selection, clip_patches, precision=HIGHEST) * PATCHES ** (-0.5)
    tokens = low(low_back(pooled)).reshape(SEQ, D)
    normed1 = low(normalize(tokens, ln1_gain, ln1_bias))
    bias_three = jnp.concatenate([qv_bias[0], jnp.zeros_like(qv_bias[0]), qv_bias[1]])
    joined = low(low_back(jnp.dot(normed1, qkv_weight, precision=HIGHEST) + bias_three))
    queries = joined[:, :D].reshape(SEQ, HEADS, HEAD)
    keys_all = joined[:, D:2 * D].reshape(SEQ, HEADS, HEAD)
    values_all = joined[:, 2 * D:].reshape(SEQ, HEADS, HEAD)
    scores = low_back(jnp.einsum('qhe,khe->hqk', queries, keys_all, precision=HIGHEST) * HEAD ** (-0.5))
    probs_low = low(softmax_rows(scores))
    attended = low(low_back(jnp.einsum('hqk,khe->qhe', probs_low, values_all, precision=HIGHEST))).reshape(SEQ, D)
    branch = low_back(jnp.dot(attended, out_weight, precision=HIGHEST) + out_bias)
    mixed_rows = tokens + branch
    normed2 = low(normalize(mixed_rows, ln2_gain, ln2_bias))
    inner_pre = low_back(jnp.dot(normed2, fc1_weight, precision=HIGHEST) + fc1_bias)
    inner_act = low(gelu_tanh(inner_pre))
    outer_out = low_back(jnp.dot(inner_act, fc2_weight, precision=HIGHEST) + fc2_bias)
    return mixed_rows + outer_out

def reference(patches, keep, tl_gain, tl_bias, map_w1, map_b1, map_w2, map_b2, ln1_gain, ln1_bias, qkv_weight, qv_bias, out_weight, out_bias, ln2_gain, ln2_bias, fc1_weight, fc1_bias, fc2_weight, fc2_bias, cotangent):
    params = tuple((item.astype(jnp.float32) for item in (tl_gain, tl_bias, map_w1, map_b1, map_w2, map_b2, ln1_gain, ln1_bias, qkv_weight, qv_bias, out_weight, out_bias, ln2_gain, ln2_bias, fc1_weight, fc1_bias, fc2_weight, fc2_bias)))
    flat_inputs = patches.reshape(MICRO * CLIPS, FRAMES, PATCHES, D).astype(jnp.float32)
    flat_keep = keep.reshape(MICRO * CLIPS, FRAMES, PATCHES).astype(jnp.float32)
    checked = jax.checkpoint(clip_forward)

    def forward(params_in, inputs_in):

        def scan_step(carry, item):
            return (carry, checked(params_in, item[0], item[1]))
        _, stacked = lax.scan(scan_step, jnp.zeros((), jnp.float32), (inputs_in, flat_keep))
        return stacked
    outputs, pullback = jax.vjp(forward, params, flat_inputs)
    grad_params, grad_inputs = pullback(cotangent.reshape(MICRO * CLIPS, SEQ, D).astype(jnp.float32))
    layer_out = outputs.reshape(MICRO, CLIPS, SEQ, D).astype(jnp.bfloat16)
    patch_grad = grad_inputs.reshape(MICRO, CLIPS, FRAMES, PATCHES, D).astype(jnp.bfloat16)
    return (layer_out, patch_grad, grad_params[0], grad_params[1], grad_params[2], grad_params[3], grad_params[4], grad_params[5], grad_params[6], grad_params[7], grad_params[8], grad_params[9], grad_params[10], grad_params[11], grad_params[12], grad_params[13], grad_params[14], grad_params[15], grad_params[16], grad_params[17])
```

```python
import functools

import jax
import jax.numpy as jnp
from jax import lax
from jax.experimental import pallas as pl
from jax.experimental.pallas import tpu as pltpu
from jax.sharding import PartitionSpec as P

HEAD = 64
MAPS = 8
LANES = 128
EPS = 1e-06
GC = 0.7978845608028654
GA = 0.044715
BF = jnp.bfloat16
F32 = jnp.float32
VLIM = 61 * 1024 * 1024


def dot(a, b):
    return lax.dot_general(a, b, (((1,), (0,)), ((), ())), preferred_element_type=F32)


def dot_nt(a, b):
    return lax.dot_general(a, b, (((1,), (1,)), ((), ())), preferred_element_type=F32)


def dot_tn(a, b):
    return lax.dot_general(a, b, (((0,), (0,)), ((), ())), preferred_element_type=F32)


def gelu_parts(x):
    x2 = x * x
    t = jnp.tanh(GC * x * (1.0 + GA * x2))
    act = 0.5 * x * (1.0 + t)
    slope = 0.5 * (1.0 + t) + 0.5 * x * (1.0 - t * t) * (GC * (1.0 + 3.0 * GA * x2))
    return act, slope


def col(x, n):
    return pl.ds(pl.multiple_of(x, n), n)


def patch_fwd_kernel(
    blocks, per, rb, width, v_ref, w1_ref, w1s_ref, w2_ref, b2_ref, kx_ref, pool_ref, aux_ref, sel_ref, der_ref,
    vbuf, acc, rmat, delta, vsem,
):
    frames = rb // (kx_ref.shape[1] - 4)

    @pl.loop(0, blocks)
    def _(i):
        pltpu.make_async_copy(v_ref.at[pl.ds(i * rb, rb)], vbuf.at[pl.ds(i * rb, rb)], vsem.at[i]).start()

    r2 = lax.broadcasted_iota(jnp.int32, rmat.shape, 0)
    c2 = lax.broadcasted_iota(jnp.int32, rmat.shape, 1)
    rmat[...] = jnp.where(r2 // frames == c2, 1.0, 0.0).astype(BF)
    r1 = lax.broadcasted_iota(jnp.int32, delta.shape, 0)
    c1 = lax.broadcasted_iota(jnp.int32, delta.shape, 1)
    delta[...] = jnp.where(r1 % frames == c1 // MAPS, 1.0, 0.0)

    @pl.loop(0, blocks)
    def _(i):
        rows = pl.ds(pl.multiple_of(i * rb, 16), rb)
        pltpu.make_async_copy(v_ref.at[pl.ds(i * rb, rb)], vbuf.at[pl.ds(i * rb, rb)], vsem.at[i]).wait()
        v = vbuf[rows, :]
        mm = dot(v, w1_ref[...])
        mean = mm[:, 64:65] * (1.0 / width)
        sq = jnp.zeros((rb, LANES), F32)
        for k in range(width // LANES):
            c = v[:, k * LANES : (k + 1) * LANES].astype(F32) - mean
            sq = sq + c * c
        rstd = lax.rsqrt(jnp.sum(sq, axis=-1, keepdims=True) * (1.0 / width) + EPS)
        pre = rstd * (mm - mean * w1s_ref[0:1, :]) + w1s_ref[1:2, :]
        act, _ = gelu_parts(pre)
        logit = dot(act.astype(BF)[:, :64], w2_ref[...]) + b2_ref[...]
        sig = 1.0 / (1.0 + jnp.exp(-logit))
        mask = dot(rmat[...], kx_ref[i]) * delta[...]
        sm = sig * mask
        sel = sm.astype(BF)
        sel_ref[rows, :] = sel
        der_ref[rows, :] = (sm * (1.0 - sig)).astype(BF)
        lane = lax.broadcasted_iota(jnp.int32, (rb, LANES), 1)
        aux_ref[rows, :] = jnp.where(lane < 64, pre, jnp.where(lane < 96, mean, rstd))
        part = dot_tn(sel, v)

        @pl.when(i % per == 0)
        def _():
            acc[...] = part

        @pl.when(i % per != 0)
        def _():
            acc[...] += part

        @pl.when(i % per == per - 1)
        def _():
            pool_ref[i // per] = (acc[...] * ((rb // frames * per) ** -0.5)).astype(BF)


def patch_forward(v, w1aug, w1s, w2rep, b2rep, kx, groups, per):
    rows, width = v.shape
    blocks = kx.shape[0]
    rb = rows // blocks
    vm = pl.BlockSpec(memory_space=pltpu.VMEM)
    return pl.pallas_call(
        functools.partial(patch_fwd_kernel, blocks, per, rb, width),
        out_shape=(
            jax.ShapeDtypeStruct((groups, LANES, width), BF),
            jax.ShapeDtypeStruct((rows, LANES), F32),
            jax.ShapeDtypeStruct((rows, LANES), BF),
            jax.ShapeDtypeStruct((rows, LANES), BF),
        ),
        in_specs=[pl.BlockSpec(memory_space=pltpu.HBM)] + [vm] * 5,
        out_specs=(vm,) * 4,
        scratch_shapes=[
            pltpu.VMEM((rows, width), BF),
            pltpu.VMEM((LANES, width), F32),
            pltpu.VMEM((rb, kx.shape[1]), BF),
            pltpu.VMEM((rb, LANES), F32),
            pltpu.SemaphoreType.DMA((blocks,)),
        ],
        compiler_params=pltpu.CompilerParams(vmem_limit_bytes=VLIM),
    )(v, w1aug, w1s, w2rep, b2rep, kx)


def ln_stats(t):
    mean = jnp.mean(t, axis=-1, keepdims=True)
    c = t - mean
    rstd = lax.rsqrt(jnp.mean(c * c, axis=-1, keepdims=True) + EPS)
    return c * rstd, rstd


def token_kernel(
    tok, cot, wq, wo, w1, w2, vec, b1,
    out_ref, gq_ref, go_ref, g1_ref, g2_ref, gtok_ref, gvec_ref, gb1_ref,
    n1, joined, probs, att, mixed, n2, act, slope, gacc, gmix, gbr, gatt, gj, tr,
):
    n, d = tok.shape
    ff = w1.shape[1]
    seq = 256
    micros = n // seq
    pairs = d // LANES
    ch = 64
    cb = 256
    chunks = n // ch
    lane = lax.broadcasted_iota(jnp.int32, (1, LANES), 1)
    first = lane < HEAD

    def rows_of(i):
        return pl.ds(pl.multiple_of(i * ch, ch), ch)

    def transpose_into(src):
        @pl.loop(0, n // 128)
        def _(i):
            r = pl.ds(pl.multiple_of(i * 128, 128), 128)
            tr[:, r] = src[r, :].astype(F32).T.astype(BF)

    gvec_ref[...] = jnp.zeros(gvec_ref.shape, F32)

    def add_row(i, val):
        gvec_ref[i : i + 1, :] += jnp.sum(val, axis=0, keepdims=True)

    @pl.loop(0, chunks)
    def _(i):
        xh, _ = ln_stats(tok[rows_of(i), :].astype(F32))
        n1[rows_of(i), :] = (xh * vec[0:1, :] + vec[1:2, :]).astype(BF)

    for blk in range(3):
        @pl.loop(0, d // cb)
        def _(j):
            o = pl.multiple_of(blk * d + j * cb, cb)
            r = dot(n1[...], wq[:, pl.ds(o, cb)])
            if blk == 0:
                r = r + vec[2:3, col(j * cb, cb)]
            if blk == 2:
                r = r + vec[3:4, col(j * cb, cb)]
            joined[:, pl.ds(o, cb)] = r.astype(BF)

    def heads_of(ref, i, base):
        m, pr = i // pairs, i % pairs
        r = pl.ds(pl.multiple_of(m * seq, seq), seq)
        return ref[r, pl.ds(pl.multiple_of(base + pr * LANES, LANES), LANES)]

    def put_heads(ref, i, base, val):
        m, pr = i // pairs, i % pairs
        r = pl.ds(pl.multiple_of(m * seq, seq), seq)
        ref[r, pl.ds(pl.multiple_of(base + pr * LANES, LANES), LANES)] = val

    zero = jnp.zeros((seq, LANES), BF)

    @pl.loop(0, micros * pairs)
    def _(i):
        q = (heads_of(joined, i, 0).astype(F32) * (HEAD**-0.5)).astype(BF)
        k = heads_of(joined, i, d)
        v = heads_of(joined, i, 2 * d)
        total = jnp.zeros((seq, LANES), F32)
        for e in range(2):
            mine = first if e == 0 else jnp.logical_not(first)
            s = dot_nt(jnp.where(mine, q, zero), k)
            ex = jnp.exp(s - jnp.max(s, axis=-1, keepdims=True))
            p = ex / jnp.sum(ex, axis=-1, keepdims=True)
            probs[i * 2 + e] = p
            total = total + dot(p.astype(BF), jnp.where(mine, v, zero))
        put_heads(att, i, 0, total.astype(BF))

    @pl.loop(0, d // cb)
    def _(j):
        c = col(j * cb, cb)
        mixed[:, c] = tok[:, c].astype(F32) + (dot(att[...], wo[:, c]) + vec[4:5, c])

    @pl.loop(0, chunks)
    def _(i):
        xh, _ = ln_stats(mixed[rows_of(i), :])
        n2[rows_of(i), :] = (xh * vec[5:6, :] + vec[6:7, :]).astype(BF)

    @pl.loop(0, ff // cb)
    def _(j):
        c = col(j * cb, cb)
        a, s = gelu_parts(dot(n2[...], w1[:, c]) + b1[0:1, c])
        act[:, c] = a.astype(BF)
        slope[:, c] = s.astype(BF)

    @pl.loop(0, ff // cb)
    def _(j):
        c = col(j * cb, cb)
        g2_ref[c, :] = dot_tn(act[:, c], cot[...]).astype(BF)

    @pl.loop(0, d // cb)
    def _(j):
        c = col(j * cb, cb)
        out_ref[:, c] = (mixed[:, c] + (dot(act[...], w2[:, c]) + vec[7:8, c])).astype(BF)

    transpose_into(n2)

    @pl.loop(0, ff // cb)
    def _(j):
        c = col(j * cb, cb)
        g = (dot_nt(cot[...], w2[c, :]) * slope[:, c].astype(F32)).astype(BF)
        act[:, c] = g
        gb1_ref[0:1, c] = jnp.sum(g.astype(F32), axis=0, keepdims=True)
        g1_ref[:, c] = dot(tr[...], g).astype(BF)

    @pl.loop(0, d // cb)
    def _(j):
        c = col(j * cb, cb)
        gacc[:, c] = dot_nt(act[...], w1[c, :])

    @pl.loop(0, chunks)
    def _(i):
        r = rows_of(i)
        xh, rstd = ln_stats(mixed[r, :])
        e = gacc[r, :]
        add_row(5, e * xh)
        add_row(6, e)
        eg = e * vec[5:6, :]
        back = eg - jnp.mean(eg, axis=-1, keepdims=True) - xh * jnp.mean(eg * xh, axis=-1, keepdims=True)
        c = cot[r, :].astype(F32)
        g = c + back * rstd
        gmix[r, :] = g
        low = g.astype(BF)
        gbr[r, :] = low
        add_row(4, low.astype(F32))
        add_row(7, c)

    transpose_into(att)

    @pl.loop(0, d // cb)
    def _(j):
        c = col(j * cb, cb)
        go_ref[:, c] = dot(tr[...], gbr[:, c]).astype(BF)
        gatt[:, c] = dot_nt(gbr[...], wo[c, :]).astype(BF)

    @pl.loop(0, micros * pairs)
    def _(i):
        q = (heads_of(joined, i, 0).astype(F32) * (HEAD**-0.5)).astype(BF)
        k = heads_of(joined, i, d)
        v = heads_of(joined, i, 2 * d)
        ga = heads_of(gatt, i, 0)
        gq = jnp.zeros((seq, LANES), F32)
        gk = jnp.zeros((seq, LANES), F32)
        gv = jnp.zeros((seq, LANES), F32)
        for e in range(2):
            mine = first if e == 0 else jnp.logical_not(first)
            p = probs[i * 2 + e]
            ga_e = jnp.where(mine, ga, zero)
            gp = dot_nt(ga_e, v)
            pg = p * gp
            gs = (pg - p * jnp.sum(pg, axis=-1, keepdims=True)).astype(BF)
            gv = gv + dot_tn(p.astype(BF), ga_e)
            gq = gq + dot(gs, jnp.where(mine, k, zero))
            gk = gk + dot_tn(gs, jnp.where(mine, q, zero))
        put_heads(gj, i, 0, (gq * (HEAD**-0.5)).astype(BF))
        put_heads(gj, i, d, gk.astype(BF))
        put_heads(gj, i, 2 * d, gv.astype(BF))

    transpose_into(n1)

    @pl.loop(0, 3 * d // cb)
    def _(j):
        c = col(j * cb, cb)
        gq_ref[:, c] = dot(tr[...], gj[:, c]).astype(BF)

    @pl.loop(0, d // cb)
    def _(j):
        c = col(j * cb, cb)
        gacc[:, c] = dot_nt(gj[...], wq[c, :])

    @pl.loop(0, chunks)
    def _(i):
        r = rows_of(i)
        xh, rstd = ln_stats(tok[r, :].astype(F32))
        e = gacc[r, :]
        add_row(0, e * xh)
        add_row(1, e)
        add_row(2, gj[r, 0:d].astype(F32))
        add_row(3, gj[r, 2 * d : 3 * d].astype(F32))
        eg = e * vec[0:1, :]
        back = eg - jnp.mean(eg, axis=-1, keepdims=True) - xh * jnp.mean(eg * xh, axis=-1, keepdims=True)
        gtok_ref[r, :] = (gmix[r, :] + back * rstd).astype(BF)


def token_layer(tok, cot, wq, wo, w1, w2, vec, b1):
    n, d = tok.shape
    ff = w1.shape[1]
    vm = pl.BlockSpec(memory_space=pltpu.VMEM)
    sds = jax.ShapeDtypeStruct
    heads = (n // 256) * (d // HEAD)
    return pl.pallas_call(
        token_kernel,
        out_shape=(
            sds((n, d), BF), sds((d, 3 * d), BF), sds((d, d), BF), sds((d, ff), BF), sds((ff, d), BF), sds((n, d), BF),
            sds((8, d), F32), sds((1, ff), F32),
        ),
        in_specs=[vm] * 8,
        out_specs=(vm,) * 8,
        scratch_shapes=[
            pltpu.VMEM((n, d), BF),
            pltpu.VMEM((n, 3 * d), BF),
            pltpu.VMEM((heads, 256, 256), F32),
            pltpu.VMEM((n, d), BF),
            pltpu.VMEM((n, d), F32),
            pltpu.VMEM((n, d), BF),
            pltpu.VMEM((n, ff), BF),
            pltpu.VMEM((n, ff), BF),
            pltpu.VMEM((n, d), F32),
            pltpu.VMEM((n, d), F32),
            pltpu.VMEM((n, d), BF),
            pltpu.VMEM((n, d), BF),
            pltpu.VMEM((n, 3 * d), BF),
            pltpu.VMEM((d, n), BF),
        ],
        compiler_params=pltpu.CompilerParams(vmem_limit_bytes=VLIM),
    )(tok, cot, wq, wo, w1, w2, vec, b1)


def patch_bwd_kernel(
    blocks, per, rb, width, v_ref, aux_hbm, sel_ref, der_hbm, gt_ref, w1s_ref, w2_ref,
    co_hbm, x_ref, w2g_ref, row_ref,
    vbuf, aux_ref, der_ref, co_ref, vsem, asem, dsem, csem,
):
    def copies(i):
        r = pl.ds(i * rb, rb)
        return (
            pltpu.make_async_copy(v_ref.at[r], vbuf.at[r], vsem.at[i]),
            pltpu.make_async_copy(aux_hbm.at[r], aux_ref.at[r], asem.at[i]),
            pltpu.make_async_copy(der_hbm.at[r], der_ref.at[r], dsem.at[i]),
        )

    def put(i):
        r = pl.ds(i * rb, rb)
        return pltpu.make_async_copy(co_ref.at[r], co_hbm.at[r], csem.at[i])

    @pl.loop(0, blocks)
    def _(i):
        for c in copies(i):
            c.start()

    x_ref[...] = jnp.zeros(x_ref.shape, F32)
    w2g_ref[...] = jnp.zeros(w2g_ref.shape, F32)
    row_ref[...] = jnp.zeros(row_ref.shape, F32)
    lane = lax.broadcasted_iota(jnp.int32, (rb, LANES), 1)

    @pl.loop(0, blocks)
    def _(i):
        rows = pl.ds(pl.multiple_of(i * rb, 16), rb)
        for c in copies(i):
            c.wait()
        v = vbuf[rows, :]
        aux = aux_ref[rows, :]
        mean = aux[:, 64:65]
        rstd = aux[:, 127:128]
        g = dot_nt(v, gt_ref[i // per])
        gl_f = g * der_ref[rows, :].astype(F32)
        gl = gl_f.astype(BF)
        ga = dot_nt(gl, w2_ref[...])
        pre = jnp.where(lane < 64, aux, 0.0)
        act, slope = gelu_parts(pre)
        gmp = (ga * slope).astype(BF).astype(F32)
        u = (gmp * rstd).astype(BF)
        uf = u.astype(F32)
        m1 = jnp.sum(gmp * w1s_ref[0:1, :], axis=-1, keepdims=True) * (1.0 / width)
        m2 = jnp.sum(gmp * (pre - w1s_ref[1:2, :]), axis=-1, keepdims=True) * (1.0 / width)
        w2g_ref[...] += dot_tn(act.astype(BF)[:, :64], gl)
        x_ref[...] += dot_tn(u[:, :64], v)
        row_ref[0:1, :] += jnp.sum(gl_f, axis=0, keepdims=True)
        row_ref[1:2, :] += jnp.sum(gmp, axis=0, keepdims=True)
        row_ref[2:3, :] += jnp.sum(uf * mean, axis=0, keepdims=True)
        c1 = -rstd * m1
        s = -rstd * rstd * m2
        c1h, sh, mh = (t.astype(BF).astype(F32) for t in (c1, s, mean))
        ex = jnp.where(lane < 64, uf, 0.0)
        for pos, val in enumerate((c1h, c1 - c1h, sh, s - sh, mh, mean - mh)):
            ex = jnp.where(lane == 64 + pos, val, ex)
        co_ref[rows, :] = ex.astype(BF)
        put(i).start()

    @pl.loop(0, blocks)
    def _(i):
        put(i).wait()


def patch_backward(v, aux, sel, der, gts, w1s, w2rep, blocks, per):
    rows, width = v.shape
    rb = rows // blocks
    vm = pl.BlockSpec(memory_space=pltpu.VMEM)
    hb = pl.BlockSpec(memory_space=pltpu.HBM)
    sds = jax.ShapeDtypeStruct
    return pl.pallas_call(
        functools.partial(patch_bwd_kernel, blocks, per, rb, width),
        out_shape=(sds((rows, LANES), BF), sds((64, width), F32), sds((64, LANES), F32), sds((8, LANES), F32)),
        in_specs=[hb, hb, hb, hb, vm, vm, vm],
        out_specs=(hb, vm, vm, vm),
        scratch_shapes=[
            pltpu.VMEM((rows, width), BF),
            pltpu.VMEM((rows, LANES), F32),
            pltpu.VMEM((rows, LANES), BF),
            pltpu.VMEM((rows, LANES), BF),
        ] + [pltpu.SemaphoreType.DMA((blocks,))] * 4,
        compiler_params=pltpu.CompilerParams(vmem_limit_bytes=VLIM),
    )(v, aux, sel, der, gts, w1s, w2rep)


def patch_out_kernel(v_ref, sel_ref, co_ref, gt_ref, bt_ref, o_ref):
    co = co_ref[...]
    ex = co.astype(F32)
    s = ex[:, 66:67] + ex[:, 67:68]
    mean = ex[:, 68:69] + ex[:, 69:70]
    left = jnp.concatenate([sel_ref[...], co], axis=1)
    right = jnp.concatenate([gt_ref[0], bt_ref[...]], axis=0)
    mm = dot(left, right)
    for k in range(v_ref.shape[1] // LANES):
        c = slice(k * LANES, (k + 1) * LANES)
        o_ref[:, c] = (mm[:, c] + (v_ref[:, c].astype(F32) - mean) * s).astype(BF)


def patch_out(v, sel, co, gts, bt, blocks, per):
    rows, width = v.shape
    rb = rows // blocks
    row = pl.BlockSpec((rb, width), lambda i: (i, 0))
    thin = pl.BlockSpec((rb, LANES), lambda i: (i, 0))
    return pl.pallas_call(
        patch_out_kernel,
        grid=(blocks,),
        out_shape=jax.ShapeDtypeStruct((rows, width), BF),
        in_specs=[
            row, thin, thin,
            pl.BlockSpec((1, LANES, width), lambda i: (i // per, 0, 0)),
            pl.BlockSpec((LANES, width), lambda i: (0, 0)),
        ],
        out_specs=row,
        compiler_params=pltpu.CompilerParams(vmem_limit_bytes=VLIM),
    )(v, sel, co, gts, bt)


def on_device(
    patches, keep, tl_gain, tl_bias, map_w1, map_b1, map_w2, map_b2, ln1_gain, ln1_bias, qkv_weight, qv_bias,
    out_weight, out_bias, ln2_gain, ln2_bias, fc1_weight, fc1_bias, fc2_weight, fc2_bias, cotangent,
):
    micros, group, frames, count, width = patches.shape
    groups = micros * group
    shard = tl_gain.shape[0]
    me = lax.axis_index("clip")
    per = 7
    blocks = groups * per
    pb = count // per
    rb = pb * frames
    v = jnp.transpose(patches, (0, 1, 3, 2, 4)).reshape(groups * count * frames, width)
    kx = jnp.transpose(keep, (0, 1, 3, 2)).reshape(blocks, pb, frames)
    kx = jnp.repeat(kx, MAPS, axis=2).astype(BF)
    kx = jnp.pad(kx, ((0, 0), (0, 4), (0, LANES - frames * MAPS)))
    gather = functools.partial(lax.all_gather, axis_name="clip", tiled=True)
    gain, bias, w1, b1, w2 = (gather(t).astype(F32) for t in (tl_gain, tl_bias, map_w1, map_b1, map_w2))
    gw1 = (gain[:, None] * w1).astype(BF)
    w1aug = jnp.concatenate([gw1, jnp.ones((width, 1), BF), jnp.zeros((width, 63), BF)], axis=1)
    csum = jnp.sum(gw1.astype(F32), axis=0)
    w1s = jnp.zeros((8, LANES), F32).at[0, :64].set(csum).at[1, :64].set(b1 + bias @ w1)
    w2rep = jnp.tile(w2.astype(BF), (1, LANES // MAPS))
    b2rep = jnp.tile(map_b2.astype(F32), LANES // MAPS)[None]
    bt = jnp.concatenate([gw1.T, jnp.ones((2, width), BF), jnp.zeros((62, width), BF)], axis=0)
    pool, aux, sel, der = patch_forward(v, w1aug, w1s, w2rep, b2rep, kx, groups, per)
    pool = pool[:, : frames * MAPS].reshape(micros, group, frames * MAPS, width)
    tok = lax.all_to_all(pool, "map", split_axis=1, concat_axis=2, tiled=True)
    tok = tok.reshape(-1, width)
    vecs = jnp.stack([ln1_gain, ln1_bias, qv_bias[0], qv_bias[1], out_bias, ln2_gain, ln2_bias, fc2_bias])
    vec = gather(vecs, axis=1).astype(F32)
    fb = gather(fc1_bias).astype(F32)[None]
    wq, wo, wf1, wf2 = (gather(t) for t in (qkv_weight, out_weight, fc1_weight, fc2_weight))
    out, gq, go, g1, g2, gtok, gvec, gb1 = token_layer(tok, cotangent.reshape(tok.shape), wq, wo, wf1, wf2, vec, fb)
    gts = lax.all_to_all(
        gtok.reshape(micros, 1, -1, width), "map", split_axis=2, concat_axis=1, tiled=True
    ).reshape(groups, frames * MAPS, width)
    gts = (gts.astype(F32) * count**-0.5).astype(BF)
    gts = jnp.pad(gts, ((0, 0), (0, LANES - frames * MAPS), (0, 0)))
    w2n = jnp.pad(w2rep, ((0, 64), (0, 0)))
    co, xt, w2g, row = patch_backward(v, aux, sel, der, gts, w1s, w2n, blocks, per)
    pg = patch_out(v, sel, co, gts, bt, blocks, per)
    pg = jnp.transpose(pg.reshape(micros, group, count, frames, width), (0, 1, 3, 2, 4))
    x = (xt - row[2, :64][:, None]).T
    w2g = jnp.sum(w2g.reshape(64, LANES // MAPS, MAPS), axis=1)
    b2g = jnp.sum(row[0].reshape(LANES // MAPS, MAPS), axis=0)

    def scatter(t, axis=0):
        t = lax.psum_scatter(t.astype(BF), "clip", scatter_dimension=axis, tiled=True)
        return lax.psum(t, "map").astype(F32)

    xs = scatter(x)
    gb = lax.psum(row[1, :64], ("clip", "map"))
    b2g = lax.psum(b2g, ("clip", "map"))
    gvec = scatter(gvec, 1)
    gains, biases, w1l = tl_gain.astype(F32), tl_bias.astype(F32), map_w1.astype(F32)
    n_map = shard * 64 // width
    return (
        out.reshape(cotangent.shape),
        pg,
        jnp.sum(w1l * xs, axis=1),
        w1l @ gb,
        gains[:, None] * xs + biases[:, None] * gb[None],
        lax.dynamic_slice(gb, (me * n_map,), (n_map,)),
        scatter(w2g),
        b2g,
        gvec[0],
        gvec[1],
        scatter(gq),
        gvec[2:4],
        scatter(go),
        gvec[4],
        gvec[5],
        gvec[6],
        scatter(g1),
        scatter(gb1[0]),
        scatter(g2),
        gvec[7],
    )


def solution(mesh):
    weights = (
        P("clip"), P("clip"), P("clip", None), P("clip"), P("clip", None), P(), P("clip"), P("clip"), P("clip", None),
        P(None, "clip"), P("clip", None), P("clip"), P("clip"), P("clip"), P("clip", None), P("clip"), P("clip", None),
        P("clip"),
    )
    tokens = P(None, ("clip", "map"), None, None)
    frames = P(None, "clip", "map", None, None)
    return jax.shard_map(
        on_device,
        mesh=mesh,
        in_specs=(frames, P(None, "clip", "map", None)) + weights + (tokens,),
        out_specs=(tokens, frames) + weights,
        check_vma=False,
    )
```

```python
import functools

import jax
import jax.numpy as jnp
from jax import lax
from jax.experimental import pallas as pl
from jax.experimental.pallas import tpu as pltpu
from jax.sharding import PartitionSpec as P

HEAD = 64
MAPS = 8
LANES = 128
EPS = 1e-06
GC = 0.7978845608028654
GA = 0.044715
BF = jnp.bfloat16
F32 = jnp.float32
VLIM = 61 * 1024 * 1024


def dot(a, b):
    return lax.dot_general(a, b, (((1,), (0,)), ((), ())), preferred_element_type=F32)


def dot_nt(a, b):
    return lax.dot_general(a, b, (((1,), (1,)), ((), ())), preferred_element_type=F32)


def dot_tn(a, b):
    return lax.dot_general(a, b, (((0,), (0,)), ((), ())), preferred_element_type=F32)


def gelu_parts(x):
    x2 = x * x
    t = jnp.tanh(GC * x * (1.0 + GA * x2))
    act = 0.5 * x * (1.0 + t)
    slope = 0.5 * (1.0 + t) + 0.5 * x * (1.0 - t * t) * (GC * (1.0 + 3.0 * GA * x2))
    return act, slope


def col(x, n):
    return pl.ds(pl.multiple_of(x, n), n)


MESH = pl.DeviceIdType.MESH


class Place:
    def __init__(self, n, m):
        self.n, self.m, self.na = n, m, n // 4
        self.clip, self.map = lax.axis_index("clip"), lax.axis_index("map")
        self.a, self.b, self.c = self.clip // 4, (self.clip // 2) % 2, self.clip % 2
        self.half = self.map % 2
        self.twin = self.map + 1 - 2 * self.half
        self.core_dev = (self.shard(self.a, self.b, 1 - self.c), self.map)
        self.y_dev = (self.shard(self.a, 1 - self.b, self.c), self.map)
        self.x_dev = (self.clip, self.twin)

    def shard(self, a, b, c):
        return (a * 2 + b) * 2 + c

    def back(self, k):
        return lax.rem(self.a + self.na - k, self.na)

    def ahead(self, k):
        return lax.rem(self.a + k, self.na)

    def greet(self):
        bar = pltpu.get_barrier_semaphore()
        for k in range(1, self.n):
            pl.semaphore_signal(bar, inc=1, device_id=(lax.rem(self.clip + k, self.n), self.map), device_id_type=MESH)
        for k in range(1, self.m):
            pl.semaphore_signal(bar, inc=1, device_id=(self.clip, lax.rem(self.map + k, self.m)), device_id_type=MESH)
        pl.semaphore_wait(bar, self.n + self.m - 2)


def remote(src, dst, send, recv, dev):
    return pltpu.make_async_remote_copy(
        src_ref=src, dst_ref=dst, send_sem=send, recv_sem=recv, device_id=dev, device_id_type=MESH
    )


class Gather:
    def __init__(self, place, chunks, sends, recvs):
        self.p, self.chunks, self.sends, self.recvs = place, chunks, sends, recvs
        self.started = []

    def block(self, i, s, half):
        ref, panels, rows, pitch, skip, _ = self.chunks[i]
        r = pl.ds(pl.multiple_of(s * pitch + skip, 8), rows)
        c = slice(None) if half is None else pl.ds(pl.multiple_of(half * (ref.shape[-1] // 2), LANES), ref.shape[-1] // 2)
        return ref.at[r, c] if panels is None else ref.at[panels, r, c]

    def send(self, i, at, dev, s, half):
        b = self.block(i, s, half)
        j = i * self.per() + at
        remote(b, b, self.sends.at[j], self.recvs.at[j], dev).start()
        self.started.append((i, j, half is None))

    def wait(self, i, at, s, half):
        b = self.block(i, s, half)
        j = i * self.per() + at
        remote(b, b, self.sends.at[j], self.recvs.at[j], self.p.core_dev).wait_recv()

    def per(self):
        return 11 * self.p.na

    def at_z(self, k):
        return k - 1

    def at_y(self, k):
        return self.p.na - 1 + k

    def at_x(self, side, k):
        return (2 + side) * self.p.na + k

    def at_diag_y(self, k):
        return 4 * self.p.na + k

    def at_core(self, e):
        return 5 * self.p.na + e

    def own(self, i):
        p = self.p
        for k in range(1, p.na):
            self.send(i, self.at_z(k), (p.shard(p.ahead(k), p.b, p.c), p.map), p.clip, p.half)
        self.send(i, self.at_y(0), p.y_dev, p.clip, None)
        self.send(i, self.at_core(0), p.core_dev, p.clip, None)

    def by_x(self, i):
        return self.chunks[i][5]

    def from_z(self, i, k):
        p = self.p
        s = p.shard(p.back(k), p.b, p.c)
        self.wait(i, self.at_z(k), s, p.half)
        self.send(i, self.at_x(0, k), p.x_dev, s, p.half)
        self.send(i, self.at_y(k), p.y_dev, s, p.half)
        self.send(i, self.at_core(k), p.core_dev, s, p.half)

    def from_y(self, i, k):
        p = self.p
        if k == 0:
            s = p.shard(p.a, 1 - p.b, p.c)
            self.wait(i, self.at_y(0), s, None)
            self.send(i, self.at_core(p.na), p.core_dev, s, None)
            return
        s = p.shard(p.back(k), 1 - p.b, p.c)
        self.wait(i, self.at_y(k), s, p.half)
        if self.by_x(i):
            self.send(i, self.at_x(1, k), p.x_dev, s, p.half)
        self.send(i, self.at_core(p.na + k), p.core_dev, s, p.half)

    def from_x(self, i, side, k):
        p = self.p
        b = p.b if side == 0 else 1 - p.b
        s = p.shard(p.back(k), b, p.c)
        by_x = self.by_x(i)
        self.wait(i, self.at_x(side, k) if by_x or side == 0 else self.at_diag_y(k), s, 1 - p.half)
        if side == 0 and not by_x:
            self.send(i, self.at_diag_y(k), p.y_dev, s, 1 - p.half)
        self.send(i, self.at_core((2 + side) * p.na + k), p.core_dev, s, 1 - p.half)

    def from_core(self, i):
        p, o = self.p, 1 - self.p.c
        self.wait(i, self.at_core(0), p.shard(p.a, p.b, o), None)
        self.wait(i, self.at_core(p.na), p.shard(p.a, 1 - p.b, o), None)
        for k in range(1, p.na):
            for side in range(2):
                s = p.shard(p.back(k), p.b if side == 0 else 1 - p.b, o)
                self.wait(i, self.at_core(p.na * side + k), s, p.half)
                self.wait(i, self.at_core((2 + side) * p.na + k), s, 1 - p.half)

    def finish(self):
        for i in range(len(self.chunks)):
            self.from_core(i)
        for i, j, full in self.started:
            b = self.block(i, self.p.clip, None if full else self.p.half)
            remote(b, b, self.sends.at[j], self.recvs.at[j], self.p.core_dev).wait_send()

    def events(self):
        n, ks = len(self.chunks), range(1, self.p.na)
        call = functools.partial
        out = [call(self.own, i) for i in range(AHEAD)]
        for i in range(n + 2):
            if i < n:
                for k in ks:
                    out.append(call(self.from_z, i, k))
                    if k == self.p.na - 2 and i + AHEAD < n:
                        out.append(call(self.own, i + AHEAD))
                out.append(call(self.from_y, i, 0))
            if 0 <= i - 1 < n:
                out += [call(self.from_y, i - 1, k) for k in ks]
                out += [call(self.from_x, i - 1, 0, k) for k in ks]
            if 0 <= i - 2 < n:
                out += [call(self.from_x, i - 2, 1, k) for k in ks]
        return out


def forward_kernel(
    n, m, blocks, per, count, v_ref, kx_ref, b2_ref, pa_ref, pb_ref, wq_ref, wo_ref, w1_ref, w2_ref,
    wa_ref, wb_ref, tok_ref, aux_ref, sel_ref, der_ref, vec_ref, fb_ref, wt_ref, small_ref,
    vbuf, acc, pool, rmat, delta, pag, pbg, w1v, w2v, ss, vsem, lsem, gsend, grecv, psend, precv, tsend, trecv,
):
    rows, width = v_ref.shape
    rb = rows // blocks
    frames = rb // (kx_ref.shape[1] - 4)
    fm = tok_ref.shape[2]
    me = Place(n, m)
    shard = width // n
    ff = w1_ref.shape[1]
    fsh = ff // n

    @pl.loop(0, blocks)
    def _(i):
        pltpu.make_async_copy(v_ref.at[pl.ds(i * rb, rb)], vbuf.at[pl.ds(i * rb, rb)], vsem.at[i]).start()

    own = pl.ds(pl.multiple_of(me.clip * shard, 8), shard)
    local = []
    for p in range(3):
        local.append((wq_ref.at[:, pl.ds(p * width, width)], wa_ref.at[p, own]))
    local.append((wo_ref, wa_ref.at[3, own]))
    for p in range(ff // width):
        local.append((w1_ref.at[:, pl.ds(p * width, width)], wa_ref.at[4 + p, own]))
    local.append((w2_ref, wb_ref.at[pl.ds(pl.multiple_of(me.clip * fsh, 8), fsh)]))
    local.append((pa_ref, pag.at[me.clip]))
    local.append((pb_ref, pbg.at[me.clip]))
    local = [pltpu.make_async_copy(s, d, lsem.at[i]) for i, (s, d) in enumerate(local)]
    for d in local:
        d.start()
    me.greet()
    small = []
    for k in range(1, n):
        dev = (lax.rem(me.clip + k, n), me.map)
        small.append(remote(pa_ref, pag.at[me.clip], psend.at[0, k], precv.at[0, k], dev))
        small[-1].start()
    for d in local:
        d.wait()
    chunks = [(wa_ref, pl.ds(2 * q, 2), shard, shard, 0, True) for q in range(4)]
    chunks += [(wb_ref, None, fsh // 2, fsh, q * (fsh // 2), q == 0) for q in range(2)]
    g = Gather(me, chunks, gsend, grecv)
    todo = g.events()
    slots = [[] for _ in range(blocks + 1)]
    for at, f in enumerate(todo[AHEAD:]):
        slots[min(int(at * STEP * blocks / len(todo)), blocks)].append(f)
    for f in todo[:AHEAD]:
        f()
    for k in range(1, n):
        dev = (lax.rem(me.clip + k, n), me.map)
        small.append(remote(pb_ref, pbg.at[me.clip], psend.at[1, k], precv.at[1, k], dev))
        small[-1].start()

    r2 = lax.broadcasted_iota(jnp.int32, rmat.shape, 0)
    c2 = lax.broadcasted_iota(jnp.int32, rmat.shape, 1)
    rmat[...] = jnp.where(r2 // frames == c2, 1.0, 0.0).astype(BF)
    r1 = lax.broadcasted_iota(jnp.int32, delta.shape, 0)
    c1 = lax.broadcasted_iota(jnp.int32, delta.shape, 1)
    delta[...] = jnp.where(r1 % frames == c1 // MAPS, 1.0, 0.0)

    for k in range(1, n):
        s = lax.rem(me.clip + n - k, n)
        remote(pa_ref, pag.at[s], psend.at[0, k], precv.at[0, k], me.core_dev).wait_recv()
    par = pa_ref.shape[0]
    flat = pag[...].reshape(n * par, LANES)
    q2 = 64 // n

    def pick(lo, count_rows, want_s, want_j):
        r = lax.broadcasted_iota(jnp.int32, (count_rows, 1), 0) + lo
        kk = lax.broadcasted_iota(jnp.int32, (1, n * par), 1)
        s, j = kk // par, kk % par
        sel = jnp.logical_and(s == want_s(r), j == want_j(r))
        return dot(jnp.where(sel, 1.0, 0.0).astype(BF), flat)

    lane = lax.broadcasted_iota(jnp.int32, (1, LANES), 1)
    for q in range(width // 128):
        got = pick(q * 128, 128, lambda r: r // shard, lambda r: r % shard)
        got = jnp.where(lane < 64, got, jnp.where(lane == 64, 1.0, 0.0))
        w1v[q * 128 : (q + 1) * 128, :] = got.astype(BF)
        wt_ref[0:64, q * 128 : (q + 1) * 128] = got.T[0:64, :].astype(BF)
    tail = lax.broadcasted_iota(jnp.int32, (64, width), 0)
    wt_ref[64:128, :] = jnp.where(tail < 2, 1.0, 0.0).astype(BF)
    got = pick(0, 64, lambda r: r // q2, lambda r: shard + 1 + r % q2)
    w2v[...] = got.astype(BF)
    small_ref[...] = jnp.zeros(small_ref.shape, F32)
    small_ref[8:72, :] = got
    r = lax.broadcasted_iota(jnp.int32, (8, 1), 0)
    kk = lax.broadcasted_iota(jnp.int32, (1, n * par), 1) % par
    sums = dot(jnp.where(jnp.logical_or(jnp.logical_and(r == 0, kk < shard), jnp.logical_and(r == 1, kk == shard)), 1.0, 0.0).astype(BF), flat)
    csum = jnp.where(lane < 64, sums[0:1, :], 0.0)
    cadd = jnp.where(lane < 64, pltpu.roll(sums, 64, 1)[0:1, :] + sums[1:2, :], 0.0)
    ss[0:1, :] = csum
    ss[1:2, :] = cadd
    small_ref[0:1, :] = csum
    small_ref[1:2, :] = cadd

    @pl.loop(0, blocks)
    def _(i):
        for at, fs in enumerate(slots[:blocks]):
            if fs:

                @pl.when(i == at)
                def _():
                    for f in fs:
                        f()

        rr = pl.ds(pl.multiple_of(i * rb, 16), rb)
        pltpu.make_async_copy(v_ref.at[pl.ds(i * rb, rb)], vbuf.at[pl.ds(i * rb, rb)], vsem.at[i]).wait()
        v = vbuf[rr, :]
        mm = dot(v, w1v[...])
        mean = mm[:, 64:65] * (1.0 / width)
        sq = jnp.zeros((rb, LANES), F32)
        for k in range(width // LANES):
            c = v[:, k * LANES : (k + 1) * LANES].astype(F32) - mean
            sq = sq + c * c
        rstd = lax.rsqrt(jnp.sum(sq, axis=-1, keepdims=True) * (1.0 / width) + EPS)
        pre = rstd * (mm - mean * ss[0:1, :]) + ss[1:2, :]
        act, _ = gelu_parts(pre)
        logit = dot(act.astype(BF)[:, :64], w2v[...]) + b2_ref[...]
        sig = 1.0 / (1.0 + jnp.exp(-logit))
        mask = dot(rmat[...], kx_ref[i]) * delta[...]
        sm = sig * mask
        sel = sm.astype(BF)
        sel_ref[rr, :] = sel
        der_ref[rr, :] = (sm * (1.0 - sig)).astype(BF)
        ln = lax.broadcasted_iota(jnp.int32, (rb, LANES), 1)
        aux_ref[rr, :] = jnp.where(ln < 64, pre, jnp.where(ln < 96, mean, rstd))
        part = dot_tn(sel, v)

        @pl.when(i % per == 0)
        def _():
            acc[...] = part

        @pl.when(i % per != 0)
        def _():
            acc[...] += part

        @pl.when(i % per == per - 1)
        def _():
            pool[i // per] = (acc[...] * (count**-0.5)).astype(BF)

    micros = tok_ref.shape[0]
    out = []
    for mi in range(micros):
        for k in range(1, m):
            j = lax.rem(me.map + k, m)
            d = remote(
                pool.at[mi * m + j, pl.ds(0, fm)], tok_ref.at[mi, me.map], tsend.at[mi * m + k], trecv.at[mi * m + k], (me.clip, j)
            )
            d.start()
            out.append(d)
        mine = pltpu.make_async_copy(pool.at[mi * m + me.map, pl.ds(0, fm)], tok_ref.at[mi, me.map], tsend.at[mi * m])
        mine.start()
        mine.wait()
    for f in slots[blocks]:
        f()
    for k in range(1, n):
        s = lax.rem(me.clip + n - k, n)
        remote(pb_ref, pbg.at[s], psend.at[1, k], precv.at[1, k], me.core_dev).wait_recv()
    wide = pb_ref.shape[1]
    each = wide // shard
    for q in range(width // wide):
        t = pbg[q * each].astype(F32)
        for s in range(q * each + 1, (q + 1) * each):
            t = t + pbg[s].astype(F32)
        vec_ref[:, q * wide : (q + 1) * wide] = t[0:8, :]
    each = wide // fsh
    for q in range(ff // wide):
        t = pbg[q * each].astype(F32)
        for s in range(q * each + 1, (q + 1) * each):
            t = t + pbg[s].astype(F32)
        fb_ref[:, q * wide : (q + 1) * wide] = t[8:9, :]
    for mi in range(micros):
        for k in range(1, m):
            j = lax.rem(me.map + m - k, m)
            remote(
                pool.at[mi * m + j, pl.ds(0, fm)], tok_ref.at[mi, j], tsend.at[mi * m + k], trecv.at[mi * m + k], me.core_dev
            ).wait_recv()
    g.finish()
    for d in small + out:
        d.wait_send()


STEP = 1.0
AHEAD = 3


def forward(n, m, v, kx, b2rep, pa, pb, wq, wo, w1, w2, micros, frames, per, count):
    rows, width = v.shape
    blocks = kx.shape[0]
    rb = rows // blocks
    ff = w1.shape[1]
    groups = blocks // per
    copies = 6 * 11 * (n // 4)
    sds = jax.ShapeDtypeStruct
    vm = pl.BlockSpec(memory_space=pltpu.VMEM)
    hb = pl.BlockSpec(memory_space=pltpu.HBM)
    dma = pltpu.SemaphoreType.DMA
    return pl.pallas_call(
        functools.partial(forward_kernel, n, m, blocks, per, count),
        out_shape=(
            sds((8, width, width), BF),
            sds((ff, width), BF),
            sds((micros, m, frames * MAPS, width), BF),
            sds((rows, LANES), F32),
            sds((rows, LANES), BF),
            sds((rows, LANES), BF),
            sds((8, width), F32),
            sds((1, ff), F32),
            sds((LANES, width), BF),
            sds((72, LANES), F32),
        ),
        in_specs=[hb, vm, vm, vm, vm, hb, hb, hb, hb],
        out_specs=(hb, hb, hb) + (vm,) * 7,
        scratch_shapes=[
            pltpu.VMEM((rows, width), BF),
            pltpu.VMEM((LANES, width), F32),
            pltpu.VMEM((groups, LANES, width), BF),
            pltpu.VMEM((rb, kx.shape[1]), BF),
            pltpu.VMEM((rb, LANES), F32),
            pltpu.VMEM((n,) + pa.shape, BF),
            pltpu.VMEM((n,) + pb.shape, BF),
            pltpu.VMEM((width, LANES), BF),
            pltpu.VMEM((64, LANES), BF),
            pltpu.VMEM((8, LANES), F32),
            dma((blocks,)), dma((16,)), dma((copies,)), dma((copies,)), dma((2, n)), dma((2, n)),
            dma((micros * m,)), dma((micros * m,)),
        ],
        compiler_params=pltpu.CompilerParams(vmem_limit_bytes=VLIM, collective_id=0, has_side_effects=True),
    )(v, kx, b2rep, pa, pb, wq, wo, w1, w2)


def ln_stats(t):
    mean = jnp.mean(t, axis=-1, keepdims=True)
    c = t - mean
    rstd = lax.rsqrt(jnp.mean(c * c, axis=-1, keepdims=True) + EPS)
    return c * rstd, rstd


def token_kernel(
    tok, cot, wa, w2, vec, b1,
    out_ref, ga_ref, g2_ref, gtok_ref, gvec_ref, gb1_ref,
    n1, joined, probs, att, mixed, n2, act, slope, gacc, gmix, gbr, gatt, gj, tr,
):
    n, d = tok.shape
    ff = w2.shape[0]
    per = d // 256
    seq = 256
    micros = n // seq
    pairs = d // LANES
    ch = 64
    cb = 256
    chunks = n // ch
    lane = lax.broadcasted_iota(jnp.int32, (1, LANES), 1)
    first = lane < HEAD

    def rows_of(i):
        return pl.ds(pl.multiple_of(i * ch, ch), ch)

    def transpose_into(src):
        @pl.loop(0, n // 128)
        def _(i):
            r = pl.ds(pl.multiple_of(i * 128, 128), 128)
            tr[:, r] = src[r, :].astype(F32).T.astype(BF)

    gvec_ref[...] = jnp.zeros(gvec_ref.shape, F32)

    def add_row(i, val):
        gvec_ref[i : i + 1, :] += jnp.sum(val, axis=0, keepdims=True)

    @pl.loop(0, chunks)
    def _(i):
        xh, _ = ln_stats(tok[rows_of(i), :].astype(F32))
        n1[rows_of(i), :] = (xh * vec[0:1, :] + vec[1:2, :]).astype(BF)

    for blk in range(3):
        @pl.loop(0, d // cb)
        def _(j):
            o = pl.multiple_of(blk * d + j * cb, cb)
            r = dot(n1[...], wa[blk, :, col(j * cb, cb)])
            if blk == 0:
                r = r + vec[2:3, col(j * cb, cb)]
            if blk == 2:
                r = r + vec[3:4, col(j * cb, cb)]
            joined[:, pl.ds(o, cb)] = r.astype(BF)

    def heads_of(ref, i, base):
        m, pr = i // pairs, i % pairs
        r = pl.ds(pl.multiple_of(m * seq, seq), seq)
        return ref[r, pl.ds(pl.multiple_of(base + pr * LANES, LANES), LANES)]

    def put_heads(ref, i, base, val):
        m, pr = i // pairs, i % pairs
        r = pl.ds(pl.multiple_of(m * seq, seq), seq)
        ref[r, pl.ds(pl.multiple_of(base + pr * LANES, LANES), LANES)] = val

    zero = jnp.zeros((seq, LANES), BF)

    @pl.loop(0, micros * pairs)
    def _(i):
        q = (heads_of(joined, i, 0).astype(F32) * (HEAD**-0.5)).astype(BF)
        k = heads_of(joined, i, d)
        v = heads_of(joined, i, 2 * d)
        total = jnp.zeros((seq, LANES), F32)
        for e in range(2):
            mine = first if e == 0 else jnp.logical_not(first)
            s = dot_nt(jnp.where(mine, q, zero), k)
            ex = jnp.exp(s - jnp.max(s, axis=-1, keepdims=True))
            p = ex / jnp.sum(ex, axis=-1, keepdims=True)
            probs[i * 2 + e] = p
            total = total + dot(p.astype(BF), jnp.where(mine, v, zero))
        put_heads(att, i, 0, total.astype(BF))

    @pl.loop(0, d // cb)
    def _(j):
        c = col(j * cb, cb)
        mixed[:, c] = tok[:, c].astype(F32) + (dot(att[...], wa[3, :, c]) + vec[4:5, c])

    @pl.loop(0, chunks)
    def _(i):
        xh, _ = ln_stats(mixed[rows_of(i), :])
        n2[rows_of(i), :] = (xh * vec[5:6, :] + vec[6:7, :]).astype(BF)

    @pl.loop(0, ff // cb)
    def _(j):
        c = col(j * cb, cb)
        a, s = gelu_parts(dot(n2[...], wa[4 + j // per, :, col((j % per) * cb, cb)]) + b1[0:1, c])
        act[:, c] = a.astype(BF)
        slope[:, c] = s.astype(BF)

    @pl.loop(0, ff // cb)
    def _(j):
        c = col(j * cb, cb)
        g2_ref[c, :] = dot_tn(act[:, c], cot[...]).astype(BF)

    @pl.loop(0, d // cb)
    def _(j):
        c = col(j * cb, cb)
        out_ref[:, c] = (mixed[:, c] + (dot(act[...], w2[:, c]) + vec[7:8, c])).astype(BF)

    transpose_into(n2)

    @pl.loop(0, ff // cb)
    def _(j):
        c = col(j * cb, cb)
        g = (dot_nt(cot[...], w2[c, :]) * slope[:, c].astype(F32)).astype(BF)
        act[:, c] = g
        gb1_ref[0:1, c] = jnp.sum(g.astype(F32), axis=0, keepdims=True)
        ga_ref[4 + j // per, :, col((j % per) * cb, cb)] = dot(tr[...], g).astype(BF)

    @pl.loop(0, d // cb)
    def _(j):
        c = col(j * cb, cb)
        total = jnp.zeros((n, cb), F32)
        for q in range(ff // d):
            total = total + dot_nt(act[:, q * d : (q + 1) * d], wa[4 + q, c, :])
        gacc[:, c] = total

    @pl.loop(0, chunks)
    def _(i):
        r = rows_of(i)
        xh, rstd = ln_stats(mixed[r, :])
        e = gacc[r, :]
        add_row(5, e * xh)
        add_row(6, e)
        eg = e * vec[5:6, :]
        back = eg - jnp.mean(eg, axis=-1, keepdims=True) - xh * jnp.mean(eg * xh, axis=-1, keepdims=True)
        c = cot[r, :].astype(F32)
        g = c + back * rstd
        gmix[r, :] = g
        low = g.astype(BF)
        gbr[r, :] = low
        add_row(4, low.astype(F32))
        add_row(7, c)

    transpose_into(att)

    @pl.loop(0, d // cb)
    def _(j):
        c = col(j * cb, cb)
        ga_ref[3, :, c] = dot(tr[...], gbr[:, c]).astype(BF)
        gatt[:, c] = dot_nt(gbr[...], wa[3, c, :]).astype(BF)

    @pl.loop(0, micros * pairs)
    def _(i):
        q = (heads_of(joined, i, 0).astype(F32) * (HEAD**-0.5)).astype(BF)
        k = heads_of(joined, i, d)
        v = heads_of(joined, i, 2 * d)
        ga = heads_of(gatt, i, 0)
        gq = jnp.zeros((seq, LANES), F32)
        gk = jnp.zeros((seq, LANES), F32)
        gv = jnp.zeros((seq, LANES), F32)
        for e in range(2):
            mine = first if e == 0 else jnp.logical_not(first)
            p = probs[i * 2 + e]
            ga_e = jnp.where(mine, ga, zero)
            gp = dot_nt(ga_e, v)
            pg = p * gp
            gs = (pg - p * jnp.sum(pg, axis=-1, keepdims=True)).astype(BF)
            gv = gv + dot_tn(p.astype(BF), ga_e)
            gq = gq + dot(gs, jnp.where(mine, k, zero))
            gk = gk + dot_tn(gs, jnp.where(mine, q, zero))
        put_heads(gj, i, 0, (gq * (HEAD**-0.5)).astype(BF))
        put_heads(gj, i, d, gk.astype(BF))
        put_heads(gj, i, 2 * d, gv.astype(BF))

    transpose_into(n1)

    @pl.loop(0, 3 * d // cb)
    def _(j):
        c = col(j * cb, cb)
        ga_ref[j // per, :, col((j % per) * cb, cb)] = dot(tr[...], gj[:, c]).astype(BF)

    @pl.loop(0, d // cb)
    def _(j):
        c = col(j * cb, cb)
        total = jnp.zeros((n, cb), F32)
        for q in range(3):
            total = total + dot_nt(gj[:, q * d : (q + 1) * d], wa[q, c, :])
        gacc[:, c] = total

    @pl.loop(0, chunks)
    def _(i):
        r = rows_of(i)
        xh, rstd = ln_stats(tok[r, :].astype(F32))
        e = gacc[r, :]
        add_row(0, e * xh)
        add_row(1, e)
        add_row(2, gj[r, 0:d].astype(F32))
        add_row(3, gj[r, 2 * d : 3 * d].astype(F32))
        eg = e * vec[0:1, :]
        back = eg - jnp.mean(eg, axis=-1, keepdims=True) - xh * jnp.mean(eg * xh, axis=-1, keepdims=True)
        gtok_ref[r, :] = (gmix[r, :] + back * rstd).astype(BF)


def token_layer(tok, cot, wa, w2, vec, b1):
    n, d = tok.shape
    ff = w2.shape[0]
    vm = pl.BlockSpec(memory_space=pltpu.VMEM)
    sds = jax.ShapeDtypeStruct
    heads = (n // 256) * (d // HEAD)
    return pl.pallas_call(
        token_kernel,
        out_shape=(
            sds((n, d), BF), sds(wa.shape, BF), sds((ff, d), BF), sds((n, d), BF),
            sds((8, d), F32), sds((1, ff), F32),
        ),
        in_specs=[vm] * 6,
        out_specs=(vm,) * 6,
        scratch_shapes=[
            pltpu.VMEM((n, d), BF),
            pltpu.VMEM((n, 3 * d), BF),
            pltpu.VMEM((heads, 256, 256), F32),
            pltpu.VMEM((n, d), BF),
            pltpu.VMEM((n, d), F32),
            pltpu.VMEM((n, d), BF),
            pltpu.VMEM((n, ff), BF),
            pltpu.VMEM((n, ff), BF),
            pltpu.VMEM((n, d), F32),
            pltpu.VMEM((n, d), F32),
            pltpu.VMEM((n, d), BF),
            pltpu.VMEM((n, d), BF),
            pltpu.VMEM((n, 3 * d), BF),
            pltpu.VMEM((d, n), BF),
        ],
        compiler_params=pltpu.CompilerParams(vmem_limit_bytes=VLIM),
    )(tok, cot, wa, w2, vec, b1)


class Reduce:
    def __init__(self, place, chunks, own, rc, rx, ry, rz, rf, lsem, sends, recvs):
        self.p, self.chunks, self.own, self.rc, self.rx, self.ry, self.rz, self.rf = place, chunks, own, rc, rx, ry, rz, rf
        self.lsem, self.sends, self.recvs = lsem, sends, recvs

    def sem(self, i, at):
        j = i * 8 * self.p.na + at
        return self.sends.at[j], self.recvs.at[j]

    def send(self, i, at, src, dst, dev):
        s, r = self.sem(i, at)
        remote(src, dst, s, r, dev).start()

    def grad(self, i, k, side, core):
        p = self.p
        ref, panels, rows, pitch, skip, _ = self.chunks[i]
        s = p.shard(p.back(k), p.b if side == 0 else 1 - p.b, core)
        return ref.at[panels, pl.ds(pl.multiple_of(s * pitch + skip, 8), rows)]

    def cols(self, half):
        w = self.chunks[0][0].shape[-1] // 2
        return pl.ds(pl.multiple_of(half * w, LANES), w)

    def mine(self):
        return self.cols(self.p.half)

    def other(self):
        return self.cols(1 - self.p.half)

    def core_copies(self, i):
        p = self.p
        return [
            (2 * k + side, self.grad(i, k, side, 1 - p.c), self.rc[i].at[2 * k + side], p.core_dev)
            for k in range(p.na) for side in range(2)
        ]

    def local_copies(self, i):
        p = self.p
        return [
            pltpu.make_async_copy(self.grad(i, k, side, p.c), self.own[i].at[2 * k + side], self.lsem.at[i, 2 * k + side])
            for k in range(p.na) for side in range(2)
        ]

    def x_copies(self, i):
        p, base = self.p, 2 * self.p.na
        sides = range(2) if self.chunks[i][5] else range(1)
        return [
            (base + 2 * k + side, self.own[i].at[2 * k + side, :, :, self.other()], self.rx[i].at[2 * (k - 1) + side], p.x_dev)
            for k in range(1, p.na) for side in sides
        ]

    def y_copies(self, i):
        p, base = self.p, 4 * self.p.na
        out = []
        for k in range(p.na):
            src, dst = self.own[i].at[2 * k + 1], self.ry[i].at[k]
            if self.chunks[i][5] and k:
                src, dst = src.at[:, :, self.mine()], dst.at[:, :, self.mine()]
            out.append((base + k, src, dst, p.y_dev))
        return out

    def z_copies(self, i):
        p, base = self.p, 5 * self.p.na
        return [
            (base + k, self.own[i].at[2 * k, :, :, self.mine()], self.rz[i].at[k - 1], (p.shard(p.back(k), p.b, p.c), p.map))
            for k in range(1, p.na)
        ]

    def last_copies(self, i):
        return [(6 * self.p.na, self.own[i].at[0], self.rf[i], self.p.x_dev)]

    def start(self, i, copies):
        for at, src, dst, dev in copies:
            self.send(i, at, src, dst, dev)

    def wait(self, i, copies):
        for at, src, dst, dev in copies:
            s, r = self.sem(i, at)
            remote(dst, dst, s, r, self.p.core_dev).wait_recv()

    def add(self, ref, at, cols, inc):
        a = ref[at, :, :, cols]
        ref[at, :, :, cols] = (a.astype(F32) + inc.astype(F32)).astype(BF)

    def stage0(self, i):
        for c in self.local_copies(i):
            c.start()
        self.start(i, self.core_copies(i))

    def stage1(self, i):
        for c in self.local_copies(i):
            c.wait()
        self.wait(i, self.core_copies(i))

        @pl.loop(0, 2 * self.p.na)
        def _(j):
            self.own[i][j] = (self.own[i][j].astype(F32) + self.rc[i][j].astype(F32)).astype(BF)

        self.start(i, self.x_copies(i) if self.chunks[i][5] else self.y_copies(i))

    def add_x(self, i):
        self.wait(i, self.x_copies(i))
        both = self.chunks[i][5]

        @pl.loop(0, self.p.na - 1)
        def _(k):
            for side in range(2 if both else 1):
                self.add(self.own[i], 2 * k + 2 + side, self.mine(), self.rx[i][2 * k + side])

    def add_y(self, i):
        self.wait(i, self.y_copies(i))
        if not self.chunks[i][5]:

            @pl.loop(0, self.p.na)
            def _(k):
                self.own[i][2 * k] = (self.own[i][2 * k].astype(F32) + self.ry[i][k].astype(F32)).astype(BF)

            return
        self.own[i][0] = (self.own[i][0].astype(F32) + self.ry[i][0].astype(F32)).astype(BF)

        @pl.loop(1, self.p.na)
        def _(k):
            self.add(self.own[i], 2 * k, self.mine(), self.ry[i][k, :, :, self.mine()])

    def stage2(self, i):
        if self.chunks[i][5]:
            self.add_x(i)
            self.start(i, self.y_copies(i))
        else:
            self.add_y(i)
            self.start(i, self.x_copies(i))

    def stage3(self, i):
        if self.chunks[i][5]:
            self.add_y(i)
        else:
            self.add_x(i)
        self.start(i, self.z_copies(i))

    def stage4(self, i):
        self.wait(i, self.z_copies(i))
        c = self.mine()
        t = self.own[i][0, :, :, c].astype(F32)
        for k in range(self.p.na - 1):
            t = t + self.rz[i][k].astype(F32)
        self.own[i][0, :, :, c] = t.astype(BF)
        self.start(i, self.last_copies(i))

    def stage5(self, i, put):
        self.wait(i, self.last_copies(i))
        put(i, self.own[i][0].astype(F32) + self.rf[i][...].astype(F32))

    def events(self, put):
        call, n = functools.partial, len(self.chunks)
        out = []
        for t in range(n + 4):
            for s in range(5, 0, -1):
                i = t - (s - 1)
                if 0 <= i < n:
                    out.append(call(self.stage5, i, put) if s == 5 else call(getattr(self, "stage%d" % s), i))
        return out

    def finish(self):
        for i in range(len(self.chunks)):
            for c in (self.core_copies, self.x_copies, self.y_copies, self.z_copies, self.last_copies):
                for at, src, dst, dev in c(i):
                    s, r = self.sem(i, at)
                    remote(src, src, s, r, self.p.core_dev).wait_send()


def backward_kernel(
    n, m, blocks, per, count, v_ref, aux_hbm, der_hbm, gtok_ref, ga_ref, gb_ref, w1s_ref, w2_ref, vecs_ref,
    co_hbm, gt_ref, oa_ref, ob_ref, win_ref, tot_ref,
    vbuf, aux_ref, der_ref, co_ref, gin, x_ref, w2g_ref, row_ref,
    own_a, rc_a, rx_a, ry_a, rz_a, rf_a, own_b, rc_b, rx_b, ry_b, rz_b, rf_b,
    ms, mc, mx, my, mz, md, tc, tx, ty, tz, td, te,
    vsem, asem, dsem, csem, lsem, rsend, rrecv, tsend, trecv, ssend, srecv,
):
    rows, width = v_ref.shape
    rb = rows // blocks
    me = Place(n, m)
    shard, fsh = width // n, gb_ref.shape[1] // n
    micros, _, fm, _ = gtok_ref.shape

    def copies(i):
        r = pl.ds(i * rb, rb)
        return (
            pltpu.make_async_copy(v_ref.at[r], vbuf.at[r], vsem.at[i]),
            pltpu.make_async_copy(aux_hbm.at[r], aux_ref.at[r], asem.at[i]),
            pltpu.make_async_copy(der_hbm.at[r], der_ref.at[r], dsem.at[i]),
        )

    def put(i):
        r = pl.ds(i * rb, rb)
        return pltpu.make_async_copy(co_ref.at[r], co_hbm.at[r], csem.at[i])

    me.greet()
    out = []
    for mi in range(micros):
        for k in range(1, m):
            j = lax.rem(me.map + k, m)
            d = remote(gtok_ref.at[mi, j], gin.at[mi, me.map], tsend.at[mi * m + k], trecv.at[mi * m + k], (me.clip, j))
            d.start()
            out.append(d)
        out.append(pltpu.make_async_copy(gtok_ref.at[mi, me.map], gin.at[mi, me.map], tsend.at[mi * m]))
        out[-1].start()

    chunks = [(gb_ref, pl.ds(0, 1), fsh // 2, fsh, q * (fsh // 2), q == 0) for q in range(2)]
    chunks += [(ga_ref, pl.ds(2 * q, 2), shard, shard, 0, q % 2 == 0) for q in (2, 3, 0, 1)]

    def both(b, a):
        return [b.at[0], b.at[1]] + [a.at[q] for q in range(4)]

    red = Reduce(
        me, chunks, both(own_b, own_a), both(rc_b, rc_a), both(rx_b, rx_a), both(ry_b, ry_a), both(rz_b, rz_a),
        both(rf_b, rf_a), lsem, rsend, rrecv,
    )
    for i in range(6):
        red.stage0(i)

    def put_out(i, val):
        if i < 2:
            ob_ref[i * (fsh // 2) : (i + 1) * (fsh // 2), :] = val[0]
        else:
            q = (2, 3, 0, 1)[i - 2]
            oa_ref[2 * q : 2 * q + 2] = val

    @pl.loop(0, blocks)
    def _(i):
        for c in copies(i):
            c.start()

    x_ref[...] = jnp.zeros(x_ref.shape, F32)
    w2g_ref[...] = jnp.zeros(w2g_ref.shape, F32)
    row_ref[...] = jnp.zeros(row_ref.shape, F32)
    lane = lax.broadcasted_iota(jnp.int32, (rb, LANES), 1)

    todo = red.events(put_out)
    slots = [[] for _ in range(blocks + 1)]
    for at, f in enumerate(todo[2:]):
        slots[min(int(at * RSTEP * blocks / len(todo)), blocks)].append(f)
    todo[0]()
    todo[1]()
    for mi in range(micros):
        for k in range(1, m):
            j = lax.rem(me.map + m - k, m)
            remote(gtok_ref.at[mi, j], gin.at[mi, j], tsend.at[mi * m + k], trecv.at[mi * m + k], me.core_dev).wait_recv()
    for mi in range(micros):
        for k in range(m):
            d = out[mi * m + k]
            if k < m - 1:
                d.wait_send()
            else:
                d.wait()
    gt_ref[...] = jnp.zeros(gt_ref.shape, BF)
    for mi in range(micros):
        for j in range(m):
            gt_ref[mi * m + j, 0:fm, :] = (gin[mi, j].astype(F32) * count**-0.5).astype(BF)

    @pl.loop(0, blocks)
    def _(i):
        for at, fs in enumerate(slots[:blocks]):
            if fs:

                @pl.when(i == at)
                def _():
                    for f in fs:
                        f()

        rr = pl.ds(pl.multiple_of(i * rb, 16), rb)
        for c in copies(i):
            c.wait()
        v = vbuf[rr, :]
        aux = aux_ref[rr, :]
        mean = aux[:, 64:65]
        rstd = aux[:, 127:128]
        g = dot_nt(v, gt_ref[i // per])
        gl_f = g * der_ref[rr, :].astype(F32)
        gl = gl_f.astype(BF)
        ga = dot_nt(gl, w2_ref[...])
        pre = jnp.where(lane < 64, aux, 0.0)
        act, slope = gelu_parts(pre)
        gmp = (ga * slope).astype(BF).astype(F32)
        u = (gmp * rstd).astype(BF)
        uf = u.astype(F32)
        m1 = jnp.sum(gmp * w1s_ref[0:1, :], axis=-1, keepdims=True) * (1.0 / width)
        m2 = jnp.sum(gmp * (pre - w1s_ref[1:2, :]), axis=-1, keepdims=True) * (1.0 / width)
        w2g_ref[...] += dot_tn(act.astype(BF)[:, :64], gl)
        x_ref[...] += dot_tn(u[:, :64], v)
        row_ref[0:1, :] += jnp.sum(gl_f, axis=0, keepdims=True)
        row_ref[1:2, :] += jnp.sum(gmp, axis=0, keepdims=True)
        row_ref[2:3, :] += jnp.sum(uf * mean, axis=0, keepdims=True)
        c1 = -rstd * m1
        s = -rstd * rstd * m2
        c1h, sh, mh = (t.astype(BF).astype(F32) for t in (c1, s, mean))
        ex = jnp.where(lane < 64, uf, 0.0)
        for pos, val in enumerate((c1h, c1 - c1h, sh, s - sh, mh, mean - mh)):
            ex = jnp.where(lane == 64 + pos, val, ex)
        co_ref[rr, :] = ex.astype(BF)
        put(i).start()

    shift = row_ref[...].T[0:64, 2:3]
    ms[0:64, :] = (x_ref[...] - shift).astype(BF)
    ms[64:96, :] = jnp.concatenate([vecs_ref[...], jnp.zeros((16, width), F32)], axis=0).astype(BF)
    td[0:64, :] = w2g_ref[...]
    td[64:72, :] = row_ref[...]
    td[72:80, :] = jnp.zeros((8, LANES), F32)

    def both_ways(at, dev, msrc, mdst, tsrc, tdst):
        a = remote(msrc, mdst, ssend.at[0, at], srecv.at[0, at], dev)
        b = remote(tsrc, tdst, ssend.at[1, at], srecv.at[1, at], dev)
        a.start()
        b.start()
        return a, b

    a, b = both_ways(0, me.core_dev, ms, mc, td, tc)
    for f in slots[blocks]:
        f()
    a.wait()
    b.wait()
    ms[...] = (ms[...].astype(F32) + mc[...].astype(F32)).astype(BF)
    td[...] += tc[...]
    mr = pl.ds(pl.multiple_of(me.c * 48, 16), 48)
    tr = pl.ds(pl.multiple_of(me.c * 40, 8), 40)
    for at, dev, mb, tb in ((1, me.x_dev, mx, tx), (2, me.y_dev, my, ty)):
        a, b = both_ways(at, dev, ms.at[mr], mb, td.at[tr], tb)
        a.wait()
        b.wait()
        ms[mr, :] = (ms[mr, :].astype(F32) + mb[...].astype(F32)).astype(BF)
        td[tr, :] += tb[...]

    def window(z):
        lo = jnp.minimum(z * (width // me.na) // LANES * LANES, width - 256)
        return pl.ds(pl.multiple_of(lo, LANES), 256)

    sent = []
    for k in range(1, me.na):
        z = me.back(k)
        sent += both_ways(
            2 + k, (me.shard(z, me.b, me.c), me.map), ms.at[mr, window(z)], mz.at[me.a], td.at[tr], tz.at[me.a]
        )
    mz[me.a] = ms[mr, window(me.a)]
    tz[me.a] = td[tr, :]
    for k in range(1, me.na):
        z = me.ahead(k)
        remote(mz.at[z], mz.at[z], ssend.at[0, 2 + k], srecv.at[0, 2 + k], me.core_dev).wait_recv()
        remote(tz.at[z], tz.at[z], ssend.at[1, 2 + k], srecv.at[1, 2 + k], me.core_dev).wait_recv()
    for d in sent:
        d.wait_send()
    t = mz[0].astype(F32)
    s = tz[0]
    for z in range(1, me.na):
        t = t + mz[z].astype(F32)
        s = s + tz[z]
    md[mr, :] = t
    td[tr, :] = s
    a, b = both_ways(me.na + 2, me.core_dev, md.at[mr], md.at[mr], td.at[tr], te)
    o = 1 - me.c
    mo, to = pl.ds(pl.multiple_of(o * 48, 16), 48), pl.ds(pl.multiple_of(o * 40, 8), 40)
    remote(md.at[mo], md.at[mo], ssend.at[0, me.na + 2], srecv.at[0, me.na + 2], me.core_dev).wait_recv()
    b.wait()
    a.wait_send()
    td[to, :] = te[...]
    win_ref[...] = md[...]
    tot_ref[...] = td[...]

    @pl.loop(0, blocks)
    def _(i):
        put(i).wait()

    red.finish()


RSTEP = 1.0


def backward(n, m, v, aux, der, gtok, ga, gb, w1s, w2n, vecs, blocks, per, count):
    rows, width = v.shape
    rb = rows // blocks
    na, shard, fsh = n // 4, width // n, gb.shape[1] // n
    micros, _, fm, _ = gtok.shape
    vm = pl.BlockSpec(memory_space=pltpu.VMEM)
    hb = pl.BlockSpec(memory_space=pltpu.HBM)
    sds = jax.ShapeDtypeStruct
    dma = pltpu.SemaphoreType.DMA
    half = width // 2

    def bufs(c, np, r):
        return [
            pltpu.VMEM((c, 2 * na, np, r, width), BF),
            pltpu.VMEM((c, 2 * na, np, r, width), BF),
            pltpu.VMEM((c, 2 * na - 2, np, r, half), BF),
            pltpu.VMEM((c, na, np, r, width), BF),
            pltpu.VMEM((c, na - 1, np, r, half), BF),
            pltpu.VMEM((c, np, r, width), BF),
        ]

    return pl.pallas_call(
        functools.partial(backward_kernel, n, m, blocks, per, count),
        out_shape=(
            sds((rows, LANES), BF), sds((micros * m, LANES, width), BF), sds((8, shard, width), F32),
            sds((fsh, width), F32), sds((96, 256), F32), sds((80, LANES), F32),
        ),
        in_specs=[hb] * 6 + [vm] * 3,
        out_specs=(hb,) + (vm,) * 5,
        scratch_shapes=[
            pltpu.VMEM((rows, width), BF),
            pltpu.VMEM((rows, LANES), F32),
            pltpu.VMEM((rows, LANES), BF),
            pltpu.VMEM((rows, LANES), BF),
            pltpu.VMEM(gtok.shape, BF),
            pltpu.VMEM((64, width), F32),
            pltpu.VMEM((64, LANES), F32),
            pltpu.VMEM((8, LANES), F32),
        ]
        + bufs(4, 2, shard)
        + bufs(2, 1, fsh // 2)
        + [
            pltpu.VMEM((96, width), BF),
            pltpu.VMEM((96, width), BF),
            pltpu.VMEM((48, width), BF),
            pltpu.VMEM((48, width), BF),
            pltpu.VMEM((na, 48, 256), BF),
            pltpu.VMEM((96, 256), F32),
            pltpu.VMEM((80, LANES), F32),
            pltpu.VMEM((40, LANES), F32),
            pltpu.VMEM((40, LANES), F32),
            pltpu.VMEM((na, 40, LANES), F32),
            pltpu.VMEM((80, LANES), F32),
            pltpu.VMEM((40, LANES), F32),
        ]
        + [dma((blocks,))] * 4
        + [dma((6, 2 * na)), dma((6 * 8 * na,)), dma((6 * 8 * na,)), dma((micros * m,)), dma((micros * m,))]
        + [dma((2, na + 3)), dma((2, na + 3))],
        compiler_params=pltpu.CompilerParams(vmem_limit_bytes=VLIM, collective_id=1, has_side_effects=True),
    )(v, aux, der, gtok, ga, gb, w1s, w2n, vecs)


def patch_out_kernel(v_ref, sel_ref, co_ref, gt_ref, bt_ref, o_ref):
    co = co_ref[...]
    ex = co.astype(F32)
    s = ex[:, 66:67] + ex[:, 67:68]
    mean = ex[:, 68:69] + ex[:, 69:70]
    left = jnp.concatenate([sel_ref[...], co], axis=1)
    right = jnp.concatenate([gt_ref[0], bt_ref[...]], axis=0)
    mm = dot(left, right)
    for k in range(v_ref.shape[1] // LANES):
        c = slice(k * LANES, (k + 1) * LANES)
        o_ref[:, c] = (mm[:, c] + (v_ref[:, c].astype(F32) - mean) * s).astype(BF)


def patch_out(v, sel, co, gts, bt, blocks, per):
    rows, width = v.shape
    rb = rows // blocks
    row = pl.BlockSpec((rb, width), lambda i: (i, 0))
    thin = pl.BlockSpec((rb, LANES), lambda i: (i, 0))
    return pl.pallas_call(
        patch_out_kernel,
        grid=(blocks,),
        out_shape=jax.ShapeDtypeStruct((rows, width), BF),
        in_specs=[
            row, thin, thin,
            pl.BlockSpec((1, LANES, width), lambda i: (i // per, 0, 0)),
            pl.BlockSpec((LANES, width), lambda i: (0, 0)),
        ],
        out_specs=row,
        compiler_params=pltpu.CompilerParams(vmem_limit_bytes=VLIM),
    )(v, sel, co, gts, bt)


def on_device(
    patches, keep, tl_gain, tl_bias, map_w1, map_b1, map_w2, map_b2, ln1_gain, ln1_bias, qkv_weight, qv_bias,
    out_weight, out_bias, ln2_gain, ln2_bias, fc1_weight, fc1_bias, fc2_weight, fc2_bias, cotangent,
):
    micros, group, frames, count, width = patches.shape
    groups = micros * group
    shard = tl_gain.shape[0]
    me = lax.axis_index("clip")
    per = 7
    blocks = groups * per
    pb = count // per
    rb = pb * frames
    v = jnp.transpose(patches, (0, 1, 3, 2, 4)).reshape(groups * count * frames, width)
    kx = jnp.transpose(keep, (0, 1, 3, 2)).reshape(blocks, pb, frames)
    kx = jnp.repeat(kx, MAPS, axis=2).astype(BF)
    kx = jnp.pad(kx, ((0, 0), (0, 4), (0, LANES - frames * MAPS)))
    n, m = width // shard, group
    b2rep = jnp.tile(map_b2.astype(F32), LANES // MAPS)[None]
    gains, biases, w1l = tl_gain.astype(F32)[:, None], tl_bias.astype(F32)[:, None], map_w1.astype(F32)
    q2 = map_w2.shape[0]
    par = -(-(shard + 1 + q2) // 16) * 16
    pa = jnp.concatenate([gains * w1l, biases * w1l], axis=1).astype(BF)
    b1row = lax.dynamic_update_slice(jnp.zeros((1, LANES), BF), map_b1[None], (0, me * q2))
    pa = jnp.concatenate([pa, b1row, jnp.tile(map_w2, (1, LANES // MAPS)), jnp.zeros((par - shard - 1 - q2, LANES), BF)])
    wide = width // 2
    fsh = fc1_bias.shape[0]
    vecs = jnp.stack([ln1_gain, ln1_bias, qv_bias[0], qv_bias[1], out_bias, ln2_gain, ln2_bias, fc2_bias])
    pb = lax.dynamic_update_slice(jnp.zeros((16, wide), BF), vecs, (0, (me * shard) % wide))
    pb = lax.dynamic_update_slice(pb, fc1_bias[None], (8, (me * fsh) % wide))
    wa, wb, tok, aux, sel, der, vec, fb, bt, small = forward(
        n, m, v, kx, b2rep, pa, pb, qkv_weight, out_weight, fc1_weight, fc2_weight, micros, frames, per, count
    )
    tok = tok.reshape(-1, width)
    w1s = small[0:8]
    w2n = jnp.pad(small[8:72].astype(BF), ((0, 64), (0, 0)))
    ff = wb.shape[0]
    out, ga, gb, gtok, gvec, gb1 = token_layer(tok, cotangent.reshape(tok.shape), wa, wb, vec, fb)
    vecs = jnp.concatenate([gvec, jnp.swapaxes(gb1.reshape(n, -1, shard), 0, 1).reshape(-1, width)])
    vecs = jnp.pad(vecs, ((0, 16 - vecs.shape[0]), (0, 0)))
    co, gts, oa, ob, win, tot = backward(
        n, m, v, aux, der, gtok.reshape(micros, m, -1, width), ga, gb[None], w1s, w2n, vecs, blocks, per, count
    )
    pg = patch_out(v, sel, co, gts, bt, blocks, per)
    pg = jnp.transpose(pg.reshape(micros, group, count, frames, width), (0, 1, 3, 2, 4))
    if m > 2:
        oa, ob, win, tot = (lax.psum(t, "map") * 0.5 for t in (oa, ob, win, tot))
    lo = jnp.minimum(me // 4 * (width // (n // 4)) // LANES * LANES, width - 256)
    win = lax.dynamic_slice(win, (0, me * shard - lo), (96, shard))
    xs = win[:64].T
    gvec = win[64:72]
    fgrad = win[72 : 72 + ff // width].reshape(-1)
    gb = tot[65, :64]
    b2g = jnp.sum(tot[64].reshape(LANES // MAPS, MAPS), axis=0)
    w2g = lax.dynamic_slice(tot, (me * q2, 0), (q2, LANES)).reshape(q2, LANES // MAPS, MAPS).sum(axis=1)
    return (
        out.reshape(cotangent.shape),
        pg,
        jnp.sum(w1l * xs, axis=1),
        w1l @ gb,
        gains * xs + biases * gb[None],
        lax.dynamic_slice(gb, (me * q2,), (q2,)),
        w2g,
        b2g,
        gvec[0],
        gvec[1],
        jnp.concatenate([oa[0], oa[1], oa[2]], axis=1),
        gvec[2:4],
        oa[3],
        gvec[4],
        gvec[5],
        gvec[6],
        jnp.concatenate([oa[4 + q] for q in range(ff // width)], axis=1),
        fgrad,
        ob,
        gvec[7],
    )


def solution(mesh):
    weights = (
        P("clip"), P("clip"), P("clip", None), P("clip"), P("clip", None), P(), P("clip"), P("clip"), P("clip", None),
        P(None, "clip"), P("clip", None), P("clip"), P("clip"), P("clip"), P("clip", None), P("clip"), P("clip", None),
        P("clip"),
    )
    tokens = P(None, ("clip", "map"), None, None)
    frames = P(None, "clip", "map", None, None)
    return jax.shard_map(
        on_device,
        mesh=mesh,
        in_specs=(frames, P(None, "clip", "map", None)) + weights + (tokens,),
        out_specs=(tokens, frames) + weights,
        check_vma=False,
    )
```

```python
import functools

import jax
import jax.numpy as jnp
from jax import lax
from jax.experimental import pallas as pl
from jax.experimental.pallas import tpu as pltpu
from jax.sharding import PartitionSpec as P

HEAD = 64
MAPS = 8
LANES = 128
EPS = 1e-06
GC = 0.7978845608028654
GA = 0.044715
BF = jnp.bfloat16
F32 = jnp.float32
VLIM = 61 * 1024 * 1024


def dot(a, b):
    return lax.dot_general(a, b, (((1,), (0,)), ((), ())), preferred_element_type=F32)


def dot_nt(a, b):
    return lax.dot_general(a, b, (((1,), (1,)), ((), ())), preferred_element_type=F32)


def dot_tn(a, b):
    return lax.dot_general(a, b, (((0,), (0,)), ((), ())), preferred_element_type=F32)


def gelu_parts(x):
    x2 = x * x
    t = jnp.tanh(GC * x * (1.0 + GA * x2))
    act = 0.5 * x * (1.0 + t)
    slope = 0.5 * (1.0 + t) + 0.5 * x * (1.0 - t * t) * (GC * (1.0 + 3.0 * GA * x2))
    return act, slope


def col(x, n):
    return pl.ds(pl.multiple_of(x, n), n)


MESH = pl.DeviceIdType.MESH


class Place:
    def __init__(self, n, m):
        self.n, self.m, self.na = n, m, n // 4
        self.clip, self.map = lax.axis_index("clip"), lax.axis_index("map")
        self.a, self.b, self.c = self.clip // 4, (self.clip // 2) % 2, self.clip % 2
        self.half = self.map % 2
        self.twin = self.map + 1 - 2 * self.half
        self.core_dev = (self.shard(self.a, self.b, 1 - self.c), self.map)
        self.y_dev = (self.shard(self.a, 1 - self.b, self.c), self.map)
        self.x_dev = (self.clip, self.twin)

    def shard(self, a, b, c):
        return (a * 2 + b) * 2 + c

    def back(self, k):
        return lax.rem(self.a + self.na - k, self.na)

    def ahead(self, k):
        return lax.rem(self.a + k, self.na)

    def greet(self):
        bar = pltpu.get_barrier_semaphore()
        for k in range(1, self.n):
            pl.semaphore_signal(bar, inc=1, device_id=(lax.rem(self.clip + k, self.n), self.map), device_id_type=MESH)
        for k in range(1, self.m):
            pl.semaphore_signal(bar, inc=1, device_id=(self.clip, lax.rem(self.map + k, self.m)), device_id_type=MESH)
        pl.semaphore_wait(bar, self.n + self.m - 2)


def remote(src, dst, send, recv, dev):
    return pltpu.make_async_remote_copy(
        src_ref=src, dst_ref=dst, send_sem=send, recv_sem=recv, device_id=dev, device_id_type=MESH
    )


class Gather:
    def __init__(self, place, chunks, shards, sends, recvs):
        self.p, self.chunks, self.shards, self.sends, self.recvs = place, chunks, shards, sends, recvs
        self.started = []

    def block(self, i, s, half):
        ref, panels, rows, pitch, skip, _ = self.chunks[i]
        r = pl.ds(pl.multiple_of(s * pitch + skip, 8), rows)
        c = slice(None) if half is None else pl.ds(pl.multiple_of(half * (ref.shape[-1] // 2), LANES), ref.shape[-1] // 2)
        return ref.at[r, c] if panels is None else ref.at[panels, r, c]

    def send(self, i, at, dev, s, half, src=None):
        b = self.block(i, s, half)
        j = i * self.per() + at
        remote(b if src is None else src, b, self.sends.at[j], self.recvs.at[j], dev).start()
        self.started.append((i, j, half is None))

    def wait(self, i, at, s, half):
        b = self.block(i, s, half)
        j = i * self.per() + at
        remote(b, b, self.sends.at[j], self.recvs.at[j], self.p.core_dev).wait_recv()

    def per(self):
        return 11 * self.p.na

    def at_z(self, k):
        return k - 1

    def at_y(self, k):
        return self.p.na - 1 + k

    def at_x(self, side, k):
        return (2 + side) * self.p.na + k

    def at_diag_y(self, k):
        return 4 * self.p.na + k

    def at_core(self, e):
        return 5 * self.p.na + e

    def own(self, i):
        p, src = self.p, self.shards[i]
        w = src.shape[-1] // 2
        c = pl.ds(pl.multiple_of(p.half * w, LANES), w)
        part = src.at[:, c] if len(src.shape) == 2 else src.at[:, :, c]
        for k in range(1, p.na):
            self.send(i, self.at_z(k), (p.shard(p.ahead(k), p.b, p.c), p.map), p.clip, p.half, part)
        self.send(i, self.at_y(0), p.y_dev, p.clip, None, src)
        self.send(i, self.at_core(0), p.core_dev, p.clip, None, src)

    def by_x(self, i):
        return self.chunks[i][5]

    def from_z(self, i, k):
        p = self.p
        s = p.shard(p.back(k), p.b, p.c)
        self.wait(i, self.at_z(k), s, p.half)
        self.send(i, self.at_x(0, k), p.x_dev, s, p.half)
        self.send(i, self.at_y(k), p.y_dev, s, p.half)
        self.send(i, self.at_core(k), p.core_dev, s, p.half)

    def from_y(self, i, k):
        p = self.p
        if k == 0:
            s = p.shard(p.a, 1 - p.b, p.c)
            self.wait(i, self.at_y(0), s, None)
            self.send(i, self.at_core(p.na), p.core_dev, s, None)
            return
        s = p.shard(p.back(k), 1 - p.b, p.c)
        self.wait(i, self.at_y(k), s, p.half)
        if self.by_x(i):
            self.send(i, self.at_x(1, k), p.x_dev, s, p.half)
        self.send(i, self.at_core(p.na + k), p.core_dev, s, p.half)

    def from_x(self, i, side, k):
        p = self.p
        b = p.b if side == 0 else 1 - p.b
        s = p.shard(p.back(k), b, p.c)
        by_x = self.by_x(i)
        self.wait(i, self.at_x(side, k) if by_x or side == 0 else self.at_diag_y(k), s, 1 - p.half)
        if side == 0 and not by_x:
            self.send(i, self.at_diag_y(k), p.y_dev, s, 1 - p.half)
        self.send(i, self.at_core((2 + side) * p.na + k), p.core_dev, s, 1 - p.half)

    def from_core(self, i):
        p, o = self.p, 1 - self.p.c
        self.wait(i, self.at_core(0), p.shard(p.a, p.b, o), None)
        self.wait(i, self.at_core(p.na), p.shard(p.a, 1 - p.b, o), None)
        for k in range(1, p.na):
            for side in range(2):
                s = p.shard(p.back(k), p.b if side == 0 else 1 - p.b, o)
                self.wait(i, self.at_core(p.na * side + k), s, p.half)
                self.wait(i, self.at_core((2 + side) * p.na + k), s, 1 - p.half)

    def finish(self):
        for i in range(len(self.chunks)):
            self.from_core(i)
        for i, j, full in self.started:
            b = self.block(i, self.p.clip, None if full else self.p.half)
            remote(b, b, self.sends.at[j], self.recvs.at[j], self.p.core_dev).wait_send()

    def events(self):
        n, ks = len(self.chunks), range(1, self.p.na)
        call = functools.partial
        out = [call(self.own, i) for i in range(AHEAD)]
        for i in range(n + 2):
            if i < n:
                for k in ks:
                    out.append(call(self.from_z, i, k))
                    if k == self.p.na - 2 and i + AHEAD < n:
                        out.append(call(self.own, i + AHEAD))
                out.append(call(self.from_y, i, 0))
            if 0 <= i - 1 < n:
                out += [call(self.from_y, i - 1, k) for k in ks]
                out += [call(self.from_x, i - 1, 0, k) for k in ks]
            if 0 <= i - 2 < n:
                out += [call(self.from_x, i - 2, 1, k) for k in ks]
        return out


def forward_kernel(
    n, m, blocks, per, count, v_ref, kx_ref, b2_ref, pa_ref, pb_ref, wq_ref, wo_ref, w1_ref,
    wa_ref, tok_ref, aux_ref, sel_ref, der_ref, vec_ref, fb_ref, wt_ref, small_ref,
    vbuf, acc, pool, rmat, delta, pag, pbg, w1v, w2v, ss, ws_ref, vsem, lsem, gsend, grecv, psend, precv, tsend, trecv,
):
    rows, width = v_ref.shape
    rb = rows // blocks
    frames = rb // (kx_ref.shape[1] - 4)
    fm = tok_ref.shape[2]
    me = Place(n, m)
    shard = width // n
    ff = w1_ref.shape[1]
    fsh = ff // n

    micros = tok_ref.shape[0]

    def load(blk, i):
        r = pl.ds(blk * rb, rb)
        return pltpu.make_async_copy(v_ref.at[r], vbuf.at[r], vsem.at[i])

    def token_copy(gi, mi, j, back=False):
        dst = tok_ref.at[mi, j] if back else tok_ref.at[mi, me.map]
        return remote(pool.at[mi * m + j, pl.ds(0, fm)], dst, tsend.at[gi], trecv.at[gi], (me.clip, j))

    @pl.loop(0, blocks)
    def _(i):
        gi = i // per
        load(((gi % micros) * m + lax.rem(me.map + 1 + gi // micros, m)) * per + i % per, i).start()

    own = pl.ds(pl.multiple_of(me.clip * shard, 8), shard)
    for q in range(3):
        ws_ref[q] = wq_ref[:, q * width : (q + 1) * width]
    ws_ref[3] = wo_ref[...]
    for q in range(ff // width):
        ws_ref[4 + q] = w1_ref[:, q * width : (q + 1) * width]
    local = [(ws_ref, wa_ref.at[:, own])]
    local.append((pa_ref, pag.at[me.clip]))
    local.append((pb_ref, pbg.at[me.clip]))
    local = [pltpu.make_async_copy(s, d, lsem.at[i]) for i, (s, d) in enumerate(local)]
    for d in local:
        d.start()
    me.greet()
    small = []
    for k in range(1, n):
        dev = (lax.rem(me.clip + k, n), me.map)
        small.append(remote(pa_ref, pag.at[me.clip], psend.at[0, k], precv.at[0, k], dev))
        small[-1].start()
    for d in local[1:]:
        d.wait()
    chunks = [(wa_ref, pl.ds(2 * q, 2), shard, shard, 0, q != 2) for q in range(4)]
    shards = [ws_ref.at[pl.ds(2 * q, 2)] for q in range(4)]
    g = Gather(me, chunks, shards, gsend, grecv)
    todo = g.events()
    slots = [[] for _ in range(blocks + 1)]
    for at, f in enumerate(todo[AHEAD:]):
        slots[min(int(at * STEP * blocks / len(todo)), blocks)].append(f)
    for f in todo[:AHEAD]:
        f()
    for k in range(1, n):
        dev = (lax.rem(me.clip + k, n), me.map)
        small.append(remote(pb_ref, pbg.at[me.clip], psend.at[1, k], precv.at[1, k], dev))
        small[-1].start()

    r2 = lax.broadcasted_iota(jnp.int32, rmat.shape, 0)
    c2 = lax.broadcasted_iota(jnp.int32, rmat.shape, 1)
    rmat[...] = jnp.where(r2 // frames == c2, 1.0, 0.0).astype(BF)
    r1 = lax.broadcasted_iota(jnp.int32, delta.shape, 0)
    c1 = lax.broadcasted_iota(jnp.int32, delta.shape, 1)
    delta[...] = jnp.where(r1 % frames == c1 // MAPS, 1.0, 0.0)

    for k in range(1, n):
        s = lax.rem(me.clip + n - k, n)
        remote(pa_ref, pag.at[s], psend.at[0, k], precv.at[0, k], me.core_dev).wait_recv()
    par = pa_ref.shape[0]
    flat = pag[...].reshape(n * par, LANES)
    q2 = 64 // n

    def pick(lo, count_rows, want_s, want_j):
        r = lax.broadcasted_iota(jnp.int32, (count_rows, 1), 0) + lo
        kk = lax.broadcasted_iota(jnp.int32, (1, n * par), 1)
        s, j = kk // par, kk % par
        sel = jnp.logical_and(s == want_s(r), j == want_j(r))
        return dot(jnp.where(sel, 1.0, 0.0).astype(BF), flat)

    lane = lax.broadcasted_iota(jnp.int32, (1, LANES), 1)
    for q in range(width // 128):
        got = pick(q * 128, 128, lambda r: r // shard, lambda r: r % shard)
        got = jnp.where(lane < 64, got, jnp.where(lane == 64, 1.0, 0.0))
        w1v[q * 128 : (q + 1) * 128, :] = got.astype(BF)
        wt_ref[0:64, q * 128 : (q + 1) * 128] = got.T[0:64, :].astype(BF)
    tail = lax.broadcasted_iota(jnp.int32, (64, width), 0)
    wt_ref[64:128, :] = jnp.where(tail < 2, 1.0, 0.0).astype(BF)
    got = pick(0, 64, lambda r: r // q2, lambda r: shard + 1 + r % q2)
    w2v[...] = got.astype(BF)
    small_ref[...] = jnp.zeros(small_ref.shape, F32)
    small_ref[8:72, :] = got
    r = lax.broadcasted_iota(jnp.int32, (8, 1), 0)
    kk = lax.broadcasted_iota(jnp.int32, (1, n * par), 1) % par
    sums = dot(jnp.where(jnp.logical_or(jnp.logical_and(r == 0, kk < shard), jnp.logical_and(r == 1, kk == shard)), 1.0, 0.0).astype(BF), flat)
    csum = jnp.where(lane < 64, sums[0:1, :], 0.0)
    cadd = jnp.where(lane < 64, pltpu.roll(sums, 64, 1)[0:1, :] + sums[1:2, :], 0.0)
    ss[0:1, :] = csum
    ss[1:2, :] = cadd
    small_ref[0:1, :] = csum
    small_ref[1:2, :] = cadd

    @pl.loop(0, blocks)
    def _(i):
        for at, fs in enumerate(slots[:blocks]):
            if fs:

                @pl.when(i == at)
                def _():
                    for f in fs:
                        f()

        gi = i // per
        j = lax.rem(me.map + 1 + gi // micros, m)
        gr = (gi % micros) * m + j
        blk = gr * per + i % per
        rr = pl.ds(pl.multiple_of(blk * rb, 16), rb)
        load(blk, i).wait()
        v = vbuf[rr, :]
        mm = dot(v, w1v[...])
        mean = mm[:, 64:65] * (1.0 / width)
        sq = jnp.zeros((rb, LANES), F32)
        for k in range(width // LANES):
            c = v[:, k * LANES : (k + 1) * LANES].astype(F32) - mean
            sq = sq + c * c
        rstd = lax.rsqrt(jnp.sum(sq, axis=-1, keepdims=True) * (1.0 / width) + EPS)
        pre = rstd * (mm - mean * ss[0:1, :]) + ss[1:2, :]
        act, _ = gelu_parts(pre)
        logit = dot(act.astype(BF)[:, :64], w2v[...]) + b2_ref[...]
        sig = 1.0 / (1.0 + jnp.exp(-logit))
        mask = dot(rmat[...], kx_ref[blk]) * delta[...]
        sm = sig * mask
        sel = sm.astype(BF)
        sel_ref[rr, :] = sel
        der_ref[rr, :] = (sm * (1.0 - sig)).astype(BF)
        ln = lax.broadcasted_iota(jnp.int32, (rb, LANES), 1)
        aux_ref[rr, :] = jnp.where(ln < 64, pre, jnp.where(ln < 96, mean, rstd))
        part = dot_tn(sel, v)

        @pl.when(i % per == 0)
        def _():
            acc[...] = part

        @pl.when(i % per != 0)
        def _():
            acc[...] += part

        @pl.when(i % per == per - 1)
        def _():
            pool[gr] = (acc[...] * (count**-0.5)).astype(BF)

            @pl.when(gi < micros * (m - 1))
            def _():
                token_copy(gi, gi % micros, j).start()

    for mi in range(micros):
        mine = pltpu.make_async_copy(pool.at[mi * m + me.map, pl.ds(0, fm)], tok_ref.at[mi, me.map], lsem.at[8 + mi])
        mine.start()
        mine.wait()
    for f in slots[blocks]:
        f()
    for k in range(1, n):
        s = lax.rem(me.clip + n - k, n)
        remote(pb_ref, pbg.at[s], psend.at[1, k], precv.at[1, k], me.core_dev).wait_recv()
    wide = pb_ref.shape[1]
    each = wide // shard
    for q in range(width // wide):
        t = pbg[q * each].astype(F32)
        for s in range(q * each + 1, (q + 1) * each):
            t = t + pbg[s].astype(F32)
        vec_ref[:, q * wide : (q + 1) * wide] = t[0:8, :]
    each = wide // fsh
    for q in range(ff // wide):
        t = pbg[q * each].astype(F32)
        for s in range(q * each + 1, (q + 1) * each):
            t = t + pbg[s].astype(F32)
        fb_ref[:, q * wide : (q + 1) * wide] = t[8:9, :]
    for gi in range(micros * (m - 1)):
        token_copy(gi, gi % micros, lax.rem(me.map + 1 + gi // micros, m)).wait_send()
        k = 1 + gi // micros
        token_copy(gi, gi % micros, lax.rem(me.map + m - k, m), True).wait_recv()
    g.finish()
    for d in small:
        d.wait_send()
    local[0].wait()


STEP = 1.0
AHEAD = 3


def forward(n, m, v, kx, b2rep, pa, pb, wq, wo, w1, micros, frames, per, count):
    rows, width = v.shape
    blocks = kx.shape[0]
    rb = rows // blocks
    ff = w1.shape[1]
    groups = blocks // per
    copies = 6 * 11 * (n // 4)
    sds = jax.ShapeDtypeStruct
    vm = pl.BlockSpec(memory_space=pltpu.VMEM)
    hb = pl.BlockSpec(memory_space=pltpu.HBM)
    dma = pltpu.SemaphoreType.DMA
    return pl.pallas_call(
        functools.partial(forward_kernel, n, m, blocks, per, count),
        out_shape=(
            sds((8, width, width), BF),
            sds((micros, m, frames * MAPS, width), BF),
            sds((rows, LANES), F32),
            sds((rows, LANES), BF),
            sds((rows, LANES), BF),
            sds((8, width), F32),
            sds((1, ff), F32),
            sds((LANES, width), BF),
            sds((72, LANES), F32),
        ),
        in_specs=[hb] + [vm] * 7,
        out_specs=(hb, hb) + (vm,) * 7,
        scratch_shapes=[
            pltpu.VMEM((rows, width), BF),
            pltpu.VMEM((LANES, width), F32),
            pltpu.VMEM((groups, LANES, width), BF),
            pltpu.VMEM((rb, kx.shape[1]), BF),
            pltpu.VMEM((rb, LANES), F32),
            pltpu.VMEM((n,) + pa.shape, BF),
            pltpu.VMEM((n,) + pb.shape, BF),
            pltpu.VMEM((width, LANES), BF),
            pltpu.VMEM((64, LANES), BF),
            pltpu.VMEM((8, LANES), F32),
            pltpu.VMEM((8, width // n, width), BF),
            dma((blocks,)), dma((16,)), dma((copies,)), dma((copies,)), dma((2, n)), dma((2, n)),
            dma((micros * m,)), dma((micros * m,)),
        ],
        compiler_params=pltpu.CompilerParams(vmem_limit_bytes=VLIM, collective_id=0, has_side_effects=True),
    )(v, kx, b2rep, pa, pb, wq, wo, w1)


def ln_stats(t):
    mean = jnp.mean(t, axis=-1, keepdims=True)
    c = t - mean
    rstd = lax.rsqrt(jnp.mean(c * c, axis=-1, keepdims=True) + EPS)
    return c * rstd, rstd


def token_kernel(
    places, m, tok, cot, wa_hbm, w2s, vec, b1,
    out_ref, ga_hbm, gtok_ref, gvec_ref, gb1_ref, ob_ref,
    n1, joined, probs, att, mixed, n2, act, slope, gacc, gbr, tr, wa, w2, ga_ref, g2_ref,
    own_b, rc_b, rx_b, ry_b, rz_b, rf_b, wsem, osem, lsem, gsend, grecv, rsend, rrecv,
):
    n, d = tok.shape
    ff = g2_ref.shape[1]
    fsh = ff // places
    per = d // 256
    seq = 256
    micros = n // seq
    pairs = d // LANES
    ch = 64
    cb = 256
    chunks = n // ch
    lane = lax.broadcasted_iota(jnp.int32, (1, LANES), 1)
    first = lane < HEAD
    me = Place(places, m)

    def panel(q):
        return pltpu.make_async_copy(wa_hbm.at[q], wa.at[q], wsem.at[q])

    def panel_out(q):
        return pltpu.make_async_copy(ga_ref.at[q], ga_hbm.at[q], osem.at[q])

    for q in range(8):
        panel(q).start()
    own = pltpu.make_async_copy(w2s, w2.at[pl.ds(pl.multiple_of(me.clip * fsh, 8), fsh)], wsem.at[8])
    own.start()
    me.greet()
    g = Gather(
        me,
        [(w2, None, fsh // 2, fsh, q * (fsh // 2), q == 0) for q in range(2)],
        [w2s.at[pl.ds(q * (fsh // 2), fsh // 2)] for q in range(2)],
        gsend,
        grecv,
    )
    g.own(0)
    g.own(1)
    todo = [f for f in g.events() if f.func.__name__ != "own"]
    early = [[] for _ in range(9 + micros * pairs + ff // cb)]
    for at, f in enumerate(todo):
        early[at * len(early) // len(todo)].append(f)

    red = Reduce(
        me, [(g2_ref, pl.ds(0, 1), fsh // 2, fsh, q * (fsh // 2), q == 0) for q in range(2)],
        *([t.at[0], t.at[1]] for t in (own_b, rc_b, rx_b, ry_b, rz_b, rf_b)), lsem, rsend, rrecv,
    )

    def put_out(i, val):
        ob_ref[i * (fsh // 2) : (i + 1) * (fsh // 2), :] = val[0]

    steps = red.events(put_out)

    def at_step(i, slots):
        for at, fs in enumerate(slots):
            if fs:

                @pl.when(i == at)
                def _():
                    for f in fs:
                        f()

    def rows_of(i):
        return pl.ds(pl.multiple_of(i * ch, ch), ch)

    def transpose_into(src):
        @pl.loop(0, n // 128)
        def _(i):
            r = pl.ds(pl.multiple_of(i * 128, 128), 128)
            tr[:, r] = src[r, :].astype(F32).T.astype(BF)

    gvec_ref[...] = jnp.zeros(gvec_ref.shape, F32)

    def add_row(i, val):
        gvec_ref[i : i + 1, :] += jnp.sum(val, axis=0, keepdims=True)

    @pl.loop(0, chunks)
    def _(i):
        xh, _ = ln_stats(tok[rows_of(i), :].astype(F32))
        n1[rows_of(i), :] = (xh * vec[0:1, :] + vec[1:2, :]).astype(BF)

    for blk in range(3):
        panel(blk).wait()

        @pl.loop(0, d // cb)
        def _(j):
            at_step(j, early[3 * blk : 3 * blk + 3])
            o = pl.multiple_of(blk * d + j * cb, cb)
            r = dot(n1[...], wa[blk, :, col(j * cb, cb)])
            if blk == 0:
                r = r + vec[2:3, col(j * cb, cb)]
            if blk == 2:
                r = r + vec[3:4, col(j * cb, cb)]
            joined[:, pl.ds(o, cb)] = r.astype(BF)

    def heads_of(ref, i, base):
        m, pr = i // pairs, i % pairs
        r = pl.ds(pl.multiple_of(m * seq, seq), seq)
        return ref[r, pl.ds(pl.multiple_of(base + pr * LANES, LANES), LANES)]

    def put_heads(ref, i, base, val):
        m, pr = i // pairs, i % pairs
        r = pl.ds(pl.multiple_of(m * seq, seq), seq)
        ref[r, pl.ds(pl.multiple_of(base + pr * LANES, LANES), LANES)] = val

    zero = jnp.zeros((seq, LANES), BF)

    @pl.loop(0, micros * pairs)
    def _(i):
        at_step(i, early[9 : 9 + micros * pairs])
        q = (heads_of(joined, i, 0).astype(F32) * (HEAD**-0.5)).astype(BF)
        k = heads_of(joined, i, d)
        v = heads_of(joined, i, 2 * d)
        total = jnp.zeros((seq, LANES), F32)
        for e in range(2):
            mine = first if e == 0 else jnp.logical_not(first)
            s = dot_nt(jnp.where(mine, q, zero), k)
            ex = jnp.exp(s - jnp.max(s, axis=-1, keepdims=True))
            p = ex / jnp.sum(ex, axis=-1, keepdims=True)
            low = p.astype(BF)
            probs[i * 2 + e] = low
            total = total + dot(low, jnp.where(mine, v, zero))
        put_heads(att, i, 0, total.astype(BF))

    for q in range(3, 8):
        panel(q).wait()

    @pl.loop(0, d // cb)
    def _(j):
        c = col(j * cb, cb)
        mixed[:, c] = tok[:, c].astype(F32) + (dot(att[...], wa[3, :, c]) + vec[4:5, c])

    @pl.loop(0, chunks)
    def _(i):
        xh, _ = ln_stats(mixed[rows_of(i), :])
        n2[rows_of(i), :] = (xh * vec[5:6, :] + vec[6:7, :]).astype(BF)

    @pl.loop(0, ff // cb)
    def _(j):
        at_step(j, early[9 + micros * pairs :])
        c = col(j * cb, cb)
        a, s = gelu_parts(dot(n2[...], wa[4 + j // per, :, col((j % per) * cb, cb)]) + b1[0:1, c])
        act[:, c] = a.astype(BF)
        slope[:, c] = s.astype(BF)

    @pl.loop(0, ff // cb)
    def _(j):
        c = col(j * cb, cb)
        g2_ref[0, c, :] = dot_tn(act[:, c], cot[...]).astype(BF)

    red.stage0(0)
    red.stage0(1)
    g.finish()
    own.wait()

    @pl.loop(0, d // cb)
    def _(j):
        c = col(j * cb, cb)
        out_ref[:, c] = (mixed[:, c] + (dot(act[...], w2[:, c]) + vec[7:8, c])).astype(BF)

    transpose_into(n2)
    for f in steps[:2]:
        f()

    @pl.loop(0, ff // cb)
    def _(j):
        c = col(j * cb, cb)
        g = (dot_nt(cot[...], w2[c, :]) * slope[:, c].astype(F32)).astype(BF)
        act[:, c] = g
        gb1_ref[0:1, c] = jnp.sum(g.astype(F32), axis=0, keepdims=True)
        ga_ref[4 + j // per, :, col((j % per) * cb, cb)] = dot(tr[...], g).astype(BF)

    for q in range(4, 8):
        panel_out(q).start()

    @pl.loop(0, d // cb)
    def _(j):
        c = col(j * cb, cb)
        total = jnp.zeros((n, cb), F32)
        for q in range(ff // d):
            total = total + dot_nt(act[:, q * d : (q + 1) * d], wa[4 + q, c, :])
        gacc[:, c] = total

    for f in steps[2:4]:
        f()

    @pl.loop(0, chunks)
    def _(i):
        r = rows_of(i)
        xh, rstd = ln_stats(mixed[r, :])
        e = gacc[r, :]
        add_row(5, e * xh)
        add_row(6, e)
        eg = e * vec[5:6, :]
        back = eg - jnp.mean(eg, axis=-1, keepdims=True) - xh * jnp.mean(eg * xh, axis=-1, keepdims=True)
        c = cot[r, :].astype(F32)
        g = c + back * rstd
        mixed[r, :] = g
        low = g.astype(BF)
        gbr[r, :] = low
        add_row(4, low.astype(F32))
        add_row(7, c)

    transpose_into(att)

    @pl.loop(0, d // cb)
    def _(j):
        c = col(j * cb, cb)
        ga_ref[3, :, c] = dot(tr[...], gbr[:, c]).astype(BF)
        att[:, c] = dot_nt(gbr[...], wa[3, c, :]).astype(BF)

    panel_out(3).start()
    late = [[] for _ in range(micros * pairs)]
    late[len(late) // 4] = steps[4:6]

    @pl.loop(0, micros * pairs)
    def _(i):
        at_step(i, late)
        q = (heads_of(joined, i, 0).astype(F32) * (HEAD**-0.5)).astype(BF)
        k = heads_of(joined, i, d)
        v = heads_of(joined, i, 2 * d)
        ga = heads_of(att, i, 0)
        gq = jnp.zeros((seq, LANES), F32)
        gk = jnp.zeros((seq, LANES), F32)
        gv = jnp.zeros((seq, LANES), F32)
        for e in range(2):
            mine = first if e == 0 else jnp.logical_not(first)
            low = probs[i * 2 + e]
            p = low.astype(F32)
            ga_e = jnp.where(mine, ga, zero)
            gp = dot_nt(ga_e, v)
            pg = p * gp
            gs = (pg - p * jnp.sum(pg, axis=-1, keepdims=True)).astype(BF)
            gv = gv + dot_tn(low, ga_e)
            gq = gq + dot(gs, jnp.where(mine, k, zero))
            gk = gk + dot_tn(gs, jnp.where(mine, q, zero))
        put_heads(joined, i, 0, (gq * (HEAD**-0.5)).astype(BF))
        put_heads(joined, i, d, gk.astype(BF))
        put_heads(joined, i, 2 * d, gv.astype(BF))

    transpose_into(n1)
    for f in steps[6:8]:
        f()

    @pl.loop(0, 3 * d // cb)
    def _(j):
        c = col(j * cb, cb)
        ga_ref[j // per, :, col((j % per) * cb, cb)] = dot(tr[...], joined[:, c]).astype(BF)

    for q in range(3):
        panel_out(q).start()

    @pl.loop(0, d // cb)
    def _(j):
        c = col(j * cb, cb)
        total = jnp.zeros((n, cb), F32)
        for q in range(3):
            total = total + dot_nt(joined[:, q * d : (q + 1) * d], wa[q, c, :])
        gacc[:, c] = total

    @pl.loop(0, chunks)
    def _(i):
        r = rows_of(i)
        xh, rstd = ln_stats(tok[r, :].astype(F32))
        e = gacc[r, :]
        add_row(0, e * xh)
        add_row(1, e)
        add_row(2, joined[r, 0:d].astype(F32))
        add_row(3, joined[r, 2 * d : 3 * d].astype(F32))
        eg = e * vec[0:1, :]
        back = eg - jnp.mean(eg, axis=-1, keepdims=True) - xh * jnp.mean(eg * xh, axis=-1, keepdims=True)
        gtok_ref[r, :] = (mixed[r, :] + back * rstd).astype(BF)

    for f in steps[8:]:
        f()
    for q in range(8):
        panel_out(q).wait()
    red.finish()


def token_layer(places, m, tok, cot, wa, w2s, vec, b1):
    n, d = tok.shape
    fsh = w2s.shape[0]
    ff = places * fsh
    vm = pl.BlockSpec(memory_space=pltpu.VMEM)
    hb = pl.BlockSpec(memory_space=pltpu.HBM)
    sds = jax.ShapeDtypeStruct
    heads = (n // 256) * (d // HEAD)
    na = places // 4
    dma = pltpu.SemaphoreType.DMA
    return pl.pallas_call(
        functools.partial(token_kernel, places, m),
        out_shape=(
            sds((n, d), BF), sds(wa.shape, BF), sds((n, d), BF), sds((8, d), F32), sds((1, ff), F32), sds((fsh, d), F32),
        ),
        in_specs=[vm, vm, hb, vm, vm, vm],
        out_specs=(vm, hb, vm, vm, vm, vm),
        scratch_shapes=[
            pltpu.VMEM((n, d), BF),
            pltpu.VMEM((n, 3 * d), BF),
            pltpu.VMEM((heads, 256, 256), BF),
            pltpu.VMEM((n, d), BF),
            pltpu.VMEM((n, d), F32),
            pltpu.VMEM((n, d), BF),
            pltpu.VMEM((n, ff), BF),
            pltpu.VMEM((n, ff), BF),
            pltpu.VMEM((n, d), F32),
            pltpu.VMEM((n, d), BF),
            pltpu.VMEM((d, n), BF),
            pltpu.VMEM(wa.shape, BF),
            pltpu.VMEM((ff, d), BF),
            pltpu.VMEM(wa.shape, BF),
            pltpu.VMEM((1, ff, d), BF),
        ]
        + reduce_buffers(na, 2, 1, fsh // 2, d)
        + [dma((9,)), dma((8,)), dma((2, 2 * na)), dma((22 * na,)), dma((22 * na,)), dma((16 * na,)), dma((16 * na,))],
        compiler_params=pltpu.CompilerParams(vmem_limit_bytes=VLIM, collective_id=2, has_side_effects=True),
    )(tok, cot, wa, w2s, vec, b1)


def reduce_buffers(na, chunks, panels, rows, width):
    return [
        pltpu.VMEM((chunks, 2 * na, panels, rows, width), BF),
        pltpu.VMEM((chunks, 2 * na, panels, rows, width), BF),
        pltpu.VMEM((chunks, 2 * na - 2, panels, rows, width // 2), BF),
        pltpu.VMEM((chunks, na, panels, rows, width), BF),
        pltpu.VMEM((chunks, na - 1, panels, rows, width // 2), BF),
        pltpu.VMEM((chunks, panels, rows, width), BF),
    ]


class Reduce:
    def __init__(self, place, chunks, own, rc, rx, ry, rz, rf, lsem, sends, recvs):
        self.p, self.chunks, self.own, self.rc, self.rx, self.ry, self.rz, self.rf = place, chunks, own, rc, rx, ry, rz, rf
        self.lsem, self.sends, self.recvs = lsem, sends, recvs

    def sem(self, i, at):
        j = i * 8 * self.p.na + at
        return self.sends.at[j], self.recvs.at[j]

    def send(self, i, at, src, dst, dev):
        s, r = self.sem(i, at)
        remote(src, dst, s, r, dev).start()

    def grad(self, i, k, side, core):
        p = self.p
        ref, panels, rows, pitch, skip, _ = self.chunks[i]
        s = p.shard(p.back(k), p.b if side == 0 else 1 - p.b, core)
        return ref.at[panels, pl.ds(pl.multiple_of(s * pitch + skip, 8), rows)]

    def cols(self, half):
        w = self.chunks[0][0].shape[-1] // 2
        return pl.ds(pl.multiple_of(half * w, LANES), w)

    def mine(self):
        return self.cols(self.p.half)

    def other(self):
        return self.cols(1 - self.p.half)

    def core_copies(self, i):
        p = self.p
        return [
            (2 * k + side, self.grad(i, k, side, 1 - p.c), self.rc[i].at[2 * k + side], p.core_dev)
            for k in range(p.na) for side in range(2)
        ]

    def local_copies(self, i):
        p = self.p
        return [
            pltpu.make_async_copy(self.grad(i, k, side, p.c), self.own[i].at[2 * k + side], self.lsem.at[i, 2 * k + side])
            for k in range(p.na) for side in range(2)
        ]

    def x_copies(self, i):
        p, base = self.p, 2 * self.p.na
        sides = range(2) if self.chunks[i][5] else range(1)
        return [
            (base + 2 * k + side, self.own[i].at[2 * k + side, :, :, self.other()], self.rx[i].at[2 * (k - 1) + side], p.x_dev)
            for k in range(1, p.na) for side in sides
        ]

    def y_copies(self, i):
        p, base = self.p, 4 * self.p.na
        out = []
        for k in range(p.na):
            src, dst = self.own[i].at[2 * k + 1], self.ry[i].at[k]
            if self.chunks[i][5] and k:
                src, dst = src.at[:, :, self.mine()], dst.at[:, :, self.mine()]
            out.append((base + k, src, dst, p.y_dev))
        return out

    def z_copies(self, i):
        p, base = self.p, 5 * self.p.na
        return [
            (base + k, self.own[i].at[2 * k, :, :, self.mine()], self.rz[i].at[k - 1], (p.shard(p.back(k), p.b, p.c), p.map))
            for k in range(1, p.na)
        ]

    def last_copies(self, i):
        return [(6 * self.p.na, self.own[i].at[0], self.rf[i], self.p.x_dev)]

    def start(self, i, copies):
        for at, src, dst, dev in copies:
            self.send(i, at, src, dst, dev)

    def wait(self, i, copies):
        for at, src, dst, dev in copies:
            s, r = self.sem(i, at)
            remote(dst, dst, s, r, self.p.core_dev).wait_recv()

    def add(self, ref, at, cols, inc):
        a = ref[at, :, :, cols]
        ref[at, :, :, cols] = (a.astype(F32) + inc.astype(F32)).astype(BF)

    def stage0(self, i):
        for c in self.local_copies(i):
            c.start()
        self.start(i, self.core_copies(i))

    def stage1(self, i):
        for c in self.local_copies(i):
            c.wait()
        self.wait(i, self.core_copies(i))

        @pl.loop(0, 2 * self.p.na)
        def _(j):
            self.own[i][j] = (self.own[i][j].astype(F32) + self.rc[i][j].astype(F32)).astype(BF)

        self.start(i, self.x_copies(i) if self.chunks[i][5] else self.y_copies(i))

    def add_x(self, i):
        self.wait(i, self.x_copies(i))
        both = self.chunks[i][5]

        @pl.loop(0, self.p.na - 1)
        def _(k):
            for side in range(2 if both else 1):
                self.add(self.own[i], 2 * k + 2 + side, self.mine(), self.rx[i][2 * k + side])

    def add_y(self, i):
        self.wait(i, self.y_copies(i))
        if not self.chunks[i][5]:

            @pl.loop(0, self.p.na)
            def _(k):
                self.own[i][2 * k] = (self.own[i][2 * k].astype(F32) + self.ry[i][k].astype(F32)).astype(BF)

            return
        self.own[i][0] = (self.own[i][0].astype(F32) + self.ry[i][0].astype(F32)).astype(BF)

        @pl.loop(1, self.p.na)
        def _(k):
            self.add(self.own[i], 2 * k, self.mine(), self.ry[i][k, :, :, self.mine()])

    def stage2(self, i):
        if self.chunks[i][5]:
            self.add_x(i)
            self.start(i, self.y_copies(i))
        else:
            self.add_y(i)
            self.start(i, self.x_copies(i))

    def stage3(self, i):
        if self.chunks[i][5]:
            self.add_y(i)
        else:
            self.add_x(i)
        self.start(i, self.z_copies(i))

    def stage4(self, i):
        self.wait(i, self.z_copies(i))
        c = self.mine()
        t = self.own[i][0, :, :, c].astype(F32)
        for k in range(self.p.na - 1):
            t = t + self.rz[i][k].astype(F32)
        self.own[i][0, :, :, c] = t.astype(BF)
        self.start(i, self.last_copies(i))

    def stage5(self, i, put):
        self.wait(i, self.last_copies(i))
        put(i, self.own[i][0].astype(F32) + self.rf[i][...].astype(F32))

    def events(self, put):
        call, n = functools.partial, len(self.chunks)
        out = []
        for t in range(n // 2 + 4):
            for s in range(5, 0, -1):
                for i in (2 * (t - s + 1), 2 * (t - s + 1) + 1):
                    if 0 <= i < n:
                        out.append(call(self.stage5, i, put) if s == 5 else call(getattr(self, "stage%d" % s), i))
        return out

    def finish(self):
        for i in range(len(self.chunks)):
            for c in (self.core_copies, self.x_copies, self.y_copies, self.z_copies, self.last_copies):
                for at, src, dst, dev in c(i):
                    s, r = self.sem(i, at)
                    remote(src, src, s, r, self.p.core_dev).wait_send()


def backward_kernel(
    n, m, blocks, per, count, v_ref, aux_hbm, der_hbm, gtok_ref, ga_ref, w1s_ref, w2_ref, vecs_ref,
    co_hbm, gt_ref, oa_ref, win_ref, tot_ref,
    vbuf, aux_ref, der_ref, co_ref, gin, x_ref, w2g_ref, row_ref,
    own_a, rc_a, rx_a, ry_a, rz_a, rf_a,
    ms, mc, mx, my, mz, md, tc, tx, ty, tz, td, te,
    vsem, asem, dsem, csem, lsem, rsend, rrecv, tsend, trecv, ssend, srecv,
):
    rows, width = v_ref.shape
    rb = rows // blocks
    me = Place(n, m)
    shard = width // n
    micros, _, fm, _ = gtok_ref.shape

    def copies(i):
        r = pl.ds(i * rb, rb)
        return (
            pltpu.make_async_copy(v_ref.at[r], vbuf.at[r], vsem.at[i]),
            pltpu.make_async_copy(aux_hbm.at[r], aux_ref.at[r], asem.at[i]),
            pltpu.make_async_copy(der_hbm.at[r], der_ref.at[r], dsem.at[i]),
        )

    def put(i):
        r = pl.ds(i * rb, rb)
        return pltpu.make_async_copy(co_ref.at[r], co_hbm.at[r], csem.at[i])

    me.greet()
    out = []
    for mi in range(micros):
        for k in range(1, m):
            j = lax.rem(me.map + k, m)
            d = remote(gtok_ref.at[mi, j], gin.at[mi, me.map], tsend.at[mi * m + k], trecv.at[mi * m + k], (me.clip, j))
            d.start()
            out.append(d)
        out.append(pltpu.make_async_copy(gtok_ref.at[mi, me.map], gin.at[mi, me.map], tsend.at[mi * m]))
        out[-1].start()

    order = (2, 3, 0, 1)
    chunks = [(ga_ref, pl.ds(2 * q, 2), shard, shard, 0, q % 2 == 0) for q in order]
    red = Reduce(
        me, chunks, *([t.at[q] for q in range(4)] for t in (own_a, rc_a, rx_a, ry_a, rz_a, rf_a)), lsem, rsend, rrecv
    )
    for i in range(4):
        red.stage0(i)

    def put_out(i, val):
        oa_ref[2 * order[i] : 2 * order[i] + 2] = val

    @pl.loop(0, blocks)
    def _(i):
        for c in copies(i):
            c.start()

    x_ref[...] = jnp.zeros(x_ref.shape, F32)
    w2g_ref[...] = jnp.zeros(w2g_ref.shape, F32)
    row_ref[...] = jnp.zeros(row_ref.shape, F32)
    lane = lax.broadcasted_iota(jnp.int32, (rb, LANES), 1)

    todo = red.events(put_out)
    slots = [[] for _ in range(blocks + 1)]
    for at, f in enumerate(todo[2:]):
        slots[min(int(at * RSTEP * blocks / len(todo)), blocks)].append(f)
    todo[0]()
    todo[1]()
    for mi in range(micros):
        for k in range(1, m):
            j = lax.rem(me.map + m - k, m)
            remote(gtok_ref.at[mi, j], gin.at[mi, j], tsend.at[mi * m + k], trecv.at[mi * m + k], me.core_dev).wait_recv()
    for mi in range(micros):
        for k in range(m):
            d = out[mi * m + k]
            if k < m - 1:
                d.wait_send()
            else:
                d.wait()
    gt_ref[...] = jnp.zeros(gt_ref.shape, BF)
    for mi in range(micros):
        for j in range(m):
            gt_ref[mi * m + j, 0:fm, :] = (gin[mi, j].astype(F32) * count**-0.5).astype(BF)

    @pl.loop(0, blocks)
    def _(i):
        for at, fs in enumerate(slots[:blocks]):
            if fs:

                @pl.when(i == at)
                def _():
                    for f in fs:
                        f()

        rr = pl.ds(pl.multiple_of(i * rb, 16), rb)
        for c in copies(i):
            c.wait()
        v = vbuf[rr, :]
        aux = aux_ref[rr, :]
        mean = aux[:, 64:65]
        rstd = aux[:, 127:128]
        g = dot_nt(v, gt_ref[i // per])
        gl_f = g * der_ref[rr, :].astype(F32)
        gl = gl_f.astype(BF)
        ga = dot_nt(gl, w2_ref[...])
        pre = jnp.where(lane < 64, aux, 0.0)
        act, slope = gelu_parts(pre)
        gmp = (ga * slope).astype(BF).astype(F32)
        u = (gmp * rstd).astype(BF)
        uf = u.astype(F32)
        m1 = jnp.sum(gmp * w1s_ref[0:1, :], axis=-1, keepdims=True) * (1.0 / width)
        m2 = jnp.sum(gmp * (pre - w1s_ref[1:2, :]), axis=-1, keepdims=True) * (1.0 / width)
        w2g_ref[...] += dot_tn(act.astype(BF)[:, :64], gl)
        x_ref[...] += dot_tn(u[:, :64], v)
        row_ref[0:1, :] += jnp.sum(gl_f, axis=0, keepdims=True)
        row_ref[1:2, :] += jnp.sum(gmp, axis=0, keepdims=True)
        row_ref[2:3, :] += jnp.sum(uf * mean, axis=0, keepdims=True)
        c1 = -rstd * m1
        s = -rstd * rstd * m2
        c1h, sh, mh = (t.astype(BF).astype(F32) for t in (c1, s, mean))
        ex = jnp.where(lane < 64, uf, 0.0)
        for pos, val in enumerate((c1h, c1 - c1h, sh, s - sh, mh, mean - mh)):
            ex = jnp.where(lane == 64 + pos, val, ex)
        co_ref[rr, :] = ex.astype(BF)
        put(i).start()

    shift = row_ref[...].T[0:64, 2:3]
    ms[0:64, :] = (x_ref[...] - shift).astype(BF)
    ms[64:96, :] = jnp.concatenate([vecs_ref[...], jnp.zeros((16, width), F32)], axis=0).astype(BF)
    td[0:64, :] = w2g_ref[...]
    td[64:72, :] = row_ref[...]
    td[72:80, :] = jnp.zeros((8, LANES), F32)

    def both_ways(at, dev, msrc, mdst, tsrc, tdst):
        a = remote(msrc, mdst, ssend.at[0, at], srecv.at[0, at], dev)
        b = remote(tsrc, tdst, ssend.at[1, at], srecv.at[1, at], dev)
        a.start()
        b.start()
        return a, b

    a, b = both_ways(0, me.core_dev, ms, mc, td, tc)
    for f in slots[blocks]:
        f()
    a.wait()
    b.wait()
    ms[...] = (ms[...].astype(F32) + mc[...].astype(F32)).astype(BF)
    td[...] += tc[...]
    mr = pl.ds(pl.multiple_of(me.c * 48, 16), 48)
    tr = pl.ds(pl.multiple_of(me.c * 40, 8), 40)
    for at, dev, mb, tb in ((1, me.x_dev, mx, tx), (2, me.y_dev, my, ty)):
        a, b = both_ways(at, dev, ms.at[mr], mb, td.at[tr], tb)
        a.wait()
        b.wait()
        ms[mr, :] = (ms[mr, :].astype(F32) + mb[...].astype(F32)).astype(BF)
        td[tr, :] += tb[...]

    def window(z):
        lo = jnp.minimum(z * (width // me.na) // LANES * LANES, width - 256)
        return pl.ds(pl.multiple_of(lo, LANES), 256)

    sent = []
    for k in range(1, me.na):
        z = me.back(k)
        sent += both_ways(
            2 + k, (me.shard(z, me.b, me.c), me.map), ms.at[mr, window(z)], mz.at[me.a], td.at[tr], tz.at[me.a]
        )
    mz[me.a] = ms[mr, window(me.a)]
    tz[me.a] = td[tr, :]
    for k in range(1, me.na):
        z = me.ahead(k)
        remote(mz.at[z], mz.at[z], ssend.at[0, 2 + k], srecv.at[0, 2 + k], me.core_dev).wait_recv()
        remote(tz.at[z], tz.at[z], ssend.at[1, 2 + k], srecv.at[1, 2 + k], me.core_dev).wait_recv()
    for d in sent:
        d.wait_send()
    t = mz[0].astype(F32)
    s = tz[0]
    for z in range(1, me.na):
        t = t + mz[z].astype(F32)
        s = s + tz[z]
    md[mr, :] = t
    td[tr, :] = s
    a, b = both_ways(me.na + 2, me.core_dev, md.at[mr], md.at[mr], td.at[tr], te)
    o = 1 - me.c
    mo, to = pl.ds(pl.multiple_of(o * 48, 16), 48), pl.ds(pl.multiple_of(o * 40, 8), 40)
    remote(md.at[mo], md.at[mo], ssend.at[0, me.na + 2], srecv.at[0, me.na + 2], me.core_dev).wait_recv()
    b.wait()
    a.wait_send()
    td[to, :] = te[...]
    win_ref[...] = md[...]
    tot_ref[...] = td[...]

    @pl.loop(0, blocks)
    def _(i):
        put(i).wait()

    red.finish()


RSTEP = 1.6


def backward(n, m, v, aux, der, gtok, ga, w1s, w2n, vecs, blocks, per, count):
    rows, width = v.shape
    rb = rows // blocks
    na, shard = n // 4, width // n
    micros, _, fm, _ = gtok.shape
    vm = pl.BlockSpec(memory_space=pltpu.VMEM)
    hb = pl.BlockSpec(memory_space=pltpu.HBM)
    sds = jax.ShapeDtypeStruct
    dma = pltpu.SemaphoreType.DMA

    return pl.pallas_call(
        functools.partial(backward_kernel, n, m, blocks, per, count),
        out_shape=(
            sds((rows, LANES), BF), sds((micros * m, LANES, width), BF), sds((8, shard, width), F32),
            sds((96, 256), F32), sds((80, LANES), F32),
        ),
        in_specs=[hb] * 5 + [vm] * 3,
        out_specs=(hb,) + (vm,) * 4,
        scratch_shapes=[
            pltpu.VMEM((rows, width), BF),
            pltpu.VMEM((rows, LANES), F32),
            pltpu.VMEM((rows, LANES), BF),
            pltpu.VMEM((rows, LANES), BF),
            pltpu.VMEM(gtok.shape, BF),
            pltpu.VMEM((64, width), F32),
            pltpu.VMEM((64, LANES), F32),
            pltpu.VMEM((8, LANES), F32),
        ]
        + reduce_buffers(na, 4, 2, shard, width)
        + [
            pltpu.VMEM((96, width), BF),
            pltpu.VMEM((96, width), BF),
            pltpu.VMEM((48, width), BF),
            pltpu.VMEM((48, width), BF),
            pltpu.VMEM((na, 48, 256), BF),
            pltpu.VMEM((96, 256), F32),
            pltpu.VMEM((80, LANES), F32),
            pltpu.VMEM((40, LANES), F32),
            pltpu.VMEM((40, LANES), F32),
            pltpu.VMEM((na, 40, LANES), F32),
            pltpu.VMEM((80, LANES), F32),
            pltpu.VMEM((40, LANES), F32),
        ]
        + [dma((blocks,))] * 4
        + [dma((6, 2 * na)), dma((6 * 8 * na,)), dma((6 * 8 * na,)), dma((micros * m,)), dma((micros * m,))]
        + [dma((2, na + 3)), dma((2, na + 3))],
        compiler_params=pltpu.CompilerParams(vmem_limit_bytes=VLIM, collective_id=1, has_side_effects=True),
    )(v, aux, der, gtok, ga, w1s, w2n, vecs)


def patch_out_kernel(v_ref, sel_ref, co_ref, gt_ref, bt_ref, o_ref):
    co = co_ref[...]
    ex = co.astype(F32)
    s = ex[:, 66:67] + ex[:, 67:68]
    mean = ex[:, 68:69] + ex[:, 69:70]
    left = jnp.concatenate([sel_ref[...], co], axis=1)
    right = jnp.concatenate([gt_ref[0], bt_ref[...]], axis=0)
    mm = dot(left, right)
    for k in range(v_ref.shape[1] // LANES):
        c = slice(k * LANES, (k + 1) * LANES)
        o_ref[:, c] = (mm[:, c] + (v_ref[:, c].astype(F32) - mean) * s).astype(BF)


def patch_out(v, sel, co, gts, bt, blocks, per):
    rows, width = v.shape
    rb = rows // blocks
    row = pl.BlockSpec((rb, width), lambda i: (i, 0))
    thin = pl.BlockSpec((rb, LANES), lambda i: (i, 0))
    return pl.pallas_call(
        patch_out_kernel,
        grid=(blocks,),
        out_shape=jax.ShapeDtypeStruct((rows, width), BF),
        in_specs=[
            row, thin, thin,
            pl.BlockSpec((1, LANES, width), lambda i: (i // per, 0, 0)),
            pl.BlockSpec((LANES, width), lambda i: (0, 0)),
        ],
        out_specs=row,
        compiler_params=pltpu.CompilerParams(vmem_limit_bytes=VLIM),
    )(v, sel, co, gts, bt)


def on_device(
    patches, keep, tl_gain, tl_bias, map_w1, map_b1, map_w2, map_b2, ln1_gain, ln1_bias, qkv_weight, qv_bias,
    out_weight, out_bias, ln2_gain, ln2_bias, fc1_weight, fc1_bias, fc2_weight, fc2_bias, cotangent,
):
    micros, group, frames, count, width = patches.shape
    groups = micros * group
    shard = tl_gain.shape[0]
    me = lax.axis_index("clip")
    per = 7
    blocks = groups * per
    pb = count // per
    rb = pb * frames
    v = jnp.transpose(patches, (0, 1, 3, 2, 4)).reshape(groups * count * frames, width)
    kx = jnp.transpose(keep, (0, 1, 3, 2)).reshape(blocks, pb, frames)
    kx = jnp.repeat(kx, MAPS, axis=2).astype(BF)
    kx = jnp.pad(kx, ((0, 0), (0, 4), (0, LANES - frames * MAPS)))
    n, m = width // shard, group
    b2rep = jnp.tile(map_b2.astype(F32), LANES // MAPS)[None]
    gains, biases, w1l = tl_gain.astype(F32)[:, None], tl_bias.astype(F32)[:, None], map_w1.astype(F32)
    q2 = map_w2.shape[0]
    par = -(-(shard + 1 + q2) // 16) * 16
    pa = jnp.concatenate([gains * w1l, biases * w1l], axis=1).astype(BF)
    b1row = lax.dynamic_update_slice(jnp.zeros((1, LANES), BF), map_b1[None], (0, me * q2))
    pa = jnp.concatenate([pa, b1row, jnp.tile(map_w2, (1, LANES // MAPS)), jnp.zeros((par - shard - 1 - q2, LANES), BF)])
    wide = width // 2
    fsh = fc1_bias.shape[0]
    vecs = jnp.stack([ln1_gain, ln1_bias, qv_bias[0], qv_bias[1], out_bias, ln2_gain, ln2_bias, fc2_bias])
    pb = lax.dynamic_update_slice(jnp.zeros((16, wide), BF), vecs, (0, (me * shard) % wide))
    pb = lax.dynamic_update_slice(pb, fc1_bias[None], (8, (me * fsh) % wide))
    wa, tok, aux, sel, der, vec, fb, bt, small = forward(
        n, m, v, kx, b2rep, pa, pb, qkv_weight, out_weight, fc1_weight, micros, frames, per, count
    )
    tok = tok.reshape(-1, width)
    w1s = small[0:8]
    w2n = jnp.pad(small[8:72].astype(BF), ((0, 64), (0, 0)))
    ff = fc1_weight.shape[1]
    out, ga, gtok, gvec, gb1, ob = token_layer(
        n, m, tok, cotangent.reshape(tok.shape), wa, fc2_weight, vec, fb
    )
    vecs = jnp.concatenate([gvec, jnp.swapaxes(gb1.reshape(n, -1, shard), 0, 1).reshape(-1, width)])
    vecs = jnp.pad(vecs, ((0, 16 - vecs.shape[0]), (0, 0)))
    co, gts, oa, win, tot = backward(
        n, m, v, aux, der, gtok.reshape(micros, m, -1, width), ga, w1s, w2n, vecs, blocks, per, count
    )
    pg = patch_out(v, sel, co, gts, bt, blocks, per)
    pg = jnp.transpose(pg.reshape(micros, group, count, frames, width), (0, 1, 3, 2, 4))
    if m > 2:
        oa, ob, win, tot = (lax.psum(t, "map") * 0.5 for t in (oa, ob, win, tot))
    lo = jnp.minimum(me // 4 * (width // (n // 4)) // LANES * LANES, width - 256)
    win = lax.dynamic_slice(win, (0, me * shard - lo), (96, shard))
    xs = win[:64].T
    gvec = win[64:72]
    fgrad = win[72 : 72 + ff // width].reshape(-1)
    gb = tot[65, :64]
    b2g = jnp.sum(tot[64].reshape(LANES // MAPS, MAPS), axis=0)
    w2g = lax.dynamic_slice(tot, (me * q2, 0), (q2, LANES)).reshape(q2, LANES // MAPS, MAPS).sum(axis=1)
    return (
        out.reshape(cotangent.shape),
        pg,
        jnp.sum(w1l * xs, axis=1),
        w1l @ gb,
        gains * xs + biases * gb[None],
        lax.dynamic_slice(gb, (me * q2,), (q2,)),
        w2g,
        b2g,
        gvec[0],
        gvec[1],
        jnp.concatenate([oa[0], oa[1], oa[2]], axis=1),
        gvec[2:4],
        oa[3],
        gvec[4],
        gvec[5],
        gvec[6],
        jnp.concatenate([oa[4 + q] for q in range(ff // width)], axis=1),
        fgrad,
        ob,
        gvec[7],
    )


def solution(mesh):
    weights = (
        P("clip"), P("clip"), P("clip", None), P("clip"), P("clip", None), P(), P("clip"), P("clip"), P("clip", None),
        P(None, "clip"), P("clip", None), P("clip"), P("clip"), P("clip"), P("clip", None), P("clip"), P("clip", None),
        P("clip"),
    )
    tokens = P(None, ("clip", "map"), None, None)
    frames = P(None, "clip", "map", None, None)
    return jax.shard_map(
        on_device,
        mesh=mesh,
        in_specs=(frames, P(None, "clip", "map", None)) + weights + (tokens,),
        out_specs=(tokens, frames) + weights,
        check_vma=False,
    )
```

```python
import functools

import jax
import jax.numpy as jnp
from jax import lax
from jax.experimental import pallas as pl
from jax.experimental.pallas import tpu as pltpu
from jax.sharding import PartitionSpec as P

HEAD = 64
MAPS = 8
LANES = 128
EPS = 1e-06
GC = 0.7978845608028654
GA = 0.044715
BF = jnp.bfloat16
F32 = jnp.float32
VLIM = 61 * 1024 * 1024


def dot(a, b):
    return lax.dot_general(a, b, (((1,), (0,)), ((), ())), preferred_element_type=F32)


def dot_nt(a, b):
    return lax.dot_general(a, b, (((1,), (1,)), ((), ())), preferred_element_type=F32)


def dot_tn(a, b):
    return lax.dot_general(a, b, (((0,), (0,)), ((), ())), preferred_element_type=F32)


def gelu_parts(x):
    x2 = x * x
    t = jnp.tanh(GC * x * (1.0 + GA * x2))
    act = 0.5 * x * (1.0 + t)
    slope = 0.5 * (1.0 + t) + 0.5 * x * (1.0 - t * t) * (GC * (1.0 + 3.0 * GA * x2))
    return act, slope


def col(x, n):
    return pl.ds(pl.multiple_of(x, n), n)


MESH = pl.DeviceIdType.MESH


class Place:
    def __init__(self, n, m):
        self.n, self.m, self.na = n, m, n // 4
        self.clip, self.map = lax.axis_index("clip"), lax.axis_index("map")
        self.a, self.b, self.c = self.clip // 4, (self.clip // 2) % 2, self.clip % 2
        self.half = self.map % 2
        self.twin = self.map + 1 - 2 * self.half
        self.core_dev = (self.shard(self.a, self.b, 1 - self.c), self.map)
        self.y_dev = (self.shard(self.a, 1 - self.b, self.c), self.map)
        self.x_dev = (self.clip, self.twin)

    def shard(self, a, b, c):
        return (a * 2 + b) * 2 + c

    def back(self, k):
        return lax.rem(self.a + self.na - k, self.na)

    def ahead(self, k):
        return lax.rem(self.a + k, self.na)

    def greet(self):
        bar = pltpu.get_barrier_semaphore()
        for k in range(1, self.n):
            pl.semaphore_signal(bar, inc=1, device_id=(lax.rem(self.clip + k, self.n), self.map), device_id_type=MESH)
        for k in range(1, self.m):
            pl.semaphore_signal(bar, inc=1, device_id=(self.clip, lax.rem(self.map + k, self.m)), device_id_type=MESH)
        pl.semaphore_wait(bar, self.n + self.m - 2)


def remote(src, dst, send, recv, dev):
    return pltpu.make_async_remote_copy(
        src_ref=src, dst_ref=dst, send_sem=send, recv_sem=recv, device_id=dev, device_id_type=MESH
    )


class Gather:
    def __init__(self, place, chunks, shards, sends, recvs):
        self.p, self.chunks, self.shards, self.sends, self.recvs = place, chunks, shards, sends, recvs
        self.started = []

    def block(self, i, s, half):
        ref, panels, rows, pitch, skip, _ = self.chunks[i]
        r = pl.ds(pl.multiple_of(s * pitch + skip, 8), rows)
        c = slice(None) if half is None else pl.ds(pl.multiple_of(half * (ref.shape[-1] // 2), LANES), ref.shape[-1] // 2)
        return ref.at[r, c] if panels is None else ref.at[panels, r, c]

    def send(self, i, at, dev, s, half, src=None):
        b = self.block(i, s, half)
        j = i * self.per() + at
        remote(b if src is None else src, b, self.sends.at[j], self.recvs.at[j], dev).start()
        self.started.append((i, j, half is None))

    def wait(self, i, at, s, half):
        b = self.block(i, s, half)
        j = i * self.per() + at
        remote(b, b, self.sends.at[j], self.recvs.at[j], self.p.core_dev).wait_recv()

    def per(self):
        return 11 * self.p.na

    def at_z(self, k):
        return k - 1

    def at_y(self, k):
        return self.p.na - 1 + k

    def at_x(self, side, k):
        return (2 + side) * self.p.na + k

    def at_diag_y(self, k):
        return 4 * self.p.na + k

    def at_core(self, e):
        return 5 * self.p.na + e

    def own(self, i):
        p, src = self.p, self.shards[i]
        w = src.shape[-1] // 2
        c = pl.ds(pl.multiple_of(p.half * w, LANES), w)
        part = src.at[:, c] if len(src.shape) == 2 else src.at[:, :, c]
        for k in range(1, p.na):
            self.send(i, self.at_z(k), (p.shard(p.ahead(k), p.b, p.c), p.map), p.clip, p.half, part)
        self.send(i, self.at_y(0), p.y_dev, p.clip, None, src)
        self.send(i, self.at_core(0), p.core_dev, p.clip, None, src)

    def by_x(self, i):
        return self.chunks[i][5]

    def from_z(self, i, k):
        p = self.p
        s = p.shard(p.back(k), p.b, p.c)
        self.wait(i, self.at_z(k), s, p.half)
        self.send(i, self.at_x(0, k), p.x_dev, s, p.half)
        self.send(i, self.at_y(k), p.y_dev, s, p.half)
        self.send(i, self.at_core(k), p.core_dev, s, p.half)

    def from_y(self, i, k):
        p = self.p
        if k == 0:
            s = p.shard(p.a, 1 - p.b, p.c)
            self.wait(i, self.at_y(0), s, None)
            self.send(i, self.at_core(p.na), p.core_dev, s, None)
            return
        s = p.shard(p.back(k), 1 - p.b, p.c)
        self.wait(i, self.at_y(k), s, p.half)
        if self.by_x(i):
            self.send(i, self.at_x(1, k), p.x_dev, s, p.half)
        self.send(i, self.at_core(p.na + k), p.core_dev, s, p.half)

    def from_x(self, i, side, k):
        p = self.p
        b = p.b if side == 0 else 1 - p.b
        s = p.shard(p.back(k), b, p.c)
        by_x = self.by_x(i)
        self.wait(i, self.at_x(side, k) if by_x or side == 0 else self.at_diag_y(k), s, 1 - p.half)
        if side == 0 and not by_x:
            self.send(i, self.at_diag_y(k), p.y_dev, s, 1 - p.half)
        self.send(i, self.at_core((2 + side) * p.na + k), p.core_dev, s, 1 - p.half)

    def from_core(self, i):
        p, o = self.p, 1 - self.p.c
        self.wait(i, self.at_core(0), p.shard(p.a, p.b, o), None)
        self.wait(i, self.at_core(p.na), p.shard(p.a, 1 - p.b, o), None)
        for k in range(1, p.na):
            for side in range(2):
                s = p.shard(p.back(k), p.b if side == 0 else 1 - p.b, o)
                self.wait(i, self.at_core(p.na * side + k), s, p.half)
                self.wait(i, self.at_core((2 + side) * p.na + k), s, 1 - p.half)

    def finish(self, first=0):
        for i in range(first, len(self.chunks)):
            self.from_core(i)
        for i, j, full in self.started:
            b = self.block(i, self.p.clip, None if full else self.p.half)
            remote(b, b, self.sends.at[j], self.recvs.at[j], self.p.core_dev).wait_send()

    def events(self):
        n, ks = len(self.chunks), range(1, self.p.na)
        call = functools.partial
        out = [call(self.own, i) for i in range(AHEAD)]
        for i in range(n + 2):
            if i < n:
                for k in ks:
                    out.append(call(self.from_z, i, k))
                    if k == self.p.na - 2 and i + AHEAD < n:
                        out.append(call(self.own, i + AHEAD))
                out.append(call(self.from_y, i, 0))
            if 0 <= i - 1 < n:
                out += [call(self.from_y, i - 1, k) for k in ks]
                out += [call(self.from_x, i - 1, 0, k) for k in ks]
            if 0 <= i - 2 < n:
                out += [call(self.from_x, i - 2, 1, k) for k in ks]
        return out


def forward_kernel(
    n, m, blocks, per, count, v_ref, kx_ref, b2_ref, pa_ref, pb_ref, wq_ref, wo_ref, w1_ref,
    wa_ref, tok_ref, aux_ref, sel_ref, der_ref, vec_ref, fb_ref, wt_ref, small_ref,
    vbuf, acc, pool, rmat, delta, pag, pbg, w1v, w2v, ss, ws_ref, vsem, lsem, gsend, grecv, psend, precv, tsend, trecv,
):
    rows, width = v_ref.shape
    rb = rows // blocks
    frames = rb // (kx_ref.shape[1] - 4)
    fm = tok_ref.shape[2]
    me = Place(n, m)
    shard = width // n
    ff = w1_ref.shape[1]
    fsh = ff // n

    micros = tok_ref.shape[0]

    def load(blk, i):
        r = pl.ds(blk * rb, rb)
        return pltpu.make_async_copy(v_ref.at[r], vbuf.at[r], vsem.at[i])

    def token_copy(gi, mi, j, back=False):
        dst = tok_ref.at[mi, j] if back else tok_ref.at[mi, me.map]
        return remote(pool.at[mi * m + j, pl.ds(0, fm)], dst, tsend.at[gi], trecv.at[gi], (me.clip, j))

    @pl.loop(0, blocks)
    def _(i):
        gi = i // per
        load(((gi % micros) * m + lax.rem(me.map + 1 + gi // micros, m)) * per + i % per, i).start()

    own = pl.ds(pl.multiple_of(me.clip * shard, 8), shard)
    for q in range(3):
        ws_ref[q] = wq_ref[:, q * width : (q + 1) * width]
    ws_ref[3] = wo_ref[...]
    for q in range(ff // width):
        ws_ref[4 + q] = w1_ref[:, q * width : (q + 1) * width]
    local = [(ws_ref, wa_ref.at[:, own])]
    local.append((pa_ref, pag.at[me.clip]))
    local.append((pb_ref, pbg.at[me.clip]))
    local = [pltpu.make_async_copy(s, d, lsem.at[i]) for i, (s, d) in enumerate(local)]
    for d in local:
        d.start()
    me.greet()
    small = []
    for k in range(1, n):
        dev = (lax.rem(me.clip + k, n), me.map)
        small.append(remote(pa_ref, pag.at[me.clip], psend.at[0, k], precv.at[0, k], dev))
        small[-1].start()
    for d in local[1:]:
        d.wait()
    chunks = [(wa_ref, pl.ds(2 * q, 2), shard, shard, 0, q != 2) for q in range(3)]
    shards = [ws_ref.at[pl.ds(2 * q, 2)] for q in range(3)]
    g = Gather(me, chunks, shards, gsend, grecv)
    todo = g.events()
    slots = [[] for _ in range(blocks + 1)]
    for at, f in enumerate(todo[AHEAD:]):
        slots[min(int(at * STEP * blocks / len(todo)), blocks)].append(f)
    for f in todo[:AHEAD]:
        f()
    for k in range(1, n):
        dev = (lax.rem(me.clip + k, n), me.map)
        small.append(remote(pb_ref, pbg.at[me.clip], psend.at[1, k], precv.at[1, k], dev))
        small[-1].start()

    r2 = lax.broadcasted_iota(jnp.int32, rmat.shape, 0)
    c2 = lax.broadcasted_iota(jnp.int32, rmat.shape, 1)
    rmat[...] = jnp.where(r2 // frames == c2, 1.0, 0.0).astype(BF)
    r1 = lax.broadcasted_iota(jnp.int32, delta.shape, 0)
    c1 = lax.broadcasted_iota(jnp.int32, delta.shape, 1)
    delta[...] = jnp.where(r1 % frames == c1 // MAPS, 1.0, 0.0)

    for k in range(1, n):
        s = lax.rem(me.clip + n - k, n)
        remote(pa_ref, pag.at[s], psend.at[0, k], precv.at[0, k], me.core_dev).wait_recv()
    par = pa_ref.shape[0]
    flat = pag[...].reshape(n * par, LANES)
    q2 = 64 // n

    def pick(lo, count_rows, want_s, want_j):
        r = lax.broadcasted_iota(jnp.int32, (count_rows, 1), 0) + lo
        kk = lax.broadcasted_iota(jnp.int32, (1, n * par), 1)
        s, j = kk // par, kk % par
        sel = jnp.logical_and(s == want_s(r), j == want_j(r))
        return dot(jnp.where(sel, 1.0, 0.0).astype(BF), flat)

    lane = lax.broadcasted_iota(jnp.int32, (1, LANES), 1)
    for q in range(width // 128):
        got = pick(q * 128, 128, lambda r: r // shard, lambda r: r % shard)
        got = jnp.where(lane < 64, got, jnp.where(lane == 64, 1.0, 0.0))
        w1v[q * 128 : (q + 1) * 128, :] = got.astype(BF)
        wt_ref[0:64, q * 128 : (q + 1) * 128] = got.T[0:64, :].astype(BF)
    tail = lax.broadcasted_iota(jnp.int32, (64, width), 0)
    wt_ref[64:128, :] = jnp.where(tail < 2, 1.0, 0.0).astype(BF)
    got = pick(0, 64, lambda r: r // q2, lambda r: shard + 1 + r % q2)
    w2v[...] = got.astype(BF)
    small_ref[...] = jnp.zeros(small_ref.shape, F32)
    small_ref[8:72, :] = got
    r = lax.broadcasted_iota(jnp.int32, (8, 1), 0)
    kk = lax.broadcasted_iota(jnp.int32, (1, n * par), 1) % par
    sums = dot(jnp.where(jnp.logical_or(jnp.logical_and(r == 0, kk < shard), jnp.logical_and(r == 1, kk == shard)), 1.0, 0.0).astype(BF), flat)
    csum = jnp.where(lane < 64, sums[0:1, :], 0.0)
    cadd = jnp.where(lane < 64, pltpu.roll(sums, 64, 1)[0:1, :] + sums[1:2, :], 0.0)
    ss[0:1, :] = csum
    ss[1:2, :] = cadd
    small_ref[0:1, :] = csum
    small_ref[1:2, :] = cadd

    @pl.loop(0, blocks)
    def _(i):
        for at, fs in enumerate(slots[:blocks]):
            if fs:

                @pl.when(i == at)
                def _():
                    for f in fs:
                        f()

        gi = i // per
        j = lax.rem(me.map + 1 + gi // micros, m)
        gr = (gi % micros) * m + j
        blk = gr * per + i % per
        rr = pl.ds(pl.multiple_of(blk * rb, 16), rb)
        load(blk, i).wait()
        v = vbuf[rr, :]
        mm = dot(v, w1v[...])
        mean = mm[:, 64:65] * (1.0 / width)
        sq = jnp.zeros((rb, LANES), F32)
        for k in range(width // LANES):
            c = v[:, k * LANES : (k + 1) * LANES].astype(F32) - mean
            sq = sq + c * c
        rstd = lax.rsqrt(jnp.sum(sq, axis=-1, keepdims=True) * (1.0 / width) + EPS)
        pre = rstd * (mm - mean * ss[0:1, :]) + ss[1:2, :]
        act, _ = gelu_parts(pre)
        logit = dot(act.astype(BF)[:, :64], w2v[...]) + b2_ref[...]
        sig = 1.0 / (1.0 + jnp.exp(-logit))
        mask = dot(rmat[...], kx_ref[blk]) * delta[...]
        sm = sig * mask
        sel = sm.astype(BF)
        sel_ref[rr, :] = sel
        der_ref[rr, :] = (sm * (1.0 - sig)).astype(BF)
        ln = lax.broadcasted_iota(jnp.int32, (rb, LANES), 1)
        aux_ref[rr, :] = jnp.where(ln < 64, pre, jnp.where(ln < 96, mean, rstd))
        part = dot_tn(sel, v)

        @pl.when(i % per == 0)
        def _():
            acc[...] = part

        @pl.when(i % per != 0)
        def _():
            acc[...] += part

        @pl.when(i % per == per - 1)
        def _():
            pool[gr] = (acc[...] * (count**-0.5)).astype(BF)

            @pl.when(gi < micros * (m - 1))
            def _():
                token_copy(gi, gi % micros, j).start()

    for mi in range(micros):
        mine = pltpu.make_async_copy(pool.at[mi * m + me.map, pl.ds(0, fm)], tok_ref.at[mi, me.map], lsem.at[8 + mi])
        mine.start()
        mine.wait()
    for f in slots[blocks]:
        f()
    for k in range(1, n):
        s = lax.rem(me.clip + n - k, n)
        remote(pb_ref, pbg.at[s], psend.at[1, k], precv.at[1, k], me.core_dev).wait_recv()
    wide = pb_ref.shape[1]
    each = wide // shard
    for q in range(width // wide):
        t = pbg[q * each].astype(F32)
        for s in range(q * each + 1, (q + 1) * each):
            t = t + pbg[s].astype(F32)
        vec_ref[:, q * wide : (q + 1) * wide] = t[0:8, :]
    each = wide // fsh
    for q in range(ff // wide):
        t = pbg[q * each].astype(F32)
        for s in range(q * each + 1, (q + 1) * each):
            t = t + pbg[s].astype(F32)
        fb_ref[:, q * wide : (q + 1) * wide] = t[8:9, :]
    for gi in range(micros * (m - 1)):
        token_copy(gi, gi % micros, lax.rem(me.map + 1 + gi // micros, m)).wait_send()
        k = 1 + gi // micros
        token_copy(gi, gi % micros, lax.rem(me.map + m - k, m), True).wait_recv()
    g.finish()
    for d in small:
        d.wait_send()
    local[0].wait()


STEP = 0.7
AHEAD = 2


def forward(n, m, v, kx, b2rep, pa, pb, wq, wo, w1, micros, frames, per, count):
    rows, width = v.shape
    blocks = kx.shape[0]
    rb = rows // blocks
    ff = w1.shape[1]
    groups = blocks // per
    copies = 6 * 11 * (n // 4)
    sds = jax.ShapeDtypeStruct
    vm = pl.BlockSpec(memory_space=pltpu.VMEM)
    hb = pl.BlockSpec(memory_space=pltpu.HBM)
    dma = pltpu.SemaphoreType.DMA
    return pl.pallas_call(
        functools.partial(forward_kernel, n, m, blocks, per, count),
        out_shape=(
            sds((8, width, width), BF),
            sds((micros, m, frames * MAPS, width), BF),
            sds((rows, LANES), F32),
            sds((rows, LANES), BF),
            sds((rows, LANES), BF),
            sds((8, width), F32),
            sds((1, ff), F32),
            sds((LANES, width), BF),
            sds((72, LANES), F32),
        ),
        in_specs=[hb] + [vm] * 7,
        out_specs=(hb, hb) + (vm,) * 7,
        scratch_shapes=[
            pltpu.VMEM((rows, width), BF),
            pltpu.VMEM((LANES, width), F32),
            pltpu.VMEM((groups, LANES, width), BF),
            pltpu.VMEM((rb, kx.shape[1]), BF),
            pltpu.VMEM((rb, LANES), F32),
            pltpu.VMEM((n,) + pa.shape, BF),
            pltpu.VMEM((n,) + pb.shape, BF),
            pltpu.VMEM((width, LANES), BF),
            pltpu.VMEM((64, LANES), BF),
            pltpu.VMEM((8, LANES), F32),
            pltpu.VMEM((8, width // n, width), BF),
            dma((blocks,)), dma((16,)), dma((copies,)), dma((copies,)), dma((2, n)), dma((2, n)),
            dma((micros * m,)), dma((micros * m,)),
        ],
        compiler_params=pltpu.CompilerParams(vmem_limit_bytes=VLIM, collective_id=0, has_side_effects=True),
    )(v, kx, b2rep, pa, pb, wq, wo, w1)


def ln_stats(t):
    mean = jnp.mean(t, axis=-1, keepdims=True)
    c = t - mean
    rstd = lax.rsqrt(jnp.mean(c * c, axis=-1, keepdims=True) + EPS)
    return c * rstd, rstd


def token_kernel(
    places, m, tok, cot, wa_hbm, w1s, w2s, vec, b1,
    out_ref, ga_hbm, gtok_ref, gvec_ref, gb1_ref, part_hbm,
    n1, joined, probs, att, mixed, n2, act, slope, gacc, gbr, tr, wa, w2, ga_ref, g2_ref, wsv,
    own_b, rc_b, rx_b, ry_b, wsem, osem, psem, lsem, gsend, grecv, rsend, rrecv,
):
    n, d = tok.shape
    ff = g2_ref.shape[1]
    fsh = ff // places
    per = d // 256
    seq = 256
    micros = n // seq
    pairs = d // LANES
    ch = 64
    cb = 256
    chunks = n // ch
    lane = lax.broadcasted_iota(jnp.int32, (1, LANES), 1)
    first = lane < HEAD
    me = Place(places, m)

    def panel(q):
        return pltpu.make_async_copy(wa_hbm.at[q], wa.at[q], wsem.at[q])

    def panel_out(q):
        return pltpu.make_async_copy(ga_ref.at[q], ga_hbm.at[q], osem.at[q])

    for q in range(6):
        panel(q).start()
    shard = w1s.shape[0]
    for q in range(2):
        wsv[q] = w1s[:, (2 + q) * d : (3 + q) * d]
    own6 = pltpu.make_async_copy(
        wsv, wa.at[pl.ds(6, 2), pl.ds(pl.multiple_of(me.clip * shard, 8), shard)], wsem.at[9]
    )
    own6.start()
    own = pltpu.make_async_copy(w2s, w2.at[pl.ds(pl.multiple_of(me.clip * fsh, 8), fsh)], wsem.at[8])
    own.start()
    me.greet()
    g = Gather(
        me,
        [(wa, pl.ds(6, 2), shard, shard, 0, True)]
        + [(w2, None, fsh // 2, fsh, q * (fsh // 2), q == 0) for q in range(2)],
        [wsv] + [w2s.at[pl.ds(q * (fsh // 2), fsh // 2)] for q in range(2)],
        gsend,
        grecv,
    )
    for i in range(3):
        g.own(i)
    todo = [f for f in g.events() if f.func.__name__ != "own"]
    before, beside = 9 + micros * pairs, ff // cb
    early = [[] for _ in range(before + beside)]
    cut = 1 + max(at for at, f in enumerate(todo) if f.args[0] == 0)
    for at, f in enumerate(todo[:cut]):
        early[at * before // cut].append(f)
    for at, f in enumerate(todo[cut:]):
        early[before + at * beside // (len(todo) - cut)].append(f)

    red = Reduce(
        me, [(g2_ref, pl.ds(0, 1), fsh // 2, fsh, q * (fsh // 2), q == 0) for q in range(2)],
        *([t.at[0], t.at[1]] for t in (own_b, rc_b, rx_b, ry_b)), None, None, lsem, rsend, rrecv,
    )

    steps = [functools.partial(f, i) for f in (red.stage1, red.stage2, red.add_second) for i in range(2)]

    def part_out(i, k):
        return pltpu.make_async_copy(red.own[i].at[2 * k], part_hbm.at[i, k], psem.at[i, k])

    def at_step(i, slots):
        for at, fs in enumerate(slots):
            if fs:

                @pl.when(i == at)
                def _():
                    for f in fs:
                        f()

    def rows_of(i):
        return pl.ds(pl.multiple_of(i * ch, ch), ch)

    def transpose_into(src):
        @pl.loop(0, n // 128)
        def _(i):
            r = pl.ds(pl.multiple_of(i * 128, 128), 128)
            tr[:, r] = src[r, :].astype(F32).T.astype(BF)

    gvec_ref[...] = jnp.zeros(gvec_ref.shape, F32)

    def add_row(i, val):
        gvec_ref[i : i + 1, :] += jnp.sum(val, axis=0, keepdims=True)

    @pl.loop(0, chunks)
    def _(i):
        xh, _ = ln_stats(tok[rows_of(i), :].astype(F32))
        n1[rows_of(i), :] = (xh * vec[0:1, :] + vec[1:2, :]).astype(BF)

    for blk in range(3):
        panel(blk).wait()

        @pl.loop(0, d // cb)
        def _(j):
            at_step(j, early[3 * blk : 3 * blk + 3])
            o = pl.multiple_of(blk * d + j * cb, cb)
            r = dot(n1[...], wa[blk, :, col(j * cb, cb)])
            if blk == 0:
                r = r + vec[2:3, col(j * cb, cb)]
            if blk == 2:
                r = r + vec[3:4, col(j * cb, cb)]
            joined[:, pl.ds(o, cb)] = r.astype(BF)

    def heads_of(ref, i, base):
        m, pr = i // pairs, i % pairs
        r = pl.ds(pl.multiple_of(m * seq, seq), seq)
        return ref[r, pl.ds(pl.multiple_of(base + pr * LANES, LANES), LANES)]

    def put_heads(ref, i, base, val):
        m, pr = i // pairs, i % pairs
        r = pl.ds(pl.multiple_of(m * seq, seq), seq)
        ref[r, pl.ds(pl.multiple_of(base + pr * LANES, LANES), LANES)] = val

    zero = jnp.zeros((seq, LANES), BF)

    @pl.loop(0, micros * pairs)
    def _(i):
        at_step(i, early[9 : 9 + micros * pairs])
        q = (heads_of(joined, i, 0).astype(F32) * (HEAD**-0.5)).astype(BF)
        k = heads_of(joined, i, d)
        v = heads_of(joined, i, 2 * d)
        total = jnp.zeros((seq, LANES), F32)
        for e in range(2):
            mine = first if e == 0 else jnp.logical_not(first)
            s = dot_nt(jnp.where(mine, q, zero), k)
            ex = jnp.exp(s - jnp.max(s, axis=-1, keepdims=True))
            low = (ex * (1.0 / jnp.sum(ex, axis=-1, keepdims=True))).astype(BF)
            probs[i * 2 + e] = low
            total = total + dot(low, jnp.where(mine, v, zero))
        put_heads(att, i, 0, total.astype(BF))

    for q in range(3, 6):
        panel(q).wait()

    @pl.loop(0, d // cb)
    def _(j):
        c = col(j * cb, cb)
        mixed[:, c] = tok[:, c].astype(F32) + (dot(att[...], wa[3, :, c]) + vec[4:5, c])

    @pl.loop(0, chunks)
    def _(i):
        xh, _ = ln_stats(mixed[rows_of(i), :])
        n2[rows_of(i), :] = (xh * vec[5:6, :] + vec[6:7, :]).astype(BF)

    g.from_core(0)
    own6.wait()

    @pl.loop(0, ff // cb)
    def _(j):
        at_step(j, early[9 + micros * pairs :])
        c = col(j * cb, cb)
        a, s = gelu_parts(dot(n2[...], wa[4 + j // per, :, col((j % per) * cb, cb)]) + b1[0:1, c])
        act[:, c] = a.astype(BF)
        slope[:, c] = s.astype(BF)

    @pl.loop(0, ff // cb)
    def _(j):
        c = col(j * cb, cb)
        g2_ref[0, c, :] = dot_tn(act[:, c], cot[...]).astype(BF)

    red.stage0(0)
    red.stage0(1)
    g.finish(1)
    own.wait()

    @pl.loop(0, d // cb)
    def _(j):
        c = col(j * cb, cb)
        out_ref[:, c] = (mixed[:, c] + (dot(act[...], w2[:, c]) + vec[7:8, c])).astype(BF)

    transpose_into(n2)
    for f in steps[:2]:
        f()

    @pl.loop(0, ff // cb)
    def _(j):
        c = col(j * cb, cb)
        g = (dot_nt(cot[...], w2[c, :]) * slope[:, c].astype(F32)).astype(BF)
        act[:, c] = g
        gb1_ref[0:1, c] = jnp.sum(g.astype(F32), axis=0, keepdims=True)
        ga_ref[4 + j // per, :, col((j % per) * cb, cb)] = dot(tr[...], g).astype(BF)

    for q in range(4, 8):
        panel_out(q).start()

    @pl.loop(0, d // cb)
    def _(j):
        c = col(j * cb, cb)
        total = jnp.zeros((n, cb), F32)
        for q in range(ff // d):
            total = total + dot_nt(act[:, q * d : (q + 1) * d], wa[4 + q, c, :])
        gacc[:, c] = total

    for f in steps[2:4]:
        f()

    @pl.loop(0, chunks)
    def _(i):
        r = rows_of(i)
        xh, rstd = ln_stats(mixed[r, :])
        e = gacc[r, :]
        add_row(5, e * xh)
        add_row(6, e)
        eg = e * vec[5:6, :]
        back = eg - jnp.mean(eg, axis=-1, keepdims=True) - xh * jnp.mean(eg * xh, axis=-1, keepdims=True)
        c = cot[r, :].astype(F32)
        g = c + back * rstd
        mixed[r, :] = g
        low = g.astype(BF)
        gbr[r, :] = low
        add_row(4, low.astype(F32))
        add_row(7, c)

    transpose_into(att)

    @pl.loop(0, d // cb)
    def _(j):
        c = col(j * cb, cb)
        ga_ref[3, :, c] = dot(tr[...], gbr[:, c]).astype(BF)
        att[:, c] = dot_nt(gbr[...], wa[3, c, :]).astype(BF)

    panel_out(3).start()
    late = [[] for _ in range(micros * pairs)]
    late[len(late) // 2] = steps[4:6]

    @pl.loop(0, micros * pairs)
    def _(i):
        at_step(i, late)
        q = (heads_of(joined, i, 0).astype(F32) * (HEAD**-0.5)).astype(BF)
        k = heads_of(joined, i, d)
        v = heads_of(joined, i, 2 * d)
        ga = heads_of(att, i, 0)
        gq = jnp.zeros((seq, LANES), F32)
        gk = jnp.zeros((seq, LANES), F32)
        gv = jnp.zeros((seq, LANES), F32)
        for e in range(2):
            mine = first if e == 0 else jnp.logical_not(first)
            low = probs[i * 2 + e]
            p = low.astype(F32)
            ga_e = jnp.where(mine, ga, zero)
            gp = dot_nt(ga_e, v)
            pg = p * gp
            gs = (pg - p * jnp.sum(pg, axis=-1, keepdims=True)).astype(BF)
            gv = gv + dot_tn(low, ga_e)
            gq = gq + dot(gs, jnp.where(mine, k, zero))
            gk = gk + dot_tn(gs, jnp.where(mine, q, zero))
        put_heads(joined, i, 0, (gq * (HEAD**-0.5)).astype(BF))
        put_heads(joined, i, d, gk.astype(BF))
        put_heads(joined, i, 2 * d, gv.astype(BF))

    transpose_into(n1)
    for i in range(2):
        for k in range(me.na):
            part_out(i, k).start()

    @pl.loop(0, 3 * d // cb)
    def _(j):
        c = col(j * cb, cb)
        ga_ref[j // per, :, col((j % per) * cb, cb)] = dot(tr[...], joined[:, c]).astype(BF)

    for q in range(3):
        panel_out(q).start()

    @pl.loop(0, d // cb)
    def _(j):
        c = col(j * cb, cb)
        total = jnp.zeros((n, cb), F32)
        for q in range(3):
            total = total + dot_nt(joined[:, q * d : (q + 1) * d], wa[q, c, :])
        gacc[:, c] = total

    @pl.loop(0, chunks)
    def _(i):
        r = rows_of(i)
        xh, rstd = ln_stats(tok[r, :].astype(F32))
        e = gacc[r, :]
        add_row(0, e * xh)
        add_row(1, e)
        add_row(2, joined[r, 0:d].astype(F32))
        add_row(3, joined[r, 2 * d : 3 * d].astype(F32))
        eg = e * vec[0:1, :]
        back = eg - jnp.mean(eg, axis=-1, keepdims=True) - xh * jnp.mean(eg * xh, axis=-1, keepdims=True)
        gtok_ref[r, :] = (mixed[r, :] + back * rstd).astype(BF)

    for i in range(2):
        for k in range(me.na):
            part_out(i, k).wait()
    for q in range(8):
        panel_out(q).wait()
    red.finish(second=False)


def token_layer(places, m, tok, cot, wa, w1s, w2s, vec, b1):
    n, d = tok.shape
    fsh = w2s.shape[0]
    ff = places * fsh
    vm = pl.BlockSpec(memory_space=pltpu.VMEM)
    hb = pl.BlockSpec(memory_space=pltpu.HBM)
    sds = jax.ShapeDtypeStruct
    heads = (n // 256) * (d // HEAD)
    na = places // 4
    dma = pltpu.SemaphoreType.DMA
    return pl.pallas_call(
        functools.partial(token_kernel, places, m),
        out_shape=(
            sds((n, d), BF), sds(wa.shape, BF), sds((n, d), BF), sds((8, d), F32), sds((1, ff), F32),
            sds((2, na, 1, fsh // 2, d), BF),
        ),
        in_specs=[vm, vm, hb, vm, vm, vm, vm],
        out_specs=(vm, hb, vm, vm, vm, hb),
        scratch_shapes=[
            pltpu.VMEM((n, d), BF),
            pltpu.VMEM((n, 3 * d), BF),
            pltpu.VMEM((heads, 256, 256), BF),
            pltpu.VMEM((n, d), BF),
            pltpu.VMEM((n, d), F32),
            pltpu.VMEM((n, d), BF),
            pltpu.VMEM((n, ff), BF),
            pltpu.VMEM((n, ff), BF),
            pltpu.VMEM((n, d), F32),
            pltpu.VMEM((n, d), BF),
            pltpu.VMEM((d, n), BF),
            pltpu.VMEM(wa.shape, BF),
            pltpu.VMEM((ff, d), BF),
            pltpu.VMEM(wa.shape, BF),
            pltpu.VMEM((1, ff, d), BF),
            pltpu.VMEM((2, w1s.shape[0], d), BF),
        ]
        + reduce_buffers(na, 2, 1, fsh // 2, d)[:4]
        + [dma((10,)), dma((8,)), dma((2, na)), dma((2, 2 * na)), dma((33 * na,)), dma((33 * na,)), dma((16 * na,)), dma((16 * na,))],
        compiler_params=pltpu.CompilerParams(vmem_limit_bytes=VLIM, collective_id=2, has_side_effects=True),
    )(tok, cot, wa, w1s, w2s, vec, b1)


def reduce_buffers(na, chunks, panels, rows, width):
    return [
        pltpu.VMEM((chunks, 2 * na, panels, rows, width), BF),
        pltpu.VMEM((chunks, 2 * na, panels, rows, width), BF),
        pltpu.VMEM((chunks, 2 * na - 2, panels, rows, width // 2), BF),
        pltpu.VMEM((chunks, na, panels, rows, width), BF),
        pltpu.VMEM((chunks, na - 1, panels, rows, width // 2), BF),
        pltpu.VMEM((chunks, panels, rows, width), BF),
    ]


class Reduce:
    def __init__(self, place, chunks, own, rc, rx, ry, rz, rf, lsem, sends, recvs):
        self.p, self.chunks, self.own, self.rc, self.rx, self.ry, self.rz, self.rf = place, chunks, own, rc, rx, ry, rz, rf
        self.lsem, self.sends, self.recvs = lsem, sends, recvs

    def sem(self, i, at):
        j = i * 8 * self.p.na + at
        return self.sends.at[j], self.recvs.at[j]

    def send(self, i, at, src, dst, dev):
        s, r = self.sem(i, at)
        remote(src, dst, s, r, dev).start()

    def grad(self, i, k, side, core):
        p = self.p
        ref, panels, rows, pitch, skip, _ = self.chunks[i]
        s = p.shard(p.back(k), p.b if side == 0 else 1 - p.b, core)
        return ref.at[panels, pl.ds(pl.multiple_of(s * pitch + skip, 8), rows)]

    def cols(self, half):
        w = self.chunks[0][0].shape[-1] // 2
        return pl.ds(pl.multiple_of(half * w, LANES), w)

    def mine(self):
        return self.cols(self.p.half)

    def other(self):
        return self.cols(1 - self.p.half)

    def core_copies(self, i):
        p = self.p
        return [
            (2 * k + side, self.grad(i, k, side, 1 - p.c), self.rc[i].at[2 * k + side], p.core_dev)
            for k in range(p.na) for side in range(2)
        ]

    def local_copies(self, i):
        p = self.p
        return [
            pltpu.make_async_copy(self.grad(i, k, side, p.c), self.own[i].at[2 * k + side], self.lsem.at[i, 2 * k + side])
            for k in range(p.na) for side in range(2)
        ]

    def x_copies(self, i):
        p, base = self.p, 2 * self.p.na
        sides = range(2) if self.chunks[i][5] else range(1)
        return [
            (base + 2 * k + side, self.own[i].at[2 * k + side, :, :, self.other()], self.rx[i].at[2 * (k - 1) + side], p.x_dev)
            for k in range(1, p.na) for side in sides
        ]

    def y_copies(self, i):
        p, base = self.p, 4 * self.p.na
        out = []
        for k in range(p.na):
            src, dst = self.own[i].at[2 * k + 1], self.ry[i].at[k]
            if self.chunks[i][5] and k:
                src, dst = src.at[:, :, self.mine()], dst.at[:, :, self.mine()]
            out.append((base + k, src, dst, p.y_dev))
        return out

    def z_copies(self, i):
        p, base = self.p, 5 * self.p.na
        return [
            (base + k, self.own[i].at[2 * k, :, :, self.mine()], self.rz[i].at[k - 1], (p.shard(p.back(k), p.b, p.c), p.map))
            for k in range(1, p.na)
        ]

    def last_copies(self, i):
        return [(6 * self.p.na, self.own[i].at[0], self.rf[i], self.p.x_dev)]

    def start(self, i, copies):
        for at, src, dst, dev in copies:
            self.send(i, at, src, dst, dev)

    def wait(self, i, copies):
        for at, src, dst, dev in copies:
            s, r = self.sem(i, at)
            remote(dst, dst, s, r, self.p.core_dev).wait_recv()

    def add(self, ref, at, cols, inc):
        a = ref[at, :, :, cols]
        ref[at, :, :, cols] = (a.astype(F32) + inc.astype(F32)).astype(BF)

    def stage0(self, i):
        for c in self.local_copies(i):
            c.start()
        self.start(i, self.core_copies(i))

    def stage1(self, i):
        for c in self.local_copies(i):
            c.wait()
        self.wait(i, self.core_copies(i))

        @pl.loop(0, 2 * self.p.na)
        def _(j):
            self.own[i][j] = (self.own[i][j].astype(F32) + self.rc[i][j].astype(F32)).astype(BF)

        self.start(i, self.x_copies(i) if self.chunks[i][5] else self.y_copies(i))

    def add_x(self, i):
        self.wait(i, self.x_copies(i))
        both = self.chunks[i][5]

        @pl.loop(0, self.p.na - 1)
        def _(k):
            for side in range(2 if both else 1):
                self.add(self.own[i], 2 * k + 2 + side, self.mine(), self.rx[i][2 * k + side])

    def add_y(self, i):
        self.wait(i, self.y_copies(i))
        if not self.chunks[i][5]:

            @pl.loop(0, self.p.na)
            def _(k):
                self.own[i][2 * k] = (self.own[i][2 * k].astype(F32) + self.ry[i][k].astype(F32)).astype(BF)

            return
        self.own[i][0] = (self.own[i][0].astype(F32) + self.ry[i][0].astype(F32)).astype(BF)

        @pl.loop(1, self.p.na)
        def _(k):
            self.add(self.own[i], 2 * k, self.mine(), self.ry[i][k, :, :, self.mine()])

    def stage2(self, i):
        if self.chunks[i][5]:
            self.add_x(i)
            self.start(i, self.y_copies(i))
        else:
            self.add_y(i)
            self.start(i, self.x_copies(i))

    def add_second(self, i):
        if self.chunks[i][5]:
            self.add_y(i)
        else:
            self.add_x(i)

    def stage3(self, i):
        self.add_second(i)
        self.start(i, self.z_copies(i))

    def stage4(self, i):
        self.wait(i, self.z_copies(i))
        c = self.mine()
        t = self.own[i][0, :, :, c].astype(F32)
        for k in range(self.p.na - 1):
            t = t + self.rz[i][k].astype(F32)
        self.own[i][0, :, :, c] = t.astype(BF)
        self.start(i, self.last_copies(i))

    def stage5(self, i, put):
        self.wait(i, self.last_copies(i))
        put(i, self.own[i][0].astype(F32) + self.rf[i][...].astype(F32))

    def events(self, put):
        call, n = functools.partial, len(self.chunks)
        out = []
        for t in range(n // 2 + 4):
            for s in range(5, 0, -1):
                for i in (2 * (t - s + 1), 2 * (t - s + 1) + 1):
                    if 0 <= i < n:
                        out.append(call(self.stage5, i, put) if s == 5 else call(getattr(self, "stage%d" % s), i))
        return out

    def finish(self, first=True, second=True):
        kinds = [self.core_copies, self.x_copies, self.y_copies] if first else []
        kinds += [self.z_copies, self.last_copies] if second else []
        for i in range(len(self.chunks)):
            for c in kinds:
                for at, src, dst, dev in c(i):
                    s, r = self.sem(i, at)
                    remote(src, src, s, r, self.p.core_dev).wait_send()


def backward_kernel(
    n, m, blocks, per, count, v_ref, aux_hbm, der_hbm, gtok_ref, ga_ref, part_hbm, w1s_ref, w2_ref, vecs_ref,
    co_hbm, gt_ref, oa_ref, ob_ref, win_ref, tot_ref,
    vbuf, aux_ref, der_ref, co_ref, gin, x_ref, w2g_ref, row_ref,
    own_a, rc_a, rx_a, ry_a, rz_a, rf_a, own_b, rz_b, rf_b,
    ms, mc, mx, my, mz, md, tc, tx, ty, tz, td, te,
    vsem, asem, dsem, csem, psem, lsem, rsend, rrecv, bsend, brecv, tsend, trecv, ssend, srecv,
):
    rows, width = v_ref.shape
    rb = rows // blocks
    me = Place(n, m)
    shard = width // n
    micros, _, fm, _ = gtok_ref.shape

    def copies(i):
        r = pl.ds(i * rb, rb)
        return (
            pltpu.make_async_copy(v_ref.at[r], vbuf.at[r], vsem.at[i]),
            pltpu.make_async_copy(aux_hbm.at[r], aux_ref.at[r], asem.at[i]),
            pltpu.make_async_copy(der_hbm.at[r], der_ref.at[r], dsem.at[i]),
        )

    def put(i):
        r = pl.ds(i * rb, rb)
        return pltpu.make_async_copy(co_ref.at[r], co_hbm.at[r], csem.at[i])

    def part_in(i, k):
        return pltpu.make_async_copy(part_hbm.at[i, k], own_b.at[i, 2 * k], psem.at[i, k])

    for i in range(2):
        for k in range(me.na):
            part_in(i, k).start()
    me.greet()
    out = []
    for mi in range(micros):
        for k in range(1, m):
            j = lax.rem(me.map + k, m)
            d = remote(gtok_ref.at[mi, j], gin.at[mi, me.map], tsend.at[mi * m + k], trecv.at[mi * m + k], (me.clip, j))
            d.start()
            out.append(d)
        out.append(pltpu.make_async_copy(gtok_ref.at[mi, me.map], gin.at[mi, me.map], tsend.at[mi * m]))
        out[-1].start()

    order = (2, 3, 0, 1)
    chunks = [(ga_ref, pl.ds(2 * q, 2), shard, shard, 0, q % 2 == 0) for q in order]
    red = Reduce(
        me, chunks, *([t.at[q] for q in range(4)] for t in (own_a, rc_a, rx_a, ry_a, rz_a, rf_a)), lsem, rsend, rrecv
    )
    for i in range(4):
        red.stage0(i)
    half_fsh = ob_ref.shape[0] // 2
    fin = Reduce(
        me, [(ob_ref, None, half_fsh, half_fsh, 0, q == 0) for q in range(2)], [own_b.at[0], own_b.at[1]], None, None, None,
        [rz_b.at[0], rz_b.at[1]], [rf_b.at[0], rf_b.at[1]], None, bsend, brecv,
    )
    for i in range(2):
        for k in range(me.na):
            part_in(i, k).wait()
        fin.start(i, fin.z_copies(i))

    def put_fc2(i, val):
        ob_ref[i * half_fsh : (i + 1) * half_fsh, :] = val[0]

    def put_out(i, val):
        oa_ref[2 * order[i] : 2 * order[i] + 2] = val

    @pl.loop(0, blocks)
    def _(i):
        for c in copies(i):
            c.start()

    x_ref[...] = jnp.zeros(x_ref.shape, F32)
    w2g_ref[...] = jnp.zeros(w2g_ref.shape, F32)
    row_ref[...] = jnp.zeros(row_ref.shape, F32)
    lane = lax.broadcasted_iota(jnp.int32, (rb, LANES), 1)

    todo = red.events(put_out)
    todo[8:8] = [functools.partial(fin.stage4, i) for i in range(2)]
    todo[16:16] = [functools.partial(fin.stage5, i, put_fc2) for i in range(2)]
    slots = [[] for _ in range(blocks + 1)]
    for at, f in enumerate(todo[2:]):
        slots[min(int(at * RSTEP * blocks / len(todo)), blocks)].append(f)
    todo[0]()
    todo[1]()
    for mi in range(micros):
        for k in range(1, m):
            j = lax.rem(me.map + m - k, m)
            remote(gtok_ref.at[mi, j], gin.at[mi, j], tsend.at[mi * m + k], trecv.at[mi * m + k], me.core_dev).wait_recv()
    for mi in range(micros):
        for k in range(m):
            d = out[mi * m + k]
            if k < m - 1:
                d.wait_send()
            else:
                d.wait()
    gt_ref[...] = jnp.zeros(gt_ref.shape, BF)
    for mi in range(micros):
        for j in range(m):
            gt_ref[mi * m + j, 0:fm, :] = (gin[mi, j].astype(F32) * count**-0.5).astype(BF)

    @pl.loop(0, blocks)
    def _(i):
        for at, fs in enumerate(slots[:blocks]):
            if fs:

                @pl.when(i == at)
                def _():
                    for f in fs:
                        f()

        rr = pl.ds(pl.multiple_of(i * rb, 16), rb)
        for c in copies(i):
            c.wait()
        v = vbuf[rr, :]
        aux = aux_ref[rr, :]
        mean = aux[:, 64:65]
        rstd = aux[:, 127:128]
        g = dot_nt(v, gt_ref[i // per])
        gl_f = g * der_ref[rr, :].astype(F32)
        gl = gl_f.astype(BF)
        ga = dot_nt(gl, w2_ref[...])
        pre = jnp.where(lane < 64, aux, 0.0)
        act, slope = gelu_parts(pre)
        gmp = (ga * slope).astype(BF).astype(F32)
        u = (gmp * rstd).astype(BF)
        uf = u.astype(F32)
        m1 = jnp.sum(gmp * w1s_ref[0:1, :], axis=-1, keepdims=True) * (1.0 / width)
        m2 = jnp.sum(gmp * (pre - w1s_ref[1:2, :]), axis=-1, keepdims=True) * (1.0 / width)
        w2g_ref[...] += dot_tn(act.astype(BF)[:, :64], gl)
        x_ref[...] += dot_tn(u[:, :64], v)
        row_ref[0:1, :] += jnp.sum(gl_f, axis=0, keepdims=True)
        row_ref[1:2, :] += jnp.sum(gmp, axis=0, keepdims=True)
        row_ref[2:3, :] += jnp.sum(uf * mean, axis=0, keepdims=True)
        c1 = -rstd * m1
        s = -rstd * rstd * m2
        c1h, sh, mh = (t.astype(BF).astype(F32) for t in (c1, s, mean))
        ex = jnp.where(lane < 64, uf, 0.0)
        for pos, val in enumerate((c1h, c1 - c1h, sh, s - sh, mh, mean - mh)):
            ex = jnp.where(lane == 64 + pos, val, ex)
        co_ref[rr, :] = ex.astype(BF)
        put(i).start()

    shift = row_ref[...].T[0:64, 2:3]
    ms[0:64, :] = (x_ref[...] - shift).astype(BF)
    ms[64:96, :] = jnp.concatenate([vecs_ref[...], jnp.zeros((16, width), F32)], axis=0).astype(BF)
    td[0:64, :] = w2g_ref[...]
    td[64:72, :] = row_ref[...]
    td[72:80, :] = jnp.zeros((8, LANES), F32)

    def both_ways(at, dev, msrc, mdst, tsrc, tdst):
        a = remote(msrc, mdst, ssend.at[0, at], srecv.at[0, at], dev)
        b = remote(tsrc, tdst, ssend.at[1, at], srecv.at[1, at], dev)
        a.start()
        b.start()
        return a, b

    a, b = both_ways(0, me.core_dev, ms, mc, td, tc)
    for f in slots[blocks]:
        f()
    a.wait()
    b.wait()
    ms[...] = (ms[...].astype(F32) + mc[...].astype(F32)).astype(BF)
    td[...] += tc[...]
    mr = pl.ds(pl.multiple_of(me.c * 48, 16), 48)
    tr = pl.ds(pl.multiple_of(me.c * 40, 8), 40)
    for at, dev, mb, tb in ((1, me.x_dev, mx, tx), (2, me.y_dev, my, ty)):
        a, b = both_ways(at, dev, ms.at[mr], mb, td.at[tr], tb)
        a.wait()
        b.wait()
        ms[mr, :] = (ms[mr, :].astype(F32) + mb[...].astype(F32)).astype(BF)
        td[tr, :] += tb[...]

    def window(z):
        lo = jnp.minimum(z * (width // me.na) // LANES * LANES, width - 256)
        return pl.ds(pl.multiple_of(lo, LANES), 256)

    sent = []
    for k in range(1, me.na):
        z = me.back(k)
        sent += both_ways(
            2 + k, (me.shard(z, me.b, me.c), me.map), ms.at[mr, window(z)], mz.at[me.a], td.at[tr], tz.at[me.a]
        )
    mz[me.a] = ms[mr, window(me.a)]
    tz[me.a] = td[tr, :]
    for k in range(1, me.na):
        z = me.ahead(k)
        remote(mz.at[z], mz.at[z], ssend.at[0, 2 + k], srecv.at[0, 2 + k], me.core_dev).wait_recv()
        remote(tz.at[z], tz.at[z], ssend.at[1, 2 + k], srecv.at[1, 2 + k], me.core_dev).wait_recv()
    for d in sent:
        d.wait_send()
    t = mz[0].astype(F32)
    s = tz[0]
    for z in range(1, me.na):
        t = t + mz[z].astype(F32)
        s = s + tz[z]
    md[mr, :] = t
    td[tr, :] = s
    a, b = both_ways(me.na + 2, me.core_dev, md.at[mr], md.at[mr], td.at[tr], te)
    o = 1 - me.c
    mo, to = pl.ds(pl.multiple_of(o * 48, 16), 48), pl.ds(pl.multiple_of(o * 40, 8), 40)
    remote(md.at[mo], md.at[mo], ssend.at[0, me.na + 2], srecv.at[0, me.na + 2], me.core_dev).wait_recv()
    b.wait()
    a.wait_send()
    td[to, :] = te[...]
    win_ref[...] = md[...]
    tot_ref[...] = td[...]

    @pl.loop(0, blocks)
    def _(i):
        put(i).wait()

    red.finish()
    fin.finish(first=False)


RSTEP = 1.6


def backward(n, m, v, aux, der, gtok, ga, part, w1s, w2n, vecs, blocks, per, count):
    rows, width = v.shape
    rb = rows // blocks
    na, shard = n // 4, width // n
    micros, _, fm, _ = gtok.shape
    vm = pl.BlockSpec(memory_space=pltpu.VMEM)
    hb = pl.BlockSpec(memory_space=pltpu.HBM)
    sds = jax.ShapeDtypeStruct
    dma = pltpu.SemaphoreType.DMA

    return pl.pallas_call(
        functools.partial(backward_kernel, n, m, blocks, per, count),
        out_shape=(
            sds((rows, LANES), BF), sds((micros * m, LANES, width), BF), sds((8, shard, width), F32),
            sds((2 * part.shape[3], width), F32), sds((96, 256), F32), sds((80, LANES), F32),
        ),
        in_specs=[hb] * 6 + [vm] * 3,
        out_specs=(hb,) + (vm,) * 5,
        scratch_shapes=[
            pltpu.VMEM((rows, width), BF),
            pltpu.VMEM((rows, LANES), F32),
            pltpu.VMEM((rows, LANES), BF),
            pltpu.VMEM((rows, LANES), BF),
            pltpu.VMEM(gtok.shape, BF),
            pltpu.VMEM((64, width), F32),
            pltpu.VMEM((64, LANES), F32),
            pltpu.VMEM((8, LANES), F32),
        ]
        + reduce_buffers(na, 4, 2, shard, width)
        + [reduce_buffers(na, 2, 1, part.shape[3], width)[q] for q in (0, 4, 5)]
        + [
            pltpu.VMEM((96, width), BF),
            pltpu.VMEM((96, width), BF),
            pltpu.VMEM((48, width), BF),
            pltpu.VMEM((48, width), BF),
            pltpu.VMEM((na, 48, 256), BF),
            pltpu.VMEM((96, 256), F32),
            pltpu.VMEM((80, LANES), F32),
            pltpu.VMEM((40, LANES), F32),
            pltpu.VMEM((40, LANES), F32),
            pltpu.VMEM((na, 40, LANES), F32),
            pltpu.VMEM((80, LANES), F32),
            pltpu.VMEM((40, LANES), F32),
        ]
        + [dma((blocks,))] * 4
        + [dma((2, na)), dma((6, 2 * na)), dma((6 * 8 * na,)), dma((6 * 8 * na,)), dma((16 * na,)), dma((16 * na,)), dma((micros * m,)), dma((micros * m,))]
        + [dma((2, na + 3)), dma((2, na + 3))],
        compiler_params=pltpu.CompilerParams(vmem_limit_bytes=VLIM, collective_id=1, has_side_effects=True),
    )(v, aux, der, gtok, ga, part, w1s, w2n, vecs)


def patch_out_kernel(v_ref, sel_ref, co_ref, gt_ref, bt_ref, o_ref):
    co = co_ref[...]
    ex = co.astype(F32)
    s = ex[:, 66:67] + ex[:, 67:68]
    mean = ex[:, 68:69] + ex[:, 69:70]
    left = jnp.concatenate([sel_ref[...], co], axis=1)
    right = jnp.concatenate([gt_ref[0], bt_ref[...]], axis=0)
    mm = dot(left, right)
    for k in range(v_ref.shape[1] // LANES):
        c = slice(k * LANES, (k + 1) * LANES)
        o_ref[:, c] = (mm[:, c] + (v_ref[:, c].astype(F32) - mean) * s).astype(BF)


def patch_out(v, sel, co, gts, bt, blocks, per):
    rows, width = v.shape
    rb = rows // blocks
    row = pl.BlockSpec((rb, width), lambda i: (i, 0))
    thin = pl.BlockSpec((rb, LANES), lambda i: (i, 0))
    return pl.pallas_call(
        patch_out_kernel,
        grid=(blocks,),
        out_shape=jax.ShapeDtypeStruct((rows, width), BF),
        in_specs=[
            row, thin, thin,
            pl.BlockSpec((1, LANES, width), lambda i: (i // per, 0, 0)),
            pl.BlockSpec((LANES, width), lambda i: (0, 0)),
        ],
        out_specs=row,
        compiler_params=pltpu.CompilerParams(vmem_limit_bytes=VLIM),
    )(v, sel, co, gts, bt)


def on_device(
    patches, keep, tl_gain, tl_bias, map_w1, map_b1, map_w2, map_b2, ln1_gain, ln1_bias, qkv_weight, qv_bias,
    out_weight, out_bias, ln2_gain, ln2_bias, fc1_weight, fc1_bias, fc2_weight, fc2_bias, cotangent,
):
    micros, group, frames, count, width = patches.shape
    groups = micros * group
    shard = tl_gain.shape[0]
    me = lax.axis_index("clip")
    per = 7
    blocks = groups * per
    pb = count // per
    rb = pb * frames
    v = jnp.transpose(patches, (0, 1, 3, 2, 4)).reshape(groups * count * frames, width)
    kx = jnp.transpose(keep, (0, 1, 3, 2)).reshape(blocks, pb, frames)
    kx = jnp.repeat(kx, MAPS, axis=2).astype(BF)
    kx = jnp.pad(kx, ((0, 0), (0, 4), (0, LANES - frames * MAPS)))
    n, m = width // shard, group
    b2rep = jnp.tile(map_b2.astype(F32), LANES // MAPS)[None]
    gains, biases, w1l = tl_gain.astype(F32)[:, None], tl_bias.astype(F32)[:, None], map_w1.astype(F32)
    q2 = map_w2.shape[0]
    par = -(-(shard + 1 + q2) // 16) * 16
    pa = jnp.concatenate([gains * w1l, biases * w1l], axis=1).astype(BF)
    b1row = lax.dynamic_update_slice(jnp.zeros((1, LANES), BF), map_b1[None], (0, me * q2))
    pa = jnp.concatenate([pa, b1row, jnp.tile(map_w2, (1, LANES // MAPS)), jnp.zeros((par - shard - 1 - q2, LANES), BF)])
    wide = width // 2
    fsh = fc1_bias.shape[0]
    vecs = jnp.stack([ln1_gain, ln1_bias, qv_bias[0], qv_bias[1], out_bias, ln2_gain, ln2_bias, fc2_bias])
    pb = lax.dynamic_update_slice(jnp.zeros((16, wide), BF), vecs, (0, (me * shard) % wide))
    pb = lax.dynamic_update_slice(pb, fc1_bias[None], (8, (me * fsh) % wide))
    wa, tok, aux, sel, der, vec, fb, bt, small = forward(
        n, m, v, kx, b2rep, pa, pb, qkv_weight, out_weight, fc1_weight, micros, frames, per, count
    )
    tok = tok.reshape(-1, width)
    w1s = small[0:8]
    w2n = jnp.pad(small[8:72].astype(BF), ((0, 64), (0, 0)))
    ff = fc1_weight.shape[1]
    out, ga, gtok, gvec, gb1, part = token_layer(
        n, m, tok, cotangent.reshape(tok.shape), wa, fc1_weight, fc2_weight, vec, fb
    )
    vecs = jnp.concatenate([gvec, jnp.swapaxes(gb1.reshape(n, -1, shard), 0, 1).reshape(-1, width)])
    vecs = jnp.pad(vecs, ((0, 16 - vecs.shape[0]), (0, 0)))
    co, gts, oa, ob, win, tot = backward(
        n, m, v, aux, der, gtok.reshape(micros, m, -1, width), ga, part, w1s, w2n, vecs, blocks, per, count
    )
    pg = patch_out(v, sel, co, gts, bt, groups * 2, 2)
    pg = jnp.transpose(pg.reshape(micros, group, count, frames, width), (0, 1, 3, 2, 4))
    if m > 2:
        oa, ob, win, tot = (lax.psum(t, "map") * 0.5 for t in (oa, ob, win, tot))
    lo = jnp.minimum(me // 4 * (width // (n // 4)) // LANES * LANES, width - 256)
    win = lax.dynamic_slice(win, (0, me * shard - lo), (96, shard))
    xs = win[:64].T
    gvec = win[64:72]
    fgrad = win[72 : 72 + ff // width].reshape(-1)
    gb = tot[65, :64]
    b2g = jnp.sum(tot[64].reshape(LANES // MAPS, MAPS), axis=0)
    w2g = lax.dynamic_slice(tot, (me * q2, 0), (q2, LANES)).reshape(q2, LANES // MAPS, MAPS).sum(axis=1)
    return (
        out.reshape(cotangent.shape),
        pg,
        jnp.sum(w1l * xs, axis=1),
        w1l @ gb,
        gains * xs + biases * gb[None],
        lax.dynamic_slice(gb, (me * q2,), (q2,)),
        w2g,
        b2g,
        gvec[0],
        gvec[1],
        jnp.concatenate([oa[0], oa[1], oa[2]], axis=1),
        gvec[2:4],
        oa[3],
        gvec[4],
        gvec[5],
        gvec[6],
        jnp.concatenate([oa[4 + q] for q in range(ff // width)], axis=1),
        fgrad,
        ob,
        gvec[7],
    )


def solution(mesh):
    weights = (
        P("clip"), P("clip"), P("clip", None), P("clip"), P("clip", None), P(), P("clip"), P("clip"), P("clip", None),
        P(None, "clip"), P("clip", None), P("clip"), P("clip"), P("clip"), P("clip", None), P("clip"), P("clip", None),
        P("clip"),
    )
    tokens = P(None, ("clip", "map"), None, None)
    frames = P(None, "clip", "map", None, None)
    return jax.shard_map(
        on_device,
        mesh=mesh,
        in_specs=(frames, P(None, "clip", "map", None)) + weights + (tokens,),
        out_specs=(tokens, frames) + weights,
        check_vma=False,
    )
```
